32 devices in a mesh: rows: 4 (over x, core), seq: 8 (over z, y).
Axes of the slice: x: 2, y: 2, z: 4, core: 2. Of those that a mesh axis runs over, the one named last changes fastest.
Arguments:
- tokens: bfloat16 [4, 3, 384, 2048], P('rows', None, 'seq'), may hold values from -6 to 6
- summary: bfloat16 [4, 2, 50, 2048], P('rows'), may hold values from -6 to 6
- doc_ids: int32 [4, 3, 384], P('rows'), may hold values from 0 to 3, as said below
- gain_attn: float32 [2048], replicated, may hold values from 0.25 to 1.75
- gain_ffn: float32 [2048], replicated, may hold values from 0.25 to 1.75
- w_query: bfloat16 [2048, 2048], P(('rows', 'seq')), may hold values from -0.125 to 0.125
- w_key: bfloat16 [2048, 2048], P(('rows', 'seq')), may hold values from -0.125 to 0.125
- w_value: bfloat16 [2048, 2048], P(('rows', 'seq')), may hold values from -0.125 to 0.125
- w_out: bfloat16 [2048, 2048], P(('rows', 'seq')), may hold values from -1.25 to 1.25
- w_up: bfloat16 [2048, 8192], P(('rows', 'seq')), may hold values from -0.125 to 0.125
- w_down: bfloat16 [2048, 8192], P(('rows', 'seq')), may hold values from -0.0625 to 0.0625
- cotangent: bfloat16 [4, 3, 384, 2048], P('rows', None, 'seq'), may hold values from -6 to 6
Outputs:
- activations: bfloat16 [4, 3, 384, 2048], P('rows', None, 'seq')
- d_tokens: float32 [4, 3, 384, 2048], P('rows', None, 'seq')
- d_summary: float32 [4, 2, 50, 2048], P('rows')
- d_gain_attn: float32 [2048], P(('rows', 'seq'))
- d_gain_ffn: float32 [2048], P(('rows', 'seq'))
- d_w_query: float32 [2048, 2048], P(('rows', 'seq'))
- d_w_key: float32 [2048, 2048], P(('rows', 'seq'))
- d_w_value: float32 [2048, 2048], P(('rows', 'seq'))
- d_w_out: float32 [2048, 2048], P(('rows', 'seq'))
- d_w_up: float32 [2048, 8192], P(('rows', 'seq'))
- d_w_down: float32 [2048, 8192], P(('rows', 'seq'))
The draws below stay inside these ranges and needn't reach their ends.
Inputs may be any that keep to these rules, and one draw needn't show every extreme that they name: `doc_ids`: along each sequence the ids never fall; they start at 0 and rise by one at each document start. In each sequence one of the 3 segments lies within a single document.
All inputs are finite; a program needn't handle non-finite values.
Results may differ from the reference program's by a relative error of at most 0.025.
Values may be sent and summed in bfloat16 or wider, within the bound.
No kernel may reach another device: no remote copies, remote signals or barrier semaphores. Data moves between devices by JAX's collectives and lax.ppermute only.
A program may use at most 768 MiB of HBM per device.

```python
import jax
import jax.numpy as jnp
from jax import lax

D = 2048
H = 32
HD = 64
FF = 8192
NSUM = 50
SEGS = 3
SEG_LEN = 384
SEQ_LEN = 1152
ROWS = 4
SUMS = 100


def draw_doc_ids(key, part):
    key = jax.random.fold_in(key, 7)
    whole_key, start_key = jax.random.split(key)
    kept_seg = jax.random.randint(whole_key, (ROWS, 1), 0, SEGS, dtype=jnp.int32)
    starts = jax.random.randint(start_key, (ROWS, 3), 1, SEQ_LEN, dtype=jnp.int32)
    inside = starts // SEG_LEN == kept_seg
    starts = jnp.where(inside, kept_seg * SEG_LEN, starts)
    positions = jnp.arange(SEQ_LEN, dtype=jnp.int32)
    is_start = jnp.any(positions[None, :, None] == starts[:, None, :], axis=2) & (positions[None, :] > 0)
    doc_numbers = jnp.cumsum(is_start.astype(jnp.int32), axis=1).astype(jnp.int32)
    return doc_numbers.reshape(ROWS, SEGS, SEG_LEN)


def level_of(own_key, dims, shards, least, high):
    level = 1.0
    for dim, shards_of in shards:
        heights = jax.random.uniform(jax.random.fold_in(jax.random.fold_in(own_key, 6), dim), (shards_of,), jnp.float32, least / len(shards), high / len(shards))
        level = level * jnp.repeat(jnp.exp(heights), dims[dim] // shards_of).reshape((-1,) + (1,) * (len(dims) - 1 - dim))
    return level


def normal_values(rng, dims, scale, limit, cuts=(), held_as=jnp.bfloat16):
    factor_of = level_of(rng, dims, cuts, -0.22, 0.18) if cuts else 1.0
    drawn = jax.random.normal(rng, dims, jnp.float32) * scale * factor_of
    return jnp.minimum(jnp.maximum(drawn, -limit), limit).astype(held_as)


def setup_inputs(seed: int = 0) -> dict:
    key_of = jax.random.split(jax.random.key(seed), 13)
    tokens = normal_values(key_of[0], (ROWS, SEGS, SEG_LEN, D), 1.0, 6.0, ((0, 4), (2, 8)))
    summary = normal_values(key_of[1], (ROWS, SEGS - 1, NSUM, D), 1.0, 6.0, ((0, 4),))
    doc_ids = draw_doc_ids(jax.random.fold_in(key_of[12], 71), 0)
    gain_attn = jnp.clip(1.0 + 0.15 * jax.random.normal(key_of[3], (D,), jnp.float32), 0.25, 1.75)
    gain_ffn = jnp.clip(1.0 + 0.15 * jax.random.normal(key_of[4], (D,), jnp.float32), 0.25, 1.75)
    w_query = normal_values(key_of[5], (D, D), D ** -0.5, 0.125, ((0, 32),))
    w_key = normal_values(key_of[6], (D, D), D ** -0.5, 0.125, ((0, 32),))
    w_value = normal_values(key_of[7], (D, D), D ** -0.5, 0.125, ((0, 32),))
    w_out = normal_values(key_of[8], (D, D), (max(4 * D // SEG_LEN, 1)) ** -0.5, 1.25, ((0, 32),))
    w_up = normal_values(key_of[9], (D, FF), D ** -0.5, 0.125, ((0, 32),))
    w_down = normal_values(key_of[10], (D, FF), FF ** -0.5, 0.0625, ((0, 32),))
    cotangent = normal_values(key_of[11], (ROWS, SEGS, SEG_LEN, D), 1.0, 6.0, ((0, 4), (2, 8)))
    return {"tokens": tokens, "summary": summary, "doc_ids": doc_ids, "gain_attn": gain_attn, "gain_ffn": gain_ffn, "w_query": w_query, "w_key": w_key, "w_value": w_value, "w_out": w_out, "w_up": w_up, "w_down": w_down, "cotangent": cotangent}


@jax.custom_vjp
def low(v):
    return lax.optimization_barrier(v.astype(jnp.bfloat16)).astype(jnp.float32)

@jax.custom_vjp
def low_back(v):
    return v

def low_keep(v):
    return (low(v), None)

def low_pass(kept, grad):
    return (grad,)

def back_keep(v):
    return (v, None)

def back_low(kept, grad):
    return (low(grad),)
low.defvjp(low_keep, low_pass)
low_back.defvjp(back_keep, back_low)
EPSILON = 1e-05
MASKED = -1e+30
HIGHEST = lax.Precision.HIGHEST

def normalize(inputs, scaling):
    average = lax.optimization_barrier(jnp.mean(inputs, axis=-1, keepdims=True))
    centred = inputs - average
    return centred * lax.rsqrt(lax.optimization_barrier(jnp.mean(centred * centred, axis=-1, keepdims=True)) + EPSILON) * scaling

def row_layer(doc_rows, tokens, summary, gain_attn, gain_ffn, w_query, w_key, w_value, w_out, w_up, w_down):
    flattened = tokens.reshape(SEGS * SEG_LEN, D)
    hidden = low(normalize(flattened, gain_attn))
    summed = low(normalize(summary.reshape(SUMS, D), gain_attn))
    queries = low(low_back(jnp.dot(hidden, w_query, precision=HIGHEST) * 0.125)).reshape(SEGS, SEG_LEN, H, HD)
    keys_tok = low(low_back(jnp.dot(hidden, w_key, precision=HIGHEST))).reshape(SEGS, SEG_LEN, H, HD)
    values_tok = low(low_back(jnp.dot(hidden, w_value, precision=HIGHEST))).reshape(SEGS, SEG_LEN, H, HD)
    sum_keys = low(low_back(jnp.dot(summed, w_key, precision=HIGHEST))).reshape(SUMS, H, HD)
    sum_values = low(low_back(jnp.dot(summed, w_value, precision=HIGHEST))).reshape(SUMS, H, HD)
    last_doc = doc_rows[:, SEG_LEN - 1]
    sum_doc = jnp.repeat(last_doc[:SEGS - 1], NSUM)
    sum_seg = jnp.arange(SUMS, dtype=jnp.int32) // NSUM
    block_rows = min(512, SEG_LEN)
    per_seg = SEG_LEN // block_rows

    @jax.checkpoint
    def attend_block(number):
        segment = number // per_seg
        offset = number % per_seg * block_rows
        seg_queries = lax.dynamic_index_in_dim(queries, segment, 0, False)
        query_block = lax.dynamic_slice_in_dim(seg_queries, offset, block_rows, 0)
        seg_keys = lax.dynamic_index_in_dim(keys_tok, segment, 0, False)
        seg_values = lax.dynamic_index_in_dim(values_tok, segment, 0, False)
        seg_docs = lax.dynamic_index_in_dim(doc_rows, segment, 0, False)
        query_docs = lax.dynamic_slice_in_dim(seg_docs, offset, block_rows, 0)
        query_pos = offset + jnp.arange(block_rows, dtype=jnp.int32)
        key_pos = jnp.arange(SEG_LEN, dtype=jnp.int32)
        tok_mask = (key_pos[None, :] <= query_pos[:, None]) & (query_docs[:, None] == seg_docs[None, :])
        sum_mask = (sum_seg[None, :] < segment) & (query_docs[:, None] == sum_doc[None, :])
        allowed = jnp.concatenate([sum_mask, tok_mask], axis=1)[None]
        all_keys = jnp.concatenate([sum_keys, seg_keys], axis=0)
        all_values = jnp.concatenate([sum_values, seg_values], axis=0)
        scores = low_back(jnp.einsum('qhd,khd->hqk', query_block, all_keys, precision=HIGHEST))
        masked = jnp.where(allowed, scores, MASKED)
        row_top = lax.optimization_barrier(jnp.max(masked, axis=-1, keepdims=True))
        weights = jnp.where(allowed, jnp.exp(masked - row_top), 0.0)
        probabilities = low(weights / lax.optimization_barrier(jnp.sum(weights, axis=-1, keepdims=True)))
        return jnp.einsum('hqk,khd->qhd', probabilities, all_values, precision=HIGHEST)
    attended_raw = lax.map(attend_block, jnp.arange(SEGS * per_seg, dtype=jnp.int32))
    attended = low(low_back(attended_raw.reshape(SEGS * SEG_LEN, D)))
    mixed = flattened + low_back(jnp.dot(attended, w_out, precision=HIGHEST))
    normed = low(normalize(mixed, gain_ffn))
    upper = low_back(jnp.dot(normed, w_up, precision=HIGHEST))
    active = low(jax.nn.gelu(upper, approximate=False))
    result = mixed + low_back(jnp.dot(active, w_down.T, precision=HIGHEST))
    return result.reshape(SEGS, SEG_LEN, D)

def reference(tokens, summary, doc_ids, gain_attn, gain_ffn, w_query, w_key, w_value, w_out, w_up, w_down, cotangent):
    parameters = tuple((weight_arg.astype(jnp.float32) for weight_arg in (gain_attn, gain_ffn, w_query, w_key, w_value, w_out, w_up, w_down)))

    def row_step(grad_sums, row_data):
        row_tokens, row_summary, row_docs, row_cot = row_data

        def forward(*inputs):
            return row_layer(row_docs, *inputs)
        output, pullback = jax.vjp(forward, row_tokens.astype(jnp.float32), row_summary.astype(jnp.float32), *parameters)
        gradients = pullback(row_cot.astype(jnp.float32))
        grad_sums = tuple((running + adding for running, adding in zip(grad_sums, gradients[2:])))
        return (grad_sums, (output.astype(jnp.bfloat16), gradients[0], gradients[1]))
    zero_sums = tuple((jnp.zeros_like(weight_arg) for weight_arg in parameters))
    grad_sums, outputs = lax.scan(row_step, zero_sums, (tokens, summary, doc_ids, cotangent))
    return (outputs[0], outputs[1], outputs[2], grad_sums[0], grad_sums[1], grad_sums[2], grad_sums[3], grad_sums[4], grad_sums[5], grad_sums[6], grad_sums[7])
```

```python
import functools

import jax
import jax.numpy as jnp
from jax import lax
from jax.experimental import pallas as pl
from jax.experimental.pallas import tpu as pltpu
from jax.sharding import Mesh, PartitionSpec as P

HEAD = 64
EPSILON = 1e-05
MASKED = -1e30
SQRT_HALF = 0.7071067811865476
NORMAL_PEAK = 0.3989422804014327

AXES = ("x", "c", "zh", "zl", "y")
ROWS = ("x", "c")
SEQ = ("zh", "zl", "y")
BF = jnp.bfloat16
F32 = jnp.float32


def dot(left, right, left_dim=1, right_dim=0):
    return lax.dot_general(
        left, right, (((left_dim,), (right_dim,)), ((), ())), preferred_element_type=F32
    )


def normalize(inputs):
    average = jnp.mean(inputs, axis=-1, keepdims=True)
    centred = inputs - average
    inverse = lax.rsqrt(jnp.mean(centred * centred, axis=-1, keepdims=True) + EPSILON)
    return centred * inverse, inverse


def normalize_back(upstream, scaling, standard, inverse):
    scaled = upstream * scaling
    return inverse * (
        scaled
        - jnp.mean(scaled, axis=-1, keepdims=True)
        - standard * jnp.mean(scaled * standard, axis=-1, keepdims=True)
    )


def swap(array, axis):
    return lax.ppermute(array, axis, [(0, 1), (1, 0)])


def pair(mine, theirs, axis, dim):
    first = lax.axis_index(axis) == 0
    return jnp.concatenate(
        [jnp.where(first, mine, theirs), jnp.where(first, theirs, mine)], axis=dim
    )


def halves(array, axis, dim):
    half = array.shape[dim] // 2
    place = lax.axis_index(axis)
    return (
        lax.dynamic_slice_in_dim(array, place * half, half, dim),
        lax.dynamic_slice_in_dim(array, (1 - place) * half, half, dim),
    )


def gather_dim(array, axis, dim):
    if lax.axis_size(axis) != 2:
        return lax.all_gather(array, axis, axis=dim, tiled=True)
    return pair(array, swap(array, axis), axis, dim)


def scatter_dim(array, axis, dim):
    if lax.axis_size(axis) != 2:
        return lax.psum_scatter(array, axis, scatter_dimension=dim, tiled=True)
    mine, theirs = halves(array, axis, dim)
    return mine + swap(theirs, axis)


def exchange(array, axis, cut, joined):
    if lax.axis_size(axis) != 2:
        return lax.all_to_all(array, axis, cut, joined, tiled=True)
    mine, theirs = halves(array, axis, cut)
    return pair(mine, swap(theirs, axis), axis, joined)


def gather_near(array, axes):
    for axis in axes:
        if lax.axis_size(axis) != 2:
            array = lax.all_gather(array, axis, axis=0, tiled=True)
        else:
            array = jnp.concatenate([array, swap(array, axis)], axis=0)
    return array


def scatter_near(array, axes):
    for axis in reversed(axes):
        if lax.axis_size(axis) != 2:
            array = lax.psum_scatter(array, axis, scatter_dimension=0, tiled=True)
        else:
            half = array.shape[0] // 2
            array = array[:half] + swap(array[half:], axis)
    return array


def columns_in(weight, group, rest):
    rows, cols = weight.shape
    array = weight.reshape((1,) * len(AXES) + (rows, cols))
    for axis in group:
        array = exchange(array, axis, len(AXES) + 1, AXES.index(axis))
    for axis in rest:
        array = gather_dim(array, axis, AXES.index(axis))
    return array.reshape(-1, array.shape[-1])


def columns_out(sums, group, rest):
    sizes = tuple(lax.axis_size(axis) for axis in AXES)
    array = sums.astype(BF).reshape(sizes + (-1, sums.shape[1]))
    for axis in reversed(rest):
        array = scatter_dim(array, axis, AXES.index(axis))
    for axis in reversed(group):
        array = exchange(array, axis, AXES.index(axis), len(AXES) + 1)
    return array.reshape(array.shape[-2:]).astype(F32)


def block_mask(col_ref, row_ref, sum_ref, first, rows, keys, segment, per_seg):
    query_docs = col_ref[0, first : first + rows, :]
    query_pos = first + lax.broadcasted_iota(jnp.int32, (rows, keys), 0)
    key_pos = lax.broadcasted_iota(jnp.int32, (rows, keys), 1)
    allowed = (key_pos <= query_pos) & (query_docs == row_ref[0, :, :keys])
    padded = sum_ref.shape[-1]
    place = lax.broadcasted_iota(jnp.int32, (rows, padded), 1)
    sum_allowed = (place < segment * per_seg) & (query_docs == sum_ref[...])
    return allowed, sum_allowed


def block_probs(query, key, sum_key, allowed, sum_allowed):
    scores = jnp.where(allowed, dot(query, key, 1, 1), MASKED)
    sum_scores = jnp.where(sum_allowed, dot(query, sum_key, 1, 1), MASKED)
    top = jnp.maximum(
        jnp.max(scores, axis=1, keepdims=True), jnp.max(sum_scores, axis=1, keepdims=True)
    )
    weights = jnp.exp(scores - top)
    sum_weights = jnp.exp(sum_scores - top)
    total = jnp.sum(weights, axis=1, keepdims=True) + jnp.sum(sum_weights, axis=1, keepdims=True)
    share = 1.0 / total
    return weights * share, sum_weights * share


def forward_kernel(
    per_seg, rows, col_ref, row_ref, sum_ref, q_ref, k_ref, v_ref, sk_ref, sv_ref, out_ref
):
    segment = pl.program_id(1)
    length, width = q_ref.shape
    for first in range(0, length, rows):
        keys = first + rows
        allowed, sum_allowed = block_mask(
            col_ref, row_ref, sum_ref, first, rows, keys, segment, per_seg
        )
        for low in range(0, width, HEAD):
            cols = slice(low, low + HEAD)
            probs, sum_probs = block_probs(
                q_ref[first:keys, cols], k_ref[:keys, cols], sk_ref[:, cols], allowed, sum_allowed
            )
            out = dot(probs.astype(BF), v_ref[:keys, cols])
            out += dot(sum_probs.astype(BF), sv_ref[:, cols])
            out_ref[first:keys, cols] = out.astype(BF)


def backward_kernel(
    per_seg, rows, col_ref, row_ref, sum_ref, q_ref, k_ref, v_ref, sk_ref, sv_ref, g_ref,
    dq_ref, dk_ref, dv_ref, dsk_ref, dsv_ref, dk_sum, dv_sum,
):
    segment = pl.program_id(1)
    length, width = q_ref.shape

    @pl.when(segment == 0)
    def _():
        dsk_ref[...] = jnp.zeros_like(dsk_ref)
        dsv_ref[...] = jnp.zeros_like(dsv_ref)

    dk_sum[...] = jnp.zeros_like(dk_sum)
    dv_sum[...] = jnp.zeros_like(dv_sum)
    for first in range(0, length, rows):
        keys = first + rows
        allowed, sum_allowed = block_mask(
            col_ref, row_ref, sum_ref, first, rows, keys, segment, per_seg
        )
        for low in range(0, width, HEAD):
            cols = slice(low, low + HEAD)
            query, grad = q_ref[first:keys, cols], g_ref[first:keys, cols]
            key, sum_key = k_ref[:keys, cols], sk_ref[:, cols]
            probs, sum_probs = block_probs(query, key, sum_key, allowed, sum_allowed)
            d_probs = dot(grad, v_ref[:keys, cols], 1, 1)
            d_sum_probs = dot(grad, sv_ref[:, cols], 1, 1)
            delta = jnp.sum(probs * d_probs, axis=1, keepdims=True)
            delta += jnp.sum(sum_probs * d_sum_probs, axis=1, keepdims=True)
            d_scores = (probs * (d_probs - delta)).astype(BF)
            d_sum_scores = (sum_probs * (d_sum_probs - delta)).astype(BF)
            d_query = (dot(d_scores, key) + dot(d_sum_scores, sum_key)).astype(BF)
            dq_ref[first:keys, cols] = (d_query.astype(F32) * 0.125).astype(BF)
            dk_sum[:keys, cols] += dot(d_scores, query, 0, 0)
            dv_sum[:keys, cols] += dot(probs.astype(BF), grad, 0, 0)
            dsk_ref[:, cols] += dot(d_sum_scores, query, 0, 0)
            dsv_ref[:, cols] += dot(sum_probs.astype(BF), grad, 0, 0)
    dk_ref[...] = dk_sum[...].astype(BF)
    dv_ref[...] = dv_sum[...].astype(BF)


def attention_calls(segs, length, width, padded, per_seg):
    lanes = min(2 * HEAD, width)
    rows = 128 if length <= 512 else 256
    grid = (width // lanes, segs)
    tok = pl.BlockSpec((length, lanes), lambda h, s: (s, h))
    summed = pl.BlockSpec((padded, lanes), lambda h, s: (0, h))
    docs = [
        pl.BlockSpec((1, length, 1), lambda h, s: (s, 0, 0)),
        pl.BlockSpec((1, 1, length), lambda h, s: (s, 0, 0)),
        pl.BlockSpec((1, padded), lambda h, s: (0, 0)),
    ]
    params = pltpu.CompilerParams(
        dimension_semantics=("arbitrary", "arbitrary"), vmem_limit_bytes=48 * 2**20
    )
    tokens = jax.ShapeDtypeStruct((segs * length, width), BF)
    sums = jax.ShapeDtypeStruct((padded, width), F32)
    work = 2 * segs * length * (length // 2 + padded) * width
    forward = pl.pallas_call(
        functools.partial(forward_kernel, per_seg, rows),
        grid=grid,
        in_specs=docs + [tok] * 3 + [summed] * 2,
        out_specs=tok,
        out_shape=tokens,
        compiler_params=params,
        cost_estimate=pl.CostEstimate(
            flops=8 * work, bytes_accessed=8 * segs * length * width, transcendentals=0
        ),
    )
    backward = pl.pallas_call(
        functools.partial(backward_kernel, per_seg, rows),
        grid=grid,
        in_specs=docs + [tok] * 3 + [summed] * 2 + [tok],
        out_specs=[tok] * 3 + [summed] * 2,
        out_shape=[tokens] * 3 + [sums] * 2,
        scratch_shapes=[pltpu.VMEM((length, lanes), F32)] * 2,
        compiler_params=params,
        cost_estimate=pl.CostEstimate(
            flops=20 * work, bytes_accessed=14 * segs * length * width, transcendentals=0
        ),
    )
    return forward, backward


def gelu_both(inputs):
    share = 0.5 * (1.0 + lax.erf(inputs * SQRT_HALF))
    slope = share + inputs * jnp.exp(-0.5 * inputs * inputs) * NORMAL_PEAK
    return inputs * share, slope


ATT_GROUP, ATT_REST = ("zh", "zl", "y"), ("x", "c")
FFN_GROUP, FFN_REST = ("y", "c", "zl"), ("zh", "x")
FFN_NEAR = ("zl", "c", "y")


def per_device(
    tokens, summary, doc_ids, gain_attn, gain_ffn, w_query, w_key, w_value, w_out, w_up, w_down,
    cotangent,
):
    _, segs, here, model = tokens.shape
    per_seg = summary.shape[2]
    sum_rows = summary.shape[1] * per_seg
    padded = -(-sum_rows // 128) * 128
    length = doc_ids.shape[2]
    shards = length // here
    rows = segs * here
    shard_rows = w_query.shape[0]
    heads = model // HEAD
    row_count = lax.axis_size("x") * lax.axis_size("c")
    width = model // shards
    heads_here = width // HEAD

    flat = tokens.reshape(rows, model).astype(F32)
    standard, inverse = normalize(flat)
    hidden = (standard * gain_attn).astype(BF)
    hidden_all = lax.all_gather(hidden, SEQ, axis=0, tiled=True)

    def by_place(weight):
        return weight.reshape(shard_rows, heads_here, shards, HEAD).swapaxes(1, 2)

    qkv_here = jnp.stack([by_place(w) for w in (w_query, w_key, w_value)], axis=2)
    w_qkv = columns_in(qkv_here.reshape(shard_rows, 3 * model), ATT_GROUP, ATT_REST)
    aligned = shard_rows == HEAD
    place = lax.axis_index(SEQ)
    if aligned:
        w_out_here = w_out
        for axis in reversed(ROWS):
            w_out_here = gather_dim(w_out_here, axis, 0)
    else:
        w_out_all = lax.all_gather(w_out, AXES, axis=0, tiled=True)
        w_out_heads = w_out_all.reshape(heads_here, shards, HEAD, model)
        w_out_here = lax.dynamic_index_in_dim(w_out_heads, place, 1, False).reshape(width, model)
    w_up_here = columns_in(w_up, FFN_GROUP, FFN_REST)
    w_down_here = columns_in(w_down, FFN_GROUP, FFN_REST)
    cot = cotangent.reshape(rows, model)
    cot_all = gather_near(cot, FFN_NEAR)

    summary_flat = summary.reshape(sum_rows, model).astype(F32)
    summary_pad = jnp.pad(summary_flat, ((0, padded - sum_rows), (0, 0)))
    standard_sum, inverse_sum = normalize(summary_pad)
    hidden_sum = (standard_sum * gain_attn).astype(BF)

    def in_order(array):
        array = array.reshape(shards, segs, here, -1)
        return array.swapaxes(0, 1).reshape(segs * length, -1)

    def in_shards(array):
        array = array.reshape(segs, shards, here, -1)
        return array.swapaxes(0, 1).reshape(shards * rows, -1)

    projected = dot(hidden_all, w_qkv)
    queries = in_order((projected[:, :width] * 0.125).astype(BF))
    keys = in_order(projected[:, width : 2 * width].astype(BF))
    values = in_order(projected[:, 2 * width :].astype(BF))
    sum_proj = dot(hidden_sum, w_qkv[:, width:]).astype(BF)
    sum_keys, sum_values = sum_proj[:, :width], sum_proj[:, width:]

    docs = doc_ids.reshape(segs, length)
    last_docs = jnp.repeat(docs[: segs - 1, length - 1], per_seg)
    sum_docs = jnp.pad(last_docs, (0, padded - sum_rows), constant_values=-1)[None]
    doc_args = (docs[:, :, None], docs[:, None, :], sum_docs)
    attend, attend_back = attention_calls(segs, length, width, padded, per_seg)
    attended = in_shards(attend(*doc_args, queries, keys, values, sum_keys, sum_values))

    branch = dot(attended, w_out_here).astype(BF)
    mixed = flat + lax.psum_scatter(branch, SEQ, scatter_dimension=0, tiled=True).astype(F32)
    standard_ffn, inverse_ffn = normalize(mixed)
    normed = (standard_ffn * gain_ffn).astype(BF)
    normed_all = gather_near(normed, FFN_NEAR)

    grad_active = dot(cot_all, w_down_here)
    active, slope = gelu_both(dot(normed_all, w_up_here))
    active = active.astype(BF)
    grad_upper = (slope * grad_active).astype(BF)
    grad_normed_part = dot(grad_upper, w_up_here, 1, 1).astype(BF)
    grad_normed = scatter_near(grad_normed_part, FFN_NEAR).astype(F32)
    d_w_up = columns_out(dot(normed_all, grad_upper, 0, 0), FFN_GROUP, FFN_REST)
    d_w_down = columns_out(dot(cot_all, active, 0, 0), FFN_GROUP, FFN_REST)
    ffn_part = dot(active, w_down_here, 1, 1).astype(BF)
    activations = (mixed + scatter_near(ffn_part, FFN_NEAR).astype(F32)).astype(BF)

    grad_mixed = cot.astype(F32) + normalize_back(grad_normed, gain_ffn, standard_ffn, inverse_ffn)
    ffn_gain = jnp.sum(grad_normed * standard_ffn, axis=0)
    grad_branch = grad_mixed.astype(BF)
    grad_branch_all = lax.all_gather(grad_branch, SEQ, axis=0, tiled=True)
    grad_attended = in_order(dot(grad_branch_all, w_out_here, 1, 1).astype(BF))
    d_queries, d_keys, d_values, d_sum_keys, d_sum_values = attend_back(
        *doc_args, queries, keys, values, sum_keys, sum_values, grad_attended
    )
    d_out_part = dot(attended, grad_branch_all, 0, 0).astype(BF)
    if aligned:
        for axis in ROWS:
            d_out_part = scatter_dim(d_out_part, axis, 0)
        d_w_out = d_out_part.astype(F32)
    else:
        spread = jnp.zeros((heads_here, shards, HEAD, model), BF)
        spread = lax.dynamic_update_slice_in_dim(
            spread, d_out_part.reshape(heads_here, 1, HEAD, model), place, 1
        )
        d_w_out = lax.psum_scatter(
            spread.reshape(model, model), AXES, scatter_dimension=0, tiled=True
        ).astype(F32)

    d_projected = in_shards(jnp.concatenate([d_queries, d_keys, d_values], axis=1))
    d_sum_proj = jnp.concatenate([d_sum_keys, d_sum_values], axis=1).astype(BF)

    grad_sum_part = dot(d_sum_proj, w_qkv[:, width:], 1, 1).astype(BF)
    share_rows = padded // shards
    for axis in SEQ:
        grad_sum_part = scatter_dim(grad_sum_part, axis, 0)
    grad_sum = grad_sum_part.astype(F32)
    first_row = place * share_rows
    standard_part = lax.dynamic_slice_in_dim(standard_sum, first_row, share_rows, 0)
    inverse_part = lax.dynamic_slice_in_dim(inverse_sum, first_row, share_rows, 0)
    d_sum_part = normalize_back(grad_sum, gain_attn, standard_part, inverse_part).astype(BF)
    for axis in reversed(SEQ):
        d_sum_part = gather_dim(d_sum_part, axis, 0)
    d_summary = d_sum_part[:sum_rows].astype(F32)

    grad_hidden_part = dot(d_projected, w_qkv, 1, 1).astype(BF)
    grad_hidden = lax.psum_scatter(
        grad_hidden_part, SEQ, scatter_dimension=0, tiled=True
    ).astype(F32)
    left = jnp.concatenate([hidden_all, hidden_sum], axis=0)
    right = jnp.concatenate(
        [d_projected, jnp.pad(d_sum_proj, ((0, 0), (width, 0)))], axis=0
    )
    d_w_qkv = columns_out(dot(left, right, 0, 0), ATT_GROUP, ATT_REST)
    d_w_qkv = d_w_qkv.reshape(shard_rows, shards, 3, heads_here, HEAD)
    d_w_qkv = d_w_qkv.transpose(2, 0, 3, 1, 4).reshape(3, shard_rows, model)

    d_tokens = grad_mixed + normalize_back(grad_hidden, gain_attn, standard, inverse)
    attn_gain = jnp.sum(grad_hidden * standard, axis=0)
    attn_gain += jnp.sum(grad_sum * standard_part, axis=0)
    gains = jnp.stack([attn_gain, ffn_gain])
    for axis in AXES:
        gains = scatter_dim(gains, axis, 1)

    return (
        activations.reshape(tokens.shape),
        d_tokens.reshape(tokens.shape),
        d_summary.reshape(summary.shape),
        gains[0],
        gains[1],
        d_w_qkv[0],
        d_w_qkv[1],
        d_w_qkv[2],
        d_w_out,
        d_w_up,
        d_w_down,
    )


def solution(mesh):
    rows, seq = mesh.shape["rows"], mesh.shape["seq"]
    fine = Mesh(mesh.devices.reshape(rows // 2, 2, seq // 4, 2, 2), AXES)
    by_token = P(ROWS, None, SEQ, None)
    by_row = P(ROWS, None, None, None)
    weight = P(AXES, None)
    return jax.shard_map(
        per_device,
        mesh=fine,
        in_specs=(by_token, by_row, P(ROWS, None, None), P(), P())
        + (weight,) * 6
        + (by_token,),
        out_specs=(by_token, by_token, by_row, P(AXES), P(AXES)) + (weight,) * 6,
        check_vma=False,
    )
```

```python
import functools

import jax
import jax.numpy as jnp
from jax import lax
from jax.experimental import pallas as pl
from jax.experimental.pallas import tpu as pltpu
from jax.sharding import Mesh, PartitionSpec as P

HEAD = 64
EPSILON = 1e-05
MASKED = -1e30
SQRT_HALF = 0.7071067811865476
NORMAL_PEAK = 0.3989422804014327

AXES = ("x", "c", "zh", "zl", "y")
ROWS = ("x", "c")
SEQ = ("zh", "zl", "y")
FFN_GROUP = ("y", "c", "zl")
FFN_DIMS = ("c", "zl", "y")
FFN_NEAR = ("y", "zl", "c")
BF = jnp.bfloat16
F32 = jnp.float32


def dot(left, right, left_dim=1, right_dim=0):
    return lax.dot_general(
        left, right, (((left_dim,), (right_dim,)), ((), ())), preferred_element_type=F32
    )


def normalize(inputs):
    average = jnp.mean(inputs, axis=-1, keepdims=True)
    centred = inputs - average
    inverse = lax.rsqrt(jnp.mean(centred * centred, axis=-1, keepdims=True) + EPSILON)
    return centred * inverse, inverse


def normalize_back(upstream, scaling, standard, inverse):
    scaled = upstream * scaling
    return inverse * (
        scaled
        - jnp.mean(scaled, axis=-1, keepdims=True)
        - standard * jnp.mean(scaled * standard, axis=-1, keepdims=True)
    )


def swap(array, axis):
    return lax.ppermute(array, axis, [(0, 1), (1, 0)])


def pair(mine, theirs, axis, dim):
    first = lax.axis_index(axis) == 0
    return jnp.concatenate(
        [jnp.where(first, mine, theirs), jnp.where(first, theirs, mine)], axis=dim
    )


def halves(array, axis, dim):
    half = array.shape[dim] // 2
    place = lax.axis_index(axis)
    return (
        lax.dynamic_slice_in_dim(array, place * half, half, dim),
        lax.dynamic_slice_in_dim(array, (1 - place) * half, half, dim),
    )


def together(*transfers):
    results = [None] * len(transfers)
    flying = {}

    def advance(place, sent):
        try:
            flying[place] = transfers[place].send(sent)
        except StopIteration as end:
            flying.pop(place, None)
            results[place] = end.value

    for place in range(len(transfers)):
        advance(place, None)
    while flying:
        for place, landed in lax.optimization_barrier(dict(flying)).items():
            advance(place, landed)
    return results


def tie(*arrays):
    return lax.optimization_barrier(arrays)


def pause(rounds, transfer):
    for _ in range(rounds):
        yield ()
    return (yield from transfer)


def gather_dim(array, axis, dim):
    if lax.axis_size(axis) != 2:
        return lax.all_gather(array, axis, axis=dim, tiled=True)
    theirs = yield swap(array, axis)
    return pair(array, theirs, axis, dim)


def scatter_dim(array, axis, dim):
    if lax.axis_size(axis) != 2:
        return lax.psum_scatter(array, axis, scatter_dimension=dim, tiled=True)
    mine, theirs = halves(array, axis, dim)
    theirs = yield swap(theirs, axis)
    return mine + theirs


def exchange(array, axis, cut, joined):
    if lax.axis_size(axis) != 2:
        return lax.all_to_all(array, axis, cut, joined, tiled=True)
    mine, theirs = halves(array, axis, cut)
    theirs = yield swap(theirs, axis)
    return pair(mine, theirs, axis, joined)


def gather_plane(array, first, second, last):
    cut = -(-array.shape[0] // 32) * 16
    by_first, by_second, near = yield (swap(array, first), swap(array, second), swap(array, last))
    low, high, near_first, near_second = yield (
        swap(by_second[:cut], first),
        swap(by_first[cut:], second),
        swap(by_first, last),
        swap(by_second, last),
    )
    both = jnp.concatenate([low, high], axis=0)
    near_both = yield swap(both, last)
    return jnp.concatenate(
        [array, by_first, by_second, both, near, near_first, near_second, near_both], axis=0
    )


def scatter_plane(array, first, second, last):
    half, rows = array.shape[0] // 2, array.shape[0] // 8
    cut = -(-rows // 32) * 16
    theirs = yield swap(array[half:], last)
    array = array[:half] + theirs
    here, by_first, by_second, both = (array[i * rows : (i + 1) * rows] for i in range(4))
    low, high = yield (swap(both[:cut], first), swap(both[cut:], second))
    by_second = jnp.concatenate([by_second[:cut] + low, by_second[cut:]], axis=0)
    by_first = jnp.concatenate([by_first[:cut], by_first[cut:] + high], axis=0)
    by_first, by_second = yield (swap(by_first, first), swap(by_second, second))
    return here + by_first + by_second


def ring_size():
    return 4 if lax.axis_size("zh") == 2 else 0


def ring_shift(array, step):
    return lax.ppermute(array, ("zh", "zl"), [(i, (i + step) % 4) for i in range(4)])


def gather_ring(array):
    if not ring_size():
        return [lax.all_gather(array, SEQ, axis=0, tiled=True)]
    along, across = [array], []
    for step in range(3):
        coming = ring_shift(along[-1], 1)
        across.append(swap(along[-1], "y"))
        if step == 0:
            coming = yield coming
        else:
            coming, across[step - 1] = yield (coming, across[step - 1])
        along.append(coming)
    across.append(swap(along[-1], "y"))
    across[2], across[3] = yield (across[2], across[3])
    return [jnp.concatenate(blocks, axis=0) for blocks in zip(along, across)]


def scatter_ring(blocks):
    if not ring_size():
        return lax.psum_scatter(blocks[0], SEQ, scatter_dimension=0, tiled=True)
    half = blocks[0].shape[0] // 2
    across = swap(blocks[3][half:], "y")
    later = swap(blocks[2][half:], "y")
    across = yield across
    running = blocks[3][:half] + across
    for step in (2, 1, 0):
        across = later
        coming = ring_shift(running, -1)
        if step:
            later = swap(blocks[step - 1][half:], "y")
        coming, across = yield (coming, across)
        running = blocks[step][:half] + across + coming
    return running


def ring_order(shards):
    places = jnp.arange(shards, dtype=jnp.int32)
    if not ring_size():
        return places
    along = lax.axis_index(("zh", "zl"))
    return (along - places // 2) % 4 * 2 + (places % 2 ^ lax.axis_index("y"))


def columns_of_qkv(weights):
    array = weights.reshape((1,) * 5 + weights.shape)
    for axis in SEQ:
        array = yield from exchange(array, axis, 6, AXES.index(axis))
    for axis in ROWS:
        array = yield from gather_dim(array, axis, AXES.index(axis))
    return array.reshape(-1, array.shape[-1])


def sums_of_qkv(sums):
    sizes = tuple(lax.axis_size(axis) for axis in AXES)
    array = sums.reshape(sizes + (-1, sums.shape[1]))
    for axis in reversed(ROWS):
        array = yield from scatter_dim(array, axis, AXES.index(axis))
    for axis in reversed(SEQ):
        array = yield from exchange(array, axis, AXES.index(axis), 6)
    return array.reshape(array.shape[-2:])


def columns_of_ffn(weights):
    array = weights.reshape((weights.shape[0], 1, 1, 1) + weights.shape[1:])
    for axis in FFN_GROUP:
        array = yield from exchange(array, axis, 5, FFN_DIMS.index(axis) + 1)
    return array.reshape(weights.shape[0], -1, array.shape[-1])


def sums_of_ffn(sums):
    sizes = tuple(lax.axis_size(axis) for axis in FFN_DIMS)
    array = sums.reshape((sums.shape[0],) + sizes + (-1, sums.shape[-1]))
    for axis in reversed(FFN_GROUP):
        array = yield from exchange(array, axis, FFN_DIMS.index(axis) + 1, 5)
    return array.reshape(array.shape[0], array.shape[-2], array.shape[-1])


def gather_bulk(array):
    return lax.all_gather(array, "zh", axis=0, tiled=True)


def scatter_bulk(array):
    return lax.psum_scatter(array, "zh", scatter_dimension=0, tiled=True)


def columns_over_x(array, rounds):
    cols = array.shape[-1]
    split = array.reshape(lax.axis_size("zh"), lax.axis_size("c"), -1, cols)
    theirs = swap(array, "x")
    for _ in range(rounds):
        yield ()
    theirs = (yield theirs).reshape(split.shape)
    whole = pair(split.swapaxes(0, 1)[None], theirs.swapaxes(0, 1)[None], "x", 0)
    return whole.reshape(-1, cols)


def sums_over_x(sums, rounds):
    cols = sums.shape[-1]
    split = sums.reshape(2, lax.axis_size("c"), lax.axis_size("zh"), -1, cols)
    mine, theirs = (half[0].swapaxes(0, 1).reshape(-1, cols) for half in halves(split, "x", 0))
    theirs = swap(theirs, "x")
    for _ in range(rounds):
        yield ()
    theirs = yield theirs
    return mine + theirs


def block_mask(col_ref, row_ref, sum_ref, first, rows, keys, segment, per_seg):
    query_docs = col_ref[0, first : first + rows, :]
    query_pos = first + lax.broadcasted_iota(jnp.int32, (rows, keys), 0)
    key_pos = lax.broadcasted_iota(jnp.int32, (rows, keys), 1)
    allowed = (key_pos <= query_pos) & (query_docs == row_ref[0, :, :keys])
    padded = sum_ref.shape[-1]
    place = lax.broadcasted_iota(jnp.int32, (rows, padded), 1)
    sum_allowed = (place < segment * per_seg) & (query_docs == sum_ref[...])
    return allowed, sum_allowed


def block_probs(query, key, sum_key, allowed, sum_allowed):
    scores = jnp.where(allowed, dot(query, key, 1, 1), MASKED)
    sum_scores = jnp.where(sum_allowed, dot(query, sum_key, 1, 1), MASKED)
    top = jnp.maximum(
        jnp.max(scores, axis=1, keepdims=True), jnp.max(sum_scores, axis=1, keepdims=True)
    )
    weights = jnp.exp(scores - top)
    sum_weights = jnp.exp(sum_scores - top)
    total = jnp.sum(weights, axis=1, keepdims=True) + jnp.sum(sum_weights, axis=1, keepdims=True)
    share = 1.0 / total
    return weights * share, sum_weights * share


def load_ordered(order_ref, refs, scratches):
    shards, _, here, _ = refs[0].shape
    for place in range(shards):
        block = order_ref[place]
        for ref, scratch in zip(refs, scratches):
            scratch[place * here : (place + 1) * here, :] = ref[block, 0]


def store_ordered(order_ref, refs, scratches):
    shards, _, here, _ = refs[0].shape
    for place in range(shards):
        block = order_ref[place]
        for ref, scratch in zip(refs, scratches):
            ref[block, 0] = scratch[place * here : (place + 1) * here, :].astype(ref.dtype)


def forward_kernel(
    per_seg, rows, order_ref, col_ref, row_ref, sum_ref, q_in, k_in, v_in, sk_ref, sv_ref, out_ref,
    q_ref, k_ref, v_ref, o_ref,
):
    segment = pl.program_id(1)
    load_ordered(order_ref, (q_in, k_in, v_in), (q_ref, k_ref, v_ref))
    length, width = q_ref.shape
    for first in range(0, length, rows):
        keys = first + rows
        allowed, sum_allowed = block_mask(
            col_ref, row_ref, sum_ref, first, rows, keys, segment, per_seg
        )
        for low in range(0, width, HEAD):
            cols = slice(low, low + HEAD)
            probs, sum_probs = block_probs(
                q_ref[first:keys, cols], k_ref[:keys, cols], sk_ref[:, cols], allowed, sum_allowed
            )
            out = dot(probs.astype(BF), v_ref[:keys, cols])
            out += dot(sum_probs.astype(BF), sv_ref[:, cols])
            o_ref[first:keys, cols] = out.astype(BF)
    store_ordered(order_ref, (out_ref,), (o_ref,))


def backward_kernel(
    per_seg, rows, order_ref, col_ref, row_ref, sum_ref, q_in, k_in, v_in, sk_ref, sv_ref, g_in,
    dq_out, dk_out, dv_out, dsk_ref, dsv_ref,
    q_ref, k_ref, v_ref, g_ref, dq_ref, dk_sum, dv_sum,
):
    segment = pl.program_id(1)
    load_ordered(order_ref, (q_in, k_in, v_in, g_in), (q_ref, k_ref, v_ref, g_ref))
    length, width = q_ref.shape

    @pl.when(segment == 0)
    def _():
        dsk_ref[...] = jnp.zeros_like(dsk_ref)
        dsv_ref[...] = jnp.zeros_like(dsv_ref)

    dk_sum[...] = jnp.zeros_like(dk_sum)
    dv_sum[...] = jnp.zeros_like(dv_sum)
    for first in range(0, length, rows):
        keys = first + rows
        allowed, sum_allowed = block_mask(
            col_ref, row_ref, sum_ref, first, rows, keys, segment, per_seg
        )
        for low in range(0, width, HEAD):
            cols = slice(low, low + HEAD)
            query, grad = q_ref[first:keys, cols], g_ref[first:keys, cols]
            key, sum_key = k_ref[:keys, cols], sk_ref[:, cols]
            probs, sum_probs = block_probs(query, key, sum_key, allowed, sum_allowed)
            d_probs = dot(grad, v_ref[:keys, cols], 1, 1)
            d_sum_probs = dot(grad, sv_ref[:, cols], 1, 1)
            delta = jnp.sum(probs * d_probs, axis=1, keepdims=True)
            delta += jnp.sum(sum_probs * d_sum_probs, axis=1, keepdims=True)
            d_scores = (probs * (d_probs - delta)).astype(BF)
            d_sum_scores = (sum_probs * (d_sum_probs - delta)).astype(BF)
            d_query = (dot(d_scores, key) + dot(d_sum_scores, sum_key)).astype(BF)
            dq_ref[first:keys, cols] = (d_query.astype(F32) * 0.125).astype(BF)
            dk_sum[:keys, cols] += dot(d_scores, query, 0, 0)
            dv_sum[:keys, cols] += dot(probs.astype(BF), grad, 0, 0)
            dsk_ref[:, cols] += dot(d_sum_scores, query, 0, 0)
            dsv_ref[:, cols] += dot(sum_probs.astype(BF), grad, 0, 0)
    store_ordered(order_ref, (dq_out, dk_out, dv_out), (dq_ref, dk_sum, dv_sum))


def attention_calls(segs, shards, here, width, padded, per_seg):
    lanes = min(2 * HEAD, width)
    length = shards * here
    rows = 128 if length <= 512 else 256
    grid = (width // lanes, segs)
    tok = pl.BlockSpec((shards, 1, here, lanes), lambda h, s: (0, s, 0, h))
    summed = pl.BlockSpec((padded, lanes), lambda h, s: (0, h))
    docs = [
        pl.BlockSpec(memory_space=pltpu.SMEM),
        pl.BlockSpec((1, length, 1), lambda h, s: (s, 0, 0)),
        pl.BlockSpec((1, 1, length), lambda h, s: (s, 0, 0)),
        pl.BlockSpec((1, padded), lambda h, s: (0, 0)),
    ]
    params = pltpu.CompilerParams(
        dimension_semantics=("arbitrary", "arbitrary"), vmem_limit_bytes=48 * 2**20
    )
    tokens = jax.ShapeDtypeStruct((shards, segs, here, width), BF)
    sums = jax.ShapeDtypeStruct((padded, width), F32)
    narrow, wide = pltpu.VMEM((length, lanes), BF), pltpu.VMEM((length, lanes), F32)
    work = 2 * segs * length * (length // 2 + padded) * width
    forward = pl.pallas_call(
        functools.partial(forward_kernel, per_seg, rows),
        grid=grid,
        in_specs=docs + [tok] * 3 + [summed] * 2,
        out_specs=tok,
        out_shape=tokens,
        scratch_shapes=[narrow] * 4,
        compiler_params=params,
        cost_estimate=pl.CostEstimate(
            flops=8 * work, bytes_accessed=8 * segs * length * width, transcendentals=0
        ),
    )
    backward = pl.pallas_call(
        functools.partial(backward_kernel, per_seg, rows),
        grid=grid,
        in_specs=docs + [tok] * 3 + [summed] * 2 + [tok],
        out_specs=[tok] * 3 + [summed] * 2,
        out_shape=[tokens] * 3 + [sums] * 2,
        scratch_shapes=[narrow] * 5 + [wide] * 2,
        compiler_params=params,
        cost_estimate=pl.CostEstimate(
            flops=20 * work, bytes_accessed=14 * segs * length * width, transcendentals=0
        ),
    )
    return forward, backward


def gelu_both(inputs):
    share = 0.5 * (1.0 + lax.erf(inputs * SQRT_HALF))
    slope = share + inputs * jnp.exp(-0.5 * inputs * inputs) * NORMAL_PEAK
    return inputs * share, slope


def per_device(
    tokens, summary, doc_ids, gain_attn, gain_ffn, w_query, w_key, w_value, w_out, w_up, w_down,
    cotangent,
):
    _, segs, here, model = tokens.shape
    per_seg = summary.shape[2]
    sum_rows = summary.shape[1] * per_seg
    padded = -(-sum_rows // 128) * 128
    length = doc_ids.shape[2]
    shards = length // here
    rows = segs * here
    shard_rows = w_query.shape[0]
    width = model // shards
    heads_here = width // HEAD

    place = lax.axis_index(SEQ)
    aligned = shard_rows == HEAD

    def by_place(weight):
        return weight.reshape(shard_rows, heads_here, shards, HEAD).swapaxes(1, 2)

    def out_rows():
        if aligned:
            array = w_out
            for axis in reversed(ROWS):
                array = yield from gather_dim(array, axis, 0)
            return array
        whole = lax.all_gather(w_out, AXES, axis=0, tiled=True)
        whole = whole.reshape(heads_here, shards, HEAD, model)
        return lax.dynamic_index_in_dim(whole, place, 1, False).reshape(width, model)

    def out_sums(array):
        if aligned:
            for axis in ROWS:
                array = yield from scatter_dim(array, axis, 0)
            return array
        spread = jnp.zeros((heads_here, shards, HEAD, model), BF)
        spread = lax.dynamic_update_slice_in_dim(
            spread, array.reshape(heads_here, 1, HEAD, model), place, 1
        )
        return lax.psum_scatter(
            spread.reshape(model, model), AXES, scatter_dimension=0, tiled=True
        )

    flat = tokens.reshape(rows, model).astype(F32)
    standard, inverse = normalize(flat)
    hidden = (standard * gain_attn).astype(BF)
    qkv_here = jnp.stack([by_place(w) for w in (w_query, w_key, w_value)], axis=2)
    qkv_here = qkv_here.reshape(shard_rows, 3 * model)
    hidden_blocks, w_qkv, ffn_part = together(
        gather_ring(hidden), columns_of_qkv(qkv_here), columns_of_ffn(jnp.stack([w_up, w_down]))
    )
    w_up_half = gather_bulk(ffn_part[0])
    w_down_half = gather_bulk(ffn_part[1])

    summary_flat = summary.reshape(sum_rows, model).astype(F32)
    summary_pad = jnp.pad(summary_flat, ((0, padded - sum_rows), (0, 0)))
    standard_sum, inverse_sum = normalize(summary_pad)
    hidden_sum = (standard_sum * gain_attn).astype(BF)

    cot = cotangent.reshape(rows, model)
    cot_tied, w_out, _ = tie(cot, w_out, hidden_blocks[-1])
    cot_all, w_out_here = together(gather_plane(cot_tied, *FFN_NEAR), out_rows())
    projected = jnp.concatenate([dot(block, w_qkv) for block in hidden_blocks], axis=0)
    split = (shards, segs, here, width)
    queries = (projected[:, :width] * 0.125).astype(BF).reshape(split)
    keys = projected[:, width : 2 * width].astype(BF).reshape(split)
    values = projected[:, 2 * width :].astype(BF).reshape(split)
    sum_proj = dot(hidden_sum, w_qkv[:, width:]).astype(BF)
    sum_keys, sum_values = sum_proj[:, :width], sum_proj[:, width:]

    docs = doc_ids.reshape(segs, length)
    last_docs = jnp.repeat(docs[: segs - 1, length - 1], per_seg)
    sum_docs = jnp.pad(last_docs, (0, padded - sum_rows), constant_values=-1)[None]
    doc_args = (ring_order(shards), docs[:, :, None], docs[:, None, :], sum_docs)
    attend, attend_back = attention_calls(segs, shards, here, width, padded, per_seg)
    attended = attend(*doc_args, queries, keys, values, sum_keys, sum_values)
    attended = attended.reshape(shards * rows, width)

    block_rows = hidden_blocks[0].shape[0]

    def by_block(array):
        return [array[i : i + block_rows] for i in range(0, shards * rows, block_rows)]

    attended, cot_all, w_out_here = tie(attended, cot_all, w_out_here)
    branch = [dot(block, w_out_here).astype(BF) for block in by_block(attended)]
    summed, w_up_here = together(scatter_ring(branch), columns_over_x(w_up_half, 3))
    mixed = flat + summed.astype(F32)
    standard_ffn, inverse_ffn = normalize(mixed)
    normed = (standard_ffn * gain_ffn).astype(BF)
    normed, w_down_half = tie(normed, w_down_half)
    normed_all, w_down_here = together(
        gather_plane(normed, *FFN_NEAR), columns_over_x(w_down_half, 2)
    )

    active, slope = gelu_both(dot(normed_all, w_up_here))
    active = active.astype(BF)
    grad_active = dot(cot_all, w_down_here)
    grad_upper = (slope * grad_active).astype(BF)
    grad_normed_part = dot(grad_upper, w_up_here, 1, 1).astype(BF)
    d_w_up = dot(normed_all, grad_upper, 0, 0).astype(BF)
    d_w_down = dot(cot_all, active, 0, 0).astype(BF)
    ffn_out_part = dot(active, w_down_here, 1, 1).astype(BF)
    grad_normed, d_w_up = together(
        scatter_plane(grad_normed_part, *FFN_NEAR), sums_over_x(d_w_up, 2)
    )
    d_w_up = scatter_bulk(d_w_up)
    grad_normed = grad_normed.astype(F32)
    grad_mixed = cot.astype(F32) + normalize_back(grad_normed, gain_ffn, standard_ffn, inverse_ffn)
    ffn_gain = jnp.sum(grad_normed * standard_ffn, axis=0)
    grad_branch = grad_mixed.astype(BF)

    grad_branch, d_w_down = tie(grad_branch, d_w_down)
    grad_blocks, d_w_down = together(gather_ring(grad_branch), sums_over_x(d_w_down, 3))
    d_w_down = scatter_bulk(d_w_down)
    ffn_out_part, _ = tie(ffn_out_part, grad_blocks[-1])
    grad_attended = jnp.concatenate(
        [dot(block, w_out_here, 1, 1).astype(BF) for block in grad_blocks], axis=0
    )
    d_queries, d_keys, d_values, d_sum_keys, d_sum_values = attend_back(
        *doc_args, queries, keys, values, sum_keys, sum_values, grad_attended.reshape(split)
    )
    d_out_part = dot(attended, jnp.concatenate(grad_blocks, axis=0), 0, 0).astype(BF)
    ffn_out, d_w_out = together(scatter_plane(ffn_out_part, *FFN_NEAR), out_sums(d_out_part))
    activations = (mixed + ffn_out.astype(F32)).astype(BF)

    d_projected = jnp.concatenate(
        [part.reshape(shards * rows, width) for part in (d_queries, d_keys, d_values)], axis=1
    )
    d_projected, ffn_out = tie(d_projected, ffn_out)
    d_sum_proj = jnp.concatenate([d_sum_keys, d_sum_values], axis=1).astype(BF)
    grad_hidden_blocks = [dot(block, w_qkv, 1, 1).astype(BF) for block in by_block(d_projected)]
    grad_sum_part = dot(d_sum_proj, w_qkv[:, width:], 1, 1).astype(BF)
    left = jnp.concatenate(hidden_blocks + [hidden_sum], axis=0)
    right = jnp.concatenate([d_projected, jnp.pad(d_sum_proj, ((0, 0), (width, 0)))], axis=0)
    d_w_qkv = dot(left, right, 0, 0).astype(BF)

    attn_gain = jnp.sum(grad_sum_part.astype(F32) * hidden_sum.astype(F32), axis=0)
    for grad_block, block in zip(grad_hidden_blocks, hidden_blocks):
        attn_gain += jnp.sum(grad_block.astype(F32) * block.astype(F32), axis=0)
    gains = jnp.stack([attn_gain / gain_attn, ffn_gain])

    per_place = -(-sum_rows // shards)
    held = -(-(per_place + 1) // 16) * 16

    def in_places(array):
        array = jnp.pad(array, ((0, shards * per_place - array.shape[0]), (0, 0)))
        return array.reshape(shards, per_place, model)

    def sum_and_gains():
        by_shard = gains.reshape(2, -1, shards, shard_rows).transpose(2, 0, 1, 3)
        gain_rows = by_shard.reshape(shards, 1, -1).astype(BF)
        gain_cols = gain_rows.shape[-1]
        gain_rows = jnp.pad(gain_rows, ((0, 0), (0, held - per_place - 1), (0, model - gain_cols)))
        array = jnp.concatenate([in_places(grad_sum_part[:sum_rows]), gain_rows], axis=1)
        array = array.reshape(shards * held, model)
        for axis in SEQ:
            array = yield from scatter_dim(array, axis, 0)
        grad_sum = array[:per_place].astype(F32)
        standard_part = lax.dynamic_index_in_dim(in_places(standard_sum[:sum_rows]), place, 0, False)
        inverse_part = jnp.pad(inverse_sum[:sum_rows], ((0, shards * per_place - sum_rows), (0, 0)))
        inverse_part = lax.dynamic_slice_in_dim(inverse_part, place * per_place, per_place, 0)
        part = normalize_back(grad_sum, gain_attn, standard_part, inverse_part).astype(BF)
        part = jnp.pad(part, ((0, held - per_place), (0, 0)))
        both = array[per_place, :gain_cols].astype(F32).reshape(2, -1)
        for axis in ROWS:
            both = yield from scatter_dim(both, axis, 1)
        for axis in reversed(SEQ):
            part = yield from gather_dim(part, axis, 0)
        part = part.reshape(shards, held, model)[:, :per_place].reshape(-1, model)
        return part[:sum_rows].astype(F32), both

    grad_hidden, d_w_qkv, (d_summary, gains), d_ffn = together(
        scatter_ring(grad_hidden_blocks),
        sums_of_qkv(d_w_qkv),
        sum_and_gains(),
        pause(3, sums_of_ffn(jnp.stack([d_w_up, d_w_down]))),
    )
    grad_hidden = grad_hidden.astype(F32)
    d_tokens = grad_mixed + normalize_back(grad_hidden, gain_attn, standard, inverse)
    d_w_qkv = d_w_qkv.reshape(shard_rows, shards, 3, heads_here, HEAD)
    d_w_qkv = d_w_qkv.transpose(2, 0, 3, 1, 4).reshape(3, shard_rows, model).astype(F32)

    return (
        activations.reshape(tokens.shape),
        d_tokens.reshape(tokens.shape),
        d_summary.reshape(summary.shape),
        gains[0],
        gains[1],
        d_w_qkv[0],
        d_w_qkv[1],
        d_w_qkv[2],
        d_w_out.astype(F32),
        d_ffn[0].astype(F32),
        d_ffn[1].astype(F32),
    )


def solution(mesh):
    rows, seq = mesh.shape["rows"], mesh.shape["seq"]
    fine = Mesh(mesh.devices.reshape(rows // 2, 2, seq // 4, 2, 2), AXES)
    by_token = P(ROWS, None, SEQ, None)
    by_row = P(ROWS, None, None, None)
    weight = P(AXES, None)
    return jax.shard_map(
        per_device,
        mesh=fine,
        in_specs=(by_token, by_row, P(ROWS, None, None), P(), P())
        + (weight,) * 6
        + (by_token,),
        out_specs=(by_token, by_token, by_row, P(AXES), P(AXES)) + (weight,) * 6,
        check_vma=False,
    )
```

```python
import functools
import itertools
import math

import jax
import jax.numpy as jnp
from jax import lax
from jax.experimental import pallas as pl
from jax.experimental.pallas import tpu as pltpu
from jax.sharding import Mesh, PartitionSpec as P

HEAD = 64
EPSILON = 1e-05
MASKED = -1e30
SQRT_HALF = 0.7071067811865476
NORMAL_PEAK = 0.3989422804014327

AXES = ("x", "c", "zh", "zl", "y")
ROWS = ("x", "c")
SEQ = ("zh", "zl", "y")
FFN_GROUP = ("y", "c", "zl")
FFN_DIMS = ("c", "zl", "y")
FFN_NEAR = ("y", "zl", "c")
FFN_REST = ("x", "zh")
BF = jnp.bfloat16
F32 = jnp.float32


def dot(left, right, left_dim=1, right_dim=0):
    return lax.dot_general(
        left, right, (((left_dim,), (right_dim,)), ((), ())), preferred_element_type=F32
    )


def normalize(inputs):
    average = jnp.mean(inputs, axis=-1, keepdims=True)
    centred = inputs - average
    inverse = lax.rsqrt(jnp.mean(centred * centred, axis=-1, keepdims=True) + EPSILON)
    return centred * inverse, inverse


def normalize_back(upstream, scaling, standard, inverse):
    scaled = upstream * scaling
    return inverse * (
        scaled
        - jnp.mean(scaled, axis=-1, keepdims=True)
        - standard * jnp.mean(scaled * standard, axis=-1, keepdims=True)
    )


def swap(array, axis):
    return lax.ppermute(array, axis, [(0, 1), (1, 0)])


def pair(mine, theirs, axis, dim):
    first = lax.axis_index(axis) == 0
    return jnp.concatenate(
        [jnp.where(first, mine, theirs), jnp.where(first, theirs, mine)], axis=dim
    )


def halves(array, axis, dim):
    half = array.shape[dim] // 2
    place = lax.axis_index(axis)
    return (
        lax.dynamic_slice_in_dim(array, place * half, half, dim),
        lax.dynamic_slice_in_dim(array, (1 - place) * half, half, dim),
    )


def together(**transfers):
    flying = {}

    def advance(name, sent):
        try:
            with jax.named_scope(name):
                flying[name] = transfers[name].send(sent)
        except StopIteration:
            flying.pop(name, None)

    for name in transfers:
        advance(name, None)
    while flying:
        landed = lax.optimization_barrier(dict(flying))
        for name in transfers:
            if name in landed:
                advance(name, landed[name])


class Box(dict):
    def wait(self, key):
        while key not in self:
            yield ()
        return self[key]

    def put(self, key, transfer):
        self[key] = yield from transfer


def pause(rounds):
    for _ in range(rounds):
        yield ()


def late(rounds, *arrays):
    for _ in range(rounds):
        yield ()
    return (yield arrays)


def in_pieces(array, axis, pieces):
    step = array.shape[0] // pieces
    landed = []
    for piece in range(pieces):
        landed.append((yield swap(array[piece * step : (piece + 1) * step], axis)))
    return jnp.concatenate(landed, axis=0)


def gather_dim(array, axis, dim):
    if lax.axis_size(axis) != 2:
        return lax.all_gather(array, axis, axis=dim, tiled=True)
    theirs = yield swap(array, axis)
    return pair(array, theirs, axis, dim)


def scatter_dim(array, axis, dim):
    if lax.axis_size(axis) != 2:
        return lax.psum_scatter(array, axis, scatter_dimension=dim, tiled=True)
    mine, theirs = halves(array, axis, dim)
    theirs = yield swap(theirs, axis)
    return mine + theirs


def exchange(array, axis, cut, joined, rounds=0):
    if lax.axis_size(axis) != 2:
        return lax.all_to_all(array, axis, cut, joined, tiled=True)
    mine, theirs = halves(array, axis, cut)
    (theirs,) = yield from late(rounds, swap(theirs, axis))
    return pair(mine, theirs, axis, joined)


def gather_plane(array, first, second, last, rounds=0):
    cut = -(-array.shape[0] // 32) * 16
    by_first, by_second = yield from late(rounds, swap(array, first), swap(array, second))
    low, high = yield (swap(by_second[:cut], first), swap(by_first[cut:], second))
    near = jnp.concatenate([array, by_first, by_second, low, high], axis=0)
    far = yield swap(near, last)
    return jnp.concatenate([near, far], axis=0)


def scatter_last(array, last):
    half = array.shape[0] // 2
    theirs = yield swap(array[half:], last)
    return array[:half] + theirs


def scatter_near(array, first, second):
    rows = array.shape[0] // 4
    cut = -(-rows // 32) * 16
    here, by_first, by_second, both = (array[i * rows : (i + 1) * rows] for i in range(4))
    low, high = yield (swap(both[:cut], first), swap(both[cut:], second))
    by_second = jnp.concatenate([by_second[:cut] + low, by_second[cut:]], axis=0)
    by_first = jnp.concatenate([by_first[:cut], by_first[cut:] + high], axis=0)
    by_first, by_second = yield (swap(by_first, first), swap(by_second, second))
    return here + by_first + by_second


def ring_size():
    return 4 if lax.axis_size("zh") == 2 else 0


def ring_shift(array, step):
    return lax.ppermute(array, ("zh", "zl"), [(i, (i + step) % 4) for i in range(4)])


def gather_ring(array):
    if not ring_size():
        return [lax.all_gather(array, SEQ, axis=0, tiled=True)]
    along, across = [array], []
    for step in range(3):
        coming = ring_shift(along[-1], 1)
        across.append(swap(along[-1], "y"))
        if step == 0:
            coming = yield coming
        else:
            coming, across[step - 1] = yield (coming, across[step - 1])
        along.append(coming)
    across.append(swap(along[-1], "y"))
    across[2], across[3] = yield (across[2], across[3])
    return [jnp.concatenate(blocks, axis=0) for blocks in zip(along, across)]


def scatter_ring(blocks):
    if not ring_size():
        return lax.psum_scatter(blocks[0], SEQ, scatter_dimension=0, tiled=True)
    half = blocks[0].shape[0] // 2
    across = swap(blocks[3][half:], "y")
    later = swap(blocks[2][half:], "y")
    across = yield across
    running = blocks[3][:half] + across
    for step in (2, 1, 0):
        across = later
        coming = ring_shift(running, -1)
        if step:
            later = swap(blocks[step - 1][half:], "y")
        coming, across = yield (coming, across)
        running = blocks[step][:half] + across + coming
    return running


def ring_order(shards):
    places = jnp.arange(shards, dtype=jnp.int32)
    if not ring_size():
        return places
    along = lax.axis_index(("zh", "zl"))
    return (along - places // 2) % 4 * 2 + (places % 2 ^ lax.axis_index("y"))


def columns_of_qkv(weights):
    array = weights.reshape((3,) + (1,) * len(AXES) + weights.shape[1:])
    for axis in SEQ:
        array = yield from exchange(array, axis, 7, AXES.index(axis) + 1)
    for axis in ROWS:
        array = yield from gather_dim(array, axis, AXES.index(axis) + 1)
    return array.reshape(3, -1, array.shape[-1])


def sums_of_qkv(sums):
    sizes = tuple(lax.axis_size(axis) for axis in AXES)
    array = sums.reshape((3,) + sizes + (-1, sums.shape[-1]))
    for axis in reversed(ROWS):
        array = yield from scatter_dim(array, axis, AXES.index(axis) + 1)
    for axis in reversed(SEQ):
        array = yield from exchange(array, axis, AXES.index(axis) + 1, 7)
    return array.reshape((3,) + array.shape[-2:])


def columns_of_ffn(weight):
    array = weight.reshape((1, 1, 1) + weight.shape)
    for axis in FFN_GROUP:
        array = yield from exchange(array, axis, 4, FFN_DIMS.index(axis))
    return array.reshape(-1, array.shape[-1])


def sums_of_ffn(sums):
    sizes = tuple(lax.axis_size(axis) for axis in FFN_DIMS)
    array = sums.reshape(sizes + (-1, sums.shape[-1]))
    for axis in reversed(FFN_GROUP):
        array = yield from exchange(array, axis, FFN_DIMS.index(axis), 4)
    return array.reshape(array.shape[-2:])


def near_blocks(array, axes, kept=()):
    sizes = [lax.axis_size(axis) for axis in AXES]
    lead = list(axes) + list(kept)
    depth = max(AXES.index(axis) for axis in lead) + 1
    lanes = array.shape[1] // math.prod(sizes[:depth])
    blocks = []
    for places in itertools.product(*(range(lax.axis_size(axis)) for axis in lead)):
        at = {axis: place for axis, place in zip(lead, places)}
        for axis in axes:
            at[axis] = relative(at[axis], axis)
        first = 0
        for axis, size in zip(AXES[:depth], sizes):
            first = first * size + at[axis]
        blocks.append(lax.dynamic_slice_in_dim(array, first * lanes, lanes, 1))
    return jnp.concatenate(blocks, axis=1)


def relative(place, axis):
    return place if lax.axis_size(axis) != 2 else lax.axis_index(axis) ^ place


def near_blocks_back(array, axes, kept):
    sizes = [lax.axis_size(axis) for axis in AXES]
    lead = list(axes) + list(kept)
    depth = max(AXES.index(axis) for axis in lead) + 1
    lanes = array.shape[1] // math.prod(sizes[:depth])
    blocks = []
    for places in itertools.product(*(range(size) for size in sizes[:depth])):
        at = dict(zip(AXES, places))
        first = 0
        for axis in lead:
            place = relative(at[axis], axis) if axis in axes else at[axis]
            first = first * lax.axis_size(axis) + place
        blocks.append(lax.dynamic_slice_in_dim(array, first * lanes, lanes, 1))
    return jnp.concatenate(blocks, axis=1)


def all_rows(parts):
    if lax.axis_size("zh") != 2:
        parts = [lax.all_gather(part, "zh", axis=0, tiled=True) for part in parts]
    return jnp.concatenate(parts, axis=0)


def part_of(sums, x, zh):
    rows = sums.shape[0] // 4
    first = (2 * x + zh) * rows
    return sums[first : first + rows]


def sums_over_all_zh(sums):
    half = sums.shape[0] // 2
    theirs = yield swap(sums[half:], "x")
    return lax.psum_scatter(sums[:half] + theirs, "zh", scatter_dimension=0, tiled=True)


def block_mask(col_ref, row_ref, sum_ref, first, rows, keys, segment, per_seg):
    query_docs = col_ref[0, first : first + rows, :]
    query_pos = first + lax.broadcasted_iota(jnp.int32, (rows, keys), 0)
    key_pos = lax.broadcasted_iota(jnp.int32, (rows, keys), 1)
    allowed = (key_pos <= query_pos) & (query_docs == row_ref[0, :, :keys])
    padded = sum_ref.shape[-1]
    place = lax.broadcasted_iota(jnp.int32, (rows, padded), 1)
    sum_allowed = (place < segment * per_seg) & (query_docs == sum_ref[...])
    return allowed, sum_allowed


def block_probs(query, key, sum_key, allowed, sum_allowed):
    scores = jnp.where(allowed, dot(query, key, 1, 1), MASKED)
    sum_scores = jnp.where(sum_allowed, dot(query, sum_key, 1, 1), MASKED)
    top = jnp.maximum(
        jnp.max(scores, axis=1, keepdims=True), jnp.max(sum_scores, axis=1, keepdims=True)
    )
    weights = jnp.exp(scores - top)
    sum_weights = jnp.exp(sum_scores - top)
    total = jnp.sum(weights, axis=1, keepdims=True) + jnp.sum(sum_weights, axis=1, keepdims=True)
    share = 1.0 / total
    return weights * share, sum_weights * share


def load_ordered(order_ref, refs, scratches):
    shards, _, here, _ = refs[0].shape
    for place in range(shards):
        block = order_ref[place]
        for ref, scratch in zip(refs, scratches):
            scratch[place * here : (place + 1) * here, :] = ref[block, 0]


def store_ordered(order_ref, refs, scratches):
    shards, _, here, _ = refs[0].shape
    for place in range(shards):
        block = order_ref[place]
        for ref, scratch in zip(refs, scratches):
            ref[block, 0] = scratch[place * here : (place + 1) * here, :].astype(ref.dtype)


def forward_kernel(
    per_seg, rows, order_ref, col_ref, row_ref, sum_ref, q_in, k_in, v_in, sk_ref, sv_ref, out_ref,
    q_ref, k_ref, v_ref, o_ref,
):
    segment = pl.program_id(1)
    load_ordered(order_ref, (q_in, k_in, v_in), (q_ref, k_ref, v_ref))
    length, width = q_ref.shape
    for first in range(0, length, rows):
        keys = first + rows
        allowed, sum_allowed = block_mask(
            col_ref, row_ref, sum_ref, first, rows, keys, segment, per_seg
        )
        for low in range(0, width, HEAD):
            cols = slice(low, low + HEAD)
            probs, sum_probs = block_probs(
                q_ref[first:keys, cols], k_ref[:keys, cols], sk_ref[:, cols], allowed, sum_allowed
            )
            out = dot(probs.astype(BF), v_ref[:keys, cols])
            out += dot(sum_probs.astype(BF), sv_ref[:, cols])
            o_ref[first:keys, cols] = out.astype(BF)
    here = out_ref.shape[2]
    for place in range(out_ref.shape[0]):
        out_ref[place, 0] = o_ref[place * here : (place + 1) * here, :]


def backward_kernel(
    per_seg, rows, order_ref, col_ref, row_ref, sum_ref, q_in, k_in, v_in, sk_ref, sv_ref, g_in,
    dq_out, dk_out, dv_out, dsk_ref, dsv_ref,
    q_ref, k_ref, v_ref, g_ref, dq_ref, dk_sum, dv_sum,
):
    segment = pl.program_id(1)
    load_ordered(order_ref, (q_in, k_in, v_in), (q_ref, k_ref, v_ref))
    here = g_in.shape[2]
    for place in range(g_in.shape[0]):
        g_ref[place * here : (place + 1) * here, :] = g_in[place, 0]
    length, width = q_ref.shape

    @pl.when(segment == 0)
    def _():
        dsk_ref[...] = jnp.zeros_like(dsk_ref)
        dsv_ref[...] = jnp.zeros_like(dsv_ref)

    dk_sum[...] = jnp.zeros_like(dk_sum)
    dv_sum[...] = jnp.zeros_like(dv_sum)
    for first in range(0, length, rows):
        keys = first + rows
        allowed, sum_allowed = block_mask(
            col_ref, row_ref, sum_ref, first, rows, keys, segment, per_seg
        )
        for low in range(0, width, HEAD):
            cols = slice(low, low + HEAD)
            query, grad = q_ref[first:keys, cols], g_ref[first:keys, cols]
            key, sum_key = k_ref[:keys, cols], sk_ref[:, cols]
            probs, sum_probs = block_probs(query, key, sum_key, allowed, sum_allowed)
            d_probs = dot(grad, v_ref[:keys, cols], 1, 1)
            d_sum_probs = dot(grad, sv_ref[:, cols], 1, 1)
            delta = jnp.sum(probs * d_probs, axis=1, keepdims=True)
            delta += jnp.sum(sum_probs * d_sum_probs, axis=1, keepdims=True)
            d_scores = (probs * (d_probs - delta)).astype(BF)
            d_sum_scores = (sum_probs * (d_sum_probs - delta)).astype(BF)
            d_query = (dot(d_scores, key) + dot(d_sum_scores, sum_key)).astype(BF)
            dq_ref[first:keys, cols] = (d_query.astype(F32) * 0.125).astype(BF)
            dk_sum[:keys, cols] += dot(d_scores, query, 0, 0)
            dv_sum[:keys, cols] += dot(probs.astype(BF), grad, 0, 0)
            dsk_ref[:, cols] += dot(d_sum_scores, query, 0, 0)
            dsv_ref[:, cols] += dot(sum_probs.astype(BF), grad, 0, 0)
    store_ordered(order_ref, (dq_out, dk_out, dv_out), (dq_ref, dk_sum, dv_sum))


def attention_calls(segs, shards, here, width, padded, per_seg):
    lanes = min(2 * HEAD, width)
    length = shards * here
    rows = 128 if length <= 512 else 256
    grid = (width // lanes, segs)
    tok = pl.BlockSpec((shards, 1, here, lanes), lambda h, s: (0, s, 0, h))
    summed = pl.BlockSpec((padded, lanes), lambda h, s: (0, h))
    docs = [
        pl.BlockSpec(memory_space=pltpu.SMEM),
        pl.BlockSpec((1, length, 1), lambda h, s: (s, 0, 0)),
        pl.BlockSpec((1, 1, length), lambda h, s: (s, 0, 0)),
        pl.BlockSpec((1, padded), lambda h, s: (0, 0)),
    ]
    params = pltpu.CompilerParams(
        dimension_semantics=("arbitrary", "arbitrary"), vmem_limit_bytes=24 * 2**20
    )
    tokens = jax.ShapeDtypeStruct((shards, segs, here, width), BF)
    sums = jax.ShapeDtypeStruct((padded, width), F32)
    narrow, wide = pltpu.VMEM((length, lanes), BF), pltpu.VMEM((length, lanes), F32)
    work = 2 * segs * length * (length // 2 + padded) * width
    forward = pl.pallas_call(
        functools.partial(forward_kernel, per_seg, rows),
        grid=grid,
        in_specs=docs + [tok] * 3 + [summed] * 2,
        out_specs=tok,
        out_shape=tokens,
        scratch_shapes=[narrow] * 4,
        compiler_params=params,
        cost_estimate=pl.CostEstimate(
            flops=120 * work, bytes_accessed=8 * segs * length * width, transcendentals=0
        ),
    )
    backward = pl.pallas_call(
        functools.partial(backward_kernel, per_seg, rows),
        grid=grid,
        in_specs=docs + [tok] * 3 + [summed] * 2 + [tok],
        out_specs=[tok] * 3 + [summed] * 2,
        out_shape=[tokens] * 3 + [sums] * 2,
        scratch_shapes=[narrow] * 5 + [wide] * 2,
        compiler_params=params,
        cost_estimate=pl.CostEstimate(
            flops=160 * work, bytes_accessed=14 * segs * length * width, transcendentals=0
        ),
    )
    return forward, backward


def gelu_both(inputs):
    share = 0.5 * (1.0 + lax.erf(inputs * SQRT_HALF))
    slope = share + inputs * jnp.exp(-0.5 * inputs * inputs) * NORMAL_PEAK
    return inputs * share, slope


def per_device(
    tokens, summary, doc_ids, gain_attn, gain_ffn, w_query, w_key, w_value, w_out, w_up, w_down,
    cotangent,
):
    _, segs, here, model = tokens.shape
    per_seg = summary.shape[2]
    sum_rows = summary.shape[1] * per_seg
    padded = -(-sum_rows // 128) * 128
    length = doc_ids.shape[2]
    shards = length // here
    rows = segs * here
    shard_rows = w_query.shape[0]
    width = model // shards

    place = lax.axis_index(SEQ)

    flat = tokens.reshape(rows, model).astype(F32)
    standard, inverse = normalize(flat)
    hidden = (standard * gain_attn).astype(BF)
    cot = cotangent.reshape(rows, model)
    summary_flat = summary.reshape(sum_rows, model).astype(F32)
    summary_pad = jnp.pad(summary_flat, ((0, padded - sum_rows), (0, 0)))
    standard_sum, inverse_sum = normalize(summary_pad)
    hidden_sum = (standard_sum * gain_attn).astype(BF)

    docs = doc_ids.reshape(segs, length)
    last_docs = jnp.repeat(docs[: segs - 1, length - 1], per_seg)
    sum_docs = jnp.pad(last_docs, (0, padded - sum_rows), constant_values=-1)[None]
    doc_args = (ring_order(shards), docs[:, :, None], docs[:, None, :], sum_docs)
    attend, attend_back = attention_calls(segs, shards, here, width, padded, per_seg)
    split = (shards, segs, here, width)
    block_rows = shards * rows // max(ring_size(), 1)

    box = Box()
    out = {}

    half_sums = -(-sum_rows // 2)

    def in_halves(array):
        array = jnp.pad(array[:sum_rows], ((0, 2 * half_sums - sum_rows), (0, 0)))
        return array.reshape(2, half_sums, -1)

    def ready_early():
        yield ()
        place_y = lax.axis_index("y")
        sum_parts = [
            lax.dynamic_index_in_dim(in_halves(array), place_y, 0, False)
            for array in (standard_sum, inverse_sum)
        ]
        ready = yield (doc_args, hidden_sum, sum_parts)
        box["doc_args"], box["hidden_sum"], box["sum_parts"] = ready

    def critical():
        hidden_blocks = yield from gather_ring(hidden)
        box["A"] = True
        w_qkv = yield from box.wait("w_qkv")
        doc_args, hidden_sum = box["doc_args"], box["hidden_sum"]
        def project(weight, scale=1.0):
            blocks = [(dot(block, weight) * scale).astype(BF) for block in hidden_blocks]
            return jnp.concatenate(blocks, axis=0).reshape(split)

        operands = [project(w_qkv[0], 0.125), project(w_qkv[1]), project(w_qkv[2])]
        operands += [dot(hidden_sum, w_qkv[1]).astype(BF), dot(hidden_sum, w_qkv[2]).astype(BF)]
        operands = yield operands
        attended = yield attend(*doc_args, *operands)

        box["C"] = True
        attended = attended.reshape(shards, rows, width)
        attended = yield lax.all_to_all(attended, SEQ, 0, 0, tiled=True)
        attended = near_blocks(attended.swapaxes(0, 1).reshape(rows, model), ROWS)
        w_out_all = yield from box.wait("w_out")
        summed = dot(attended, w_out_all)
        mixed = flat + summed
        standard_ffn, inverse_ffn = normalize(mixed)
        normed = near_blocks((standard_ffn * gain_ffn).astype(BF), FFN_REST, ("c",))
        box["D"] = True

        normed_all = yield from gather_plane(normed, *FFN_NEAR)
        cot_all = yield from box.wait("cot_all")
        w_up_here = yield from box.wait("w_up")
        active, slope = gelu_both(dot(normed_all, w_up_here))
        active = active.astype(BF)
        d_w_down = dot(cot_all, active, 0, 0).astype(BF)
        active, slope, d_w_down = yield (active, slope, d_w_down)
        box["d_w_down"] = d_w_down
        w_down_here = yield from box.wait("w_down")
        grad_upper = (slope * dot(cot_all, w_down_here)).astype(BF)
        grad_normed_part = dot(grad_upper, w_up_here, 1, 1).astype(BF)
        scatter = scatter_last(grad_normed_part, FFN_NEAR[2])
        in_flight = next(scatter)
        d_w_up = dot(normed_all, grad_upper, 0, 0).astype(BF)
        in_flight, d_w_up = yield (in_flight, d_w_up)
        box["d_w_up"] = d_w_up
        try:
            scatter.send(in_flight)
        except StopIteration as end:
            near = scatter_near(end.value, *FFN_NEAR[:2])
        in_flight = next(near)
        ffn_out_part = dot(active, w_down_here, 1, 1).astype(BF)
        in_flight, ffn_out_part = yield (in_flight, ffn_out_part)
        box["ffn_out_part"] = ffn_out_part
        in_flight = yield near.send(in_flight)
        try:
            near.send(in_flight)
        except StopIteration as end:
            grad_normed = near_blocks_back(end.value, FFN_REST, ("c",)).astype(F32)
        grad_mixed = cot.astype(F32) + normalize_back(
            grad_normed, gain_ffn, standard_ffn, inverse_ffn
        )

        grad_branch = grad_mixed.astype(BF)
        grad_attended = near_blocks(dot(grad_branch, w_out_all, 1, 1).astype(BF), ROWS)
        grad_attended = grad_attended.reshape(rows, shards, width).swapaxes(0, 1)
        box["d_w_out"] = dot(attended, grad_branch, 0, 0).astype(BF)
        grad_attended = yield lax.all_to_all(grad_attended, SEQ, 0, 0, tiled=True)
        grads = yield attend_back(*doc_args, *operands, grad_attended.reshape(split))

        box["F"] = True
        d_qkv = [part.reshape(shards * rows, width) for part in grads[:3]]
        d_sums = [part.astype(BF) for part in grads[3:]]

        def grad_block(first):
            parts = [dot(d[first : first + block_rows], w, 1, 1) for d, w in zip(d_qkv, w_qkv)]
            return sum(parts).astype(BF)

        grad_hidden_blocks = [grad_block(i) for i in range(0, shards * rows, block_rows)]
        grad_sum_part = sum(dot(d, w, 1, 1) for d, w in zip(d_sums, w_qkv[1:])).astype(BF)
        left = jnp.concatenate(hidden_blocks + [hidden_sum], axis=0)
        d_w_qkv = [dot(left[: shards * rows], d_qkv[0], 0, 0).astype(BF)]
        for d, d_sum in zip(d_qkv[1:], d_sums):
            d_w_qkv.append(dot(left, jnp.concatenate([d, d_sum], axis=0), 0, 0).astype(BF))
        d_w_qkv = jnp.stack(d_w_qkv)
        box["sums"] = grad_sum_part
        scatter = scatter_ring(grad_hidden_blocks)
        try:
            in_flight = next(scatter)
            in_flight, d_w_qkv = yield (in_flight, d_w_qkv)
            box["d_w_qkv"] = d_w_qkv
            while True:
                in_flight = yield scatter.send(in_flight)
        except StopIteration as end:
            grad_hidden = end.value.astype(F32)
        box["d_w_qkv"] = d_w_qkv
        out["d_tokens"] = grad_mixed + normalize_back(grad_hidden, gain_attn, standard, inverse)
        ffn_out = yield from box.wait("ffn_out")
        ffn_out = near_blocks_back(ffn_out, FFN_REST, ("c",))
        out["activations"] = (mixed + ffn_out.astype(F32)).astype(BF)

    def cotangent_rows():
        yield from box.wait("A")
        yield from pause(2)
        box["cot_all"] = yield from gather_plane(near_blocks(cot, FFN_REST, ("c",)), *FFN_NEAR)

    def weight_up():
        part = yield from columns_of_ffn(w_up)
        box["up"] = part
        far = []
        if lax.axis_size("zh") == 2:
            far = [(yield from in_pieces(part, "zh", 4))]
            far.append((yield swap(far[0], "x")))
        part_x = yield from box.wait("up_x")
        box["w_up"] = all_rows([part] + far[:1] + [part_x] + far[1:])

    def weight_up_x():
        part = yield from box.wait("up")
        yield from pause(3)
        box["up_x"] = yield swap(part, "x")

    def weight_down():
        yield from pause(1)
        part = yield from columns_of_ffn(w_down)
        box["down"] = part
        yield from box.wait("C")
        far = far_x = []
        if lax.axis_size("zh") == 2:
            half = part.shape[0] // 2
            step = half // 2
            low = yield swap(part[:half], "zh")
            third = yield swap(part[half : half + step], "zh")
            fourth, low_x = yield (swap(part[half + step :], "zh"), swap(low, "x"))
            high = jnp.concatenate([third, fourth], axis=0)
            yield ()
            high_x = yield swap(high, "x")
            far, far_x = [low, high], [low_x, high_x]
        part_x = yield from box.wait("down_x")
        box["w_down"] = all_rows([part, *far, part_x, *far_x])

    def weight_down_x():
        yield from box.wait("C")
        part = yield from box.wait("down")
        yield from box.put("down_x", in_pieces(part, "x", 2))

    def weight_out():
        yield from pause(2)
        array = w_out.reshape((1,) * len(AXES) + w_out.shape)
        for axis in ("zh", "zl"):
            array = yield from gather_dim(array, axis, AXES.index(axis))
        yield from box.wait("A")
        half = array.shape[-1] // 2
        by_x, by_y = yield (swap(array, "x"), swap(array, "y"))
        low, high = yield (swap(by_y[..., :half], "x"), swap(by_x[..., half:], "y"))
        both = jnp.concatenate([low, high], axis=-1)
        dim_y = AXES.index("y")
        near = pair(array, by_y, "y", dim_y).reshape(-1, model)
        far = pair(by_x, both, "y", dim_y).reshape(-1, model)
        near_c, far_c = yield (swap(near, "c"), swap(far, "c"))
        box["w_out"] = jnp.concatenate([near, near_c, far, far_c], axis=0)

    def out_back():
        array = yield from box.wait("d_w_out")
        rows_c = model // 4
        near, near_c, far, far_c = (array[i * rows_c : (i + 1) * rows_c] for i in range(4))
        near_c, far_c = yield (swap(near_c, "c"), swap(far_c, "c"))
        near, far = near + near_c, far + far_c
        half = rows_c // 2
        low = yield swap(far[:half], "x")
        high = yield swap(far[half:], "x")
        array = near + jnp.concatenate([low, high], axis=0)
        seq_sizes = tuple(lax.axis_size(axis) for axis in SEQ)
        array = array.reshape((1, 1) + seq_sizes + (shard_rows, model))
        yield from pause(3)
        for axis in ("y", "zl", "zh"):
            array = yield from scatter_dim(array, axis, AXES.index(axis))
        out["d_w_out"] = array.reshape(shard_rows, model).astype(F32)

    def down_back():
        sums = yield from box.wait("d_w_down")
        if lax.axis_size("zh") != 2:
            array = yield from sums_over_all_zh(sums)
        else:
            far, sent = part_of(sums, 0, 1), part_of(sums, 1, 1)
            near = part_of(sums, 1, 0)
            half = far.shape[0] // 2
            step = half // 2
            low = (yield swap(sent[:half], "x")) + far[:half]
            first, high = yield (swap(low[:step], "zh"), swap(sent[half:], "x"))
            high = high + far[half:]
            second = yield swap(low[step:], "zh")
            third, near = yield (swap(high, "zh"), swap(near, "x"))
            far = jnp.concatenate([first, second, third], axis=0)
            array = part_of(sums, 0, 0) + near + far
        yield from box.wait("F")
        array = yield from sums_of_ffn(array)
        out["d_w_down"] = array.astype(F32)

    def up_back():
        sums = yield from box.wait("d_w_up")
        if lax.axis_size("zh") != 2:
            array = yield from sums_over_all_zh(sums)
        else:
            far, sent = part_of(sums, 0, 1), part_of(sums, 1, 1)
            near = part_of(sums, 1, 0)
            yield ()
            far = far + (yield from in_pieces(sent, "x", 2))
            half = far.shape[0] // 2
            step = half // 2
            low = yield swap(far[:half], "zh")
            third = yield swap(far[half : half + step], "zh")
            fourth, near = yield (swap(far[half + step :], "zh"), swap(near, "x"))
            far = jnp.concatenate([low, third, fourth], axis=0)
            array = part_of(sums, 0, 0) + near + far
            yield ()
        array = yield from sums_of_ffn(array)
        out["d_w_up"] = array.astype(F32)

    def activations_back():
        part = yield from box.wait("ffn_out_part")
        part = yield from scatter_last(part, FFN_NEAR[2])
        box["ffn_out"] = yield from scatter_near(part, *FFN_NEAR[:2])

    def qkv_back():
        array = yield from box.wait("d_w_qkv")
        array = yield from sums_of_qkv(array)
        array = array.astype(F32)
        out["d_w_query"], out["d_w_key"], out["d_w_value"] = array

    def sums_back():
        grad_sum_part = yield from box.wait("sums")
        yield ()
        array = yield from scatter_dim(in_halves(grad_sum_part), "y", 0)
        for axis in ("zl", "zh"):
            if lax.axis_size(axis) == 2:
                theirs = yield swap(array, axis)
                array = array + theirs
            else:
                array = lax.psum(array, axis)
        grad_sum = array[0].astype(F32)
        standard_part, inverse_part = box["sum_parts"]
        part = normalize_back(grad_sum, gain_attn, standard_part, inverse_part).astype(BF)
        theirs = yield swap(part, "y")
        part = pair(part[None], theirs[None], "y", 0).reshape(2 * half_sums, model)
        out["d_summary"] = part[:sum_rows].astype(F32)

    together(
        critical=critical(),
        ready_early=ready_early(),
        weight_qkv=box.put("w_qkv", columns_of_qkv(jnp.stack([w_query, w_key, w_value]))),
        weight_up=weight_up(),
        weight_up_x=weight_up_x(),
        weight_down=weight_down(),
        weight_down_x=weight_down_x(),
        cotangent_rows=cotangent_rows(),
        weight_out=weight_out(),
        out_back=out_back(),
        down_back=down_back(),
        up_back=up_back(),
        activations_back=activations_back(),
        sums_back=sums_back(),
        qkv_back=qkv_back(),
    )

    def gain_sum(gain, *pairs):
        total = sum(jnp.sum(w.astype(F32) * d, axis=1) for w, d in pairs)
        shard = lax.axis_index(AXES)
        return total / lax.dynamic_slice_in_dim(gain, shard * shard_rows, shard_rows, 0)

    d_gain_attn = gain_sum(
        gain_attn,
        (w_query, out["d_w_query"]),
        (w_key, out["d_w_key"]),
        (w_value, out["d_w_value"]),
    )
    d_gain_ffn = gain_sum(gain_ffn, (w_up, out["d_w_up"]))
    return (
        out["activations"].reshape(tokens.shape),
        out["d_tokens"].reshape(tokens.shape),
        out["d_summary"].reshape(summary.shape),
        d_gain_attn,
        d_gain_ffn,
        out["d_w_query"],
        out["d_w_key"],
        out["d_w_value"],
        out["d_w_out"],
        out["d_w_up"],
        out["d_w_down"],
    )


def solution(mesh):
    rows, seq = mesh.shape["rows"], mesh.shape["seq"]
    fine = Mesh(mesh.devices.reshape(rows // 2, 2, seq // 4, 2, 2), AXES)
    by_token = P(ROWS, None, SEQ, None)
    by_row = P(ROWS, None, None, None)
    weight = P(AXES, None)
    return jax.shard_map(
        per_device,
        mesh=fine,
        in_specs=(by_token, by_row, P(ROWS, None, None), P(), P())
        + (weight,) * 6
        + (by_token,),
        out_specs=(by_token, by_token, by_row, P(AXES), P(AXES)) + (weight,) * 6,
        check_vma=False,
    )
```

```python
import functools
import itertools
import math

import jax
import jax.numpy as jnp
from jax import lax
from jax.experimental import pallas as pl
from jax.experimental.pallas import tpu as pltpu
from jax.sharding import Mesh, PartitionSpec as P

HEAD = 64
EPSILON = 1e-05
MASKED = -1e30
SQRT_HALF = 0.7071067811865476
NORMAL_PEAK = 0.3989422804014327

AXES = ("x", "c", "zh", "zl", "y")
ROWS = ("x", "c")
SEQ = ("zh", "zl", "y")
FFN_GROUP = ("c", "y", "zl")
FFN_DIMS = ("c", "zl", "y")
FFN_NEAR = ("y", "zl", "c")
FFN_REST = ("x", "zh")
BF = jnp.bfloat16
F32 = jnp.float32


def dot(left, right, left_dim=1, right_dim=0):
    return lax.dot_general(
        left, right, (((left_dim,), (right_dim,)), ((), ())), preferred_element_type=F32
    )


def normalize(inputs):
    average = jnp.mean(inputs, axis=-1, keepdims=True)
    centred = inputs - average
    inverse = lax.rsqrt(jnp.mean(centred * centred, axis=-1, keepdims=True) + EPSILON)
    return centred * inverse, inverse


def normalize_back(upstream, scaling, standard, inverse):
    scaled = upstream * scaling
    return inverse * (
        scaled
        - jnp.mean(scaled, axis=-1, keepdims=True)
        - standard * jnp.mean(scaled * standard, axis=-1, keepdims=True)
    )


def swap(array, axis):
    return lax.ppermute(array, axis, [(0, 1), (1, 0)])


def pair(mine, theirs, axis, dim):
    first = lax.axis_index(axis) == 0
    return jnp.concatenate(
        [jnp.where(first, mine, theirs), jnp.where(first, theirs, mine)], axis=dim
    )


def halves(array, axis, dim):
    half = array.shape[dim] // 2
    place = lax.axis_index(axis)
    return (
        lax.dynamic_slice_in_dim(array, place * half, half, dim),
        lax.dynamic_slice_in_dim(array, (1 - place) * half, half, dim),
    )


def together(**transfers):
    flying = {}

    def advance(name, sent):
        try:
            with jax.named_scope(name):
                flying[name] = transfers[name].send(sent)
        except StopIteration:
            flying.pop(name, None)

    for name in transfers:
        advance(name, None)
    while flying:
        landed = lax.optimization_barrier(dict(flying))
        for name in transfers:
            if name in landed:
                advance(name, landed[name])


class Box(dict):
    def wait(self, key):
        while key not in self:
            yield ()
        return self[key]

    def put(self, key, transfer):
        self[key] = yield from transfer


def pause(rounds):
    for _ in range(rounds):
        yield ()


def in_pieces(array, axis, *pieces):
    first, landed = 0, []
    for piece in pieces:
        count = array.shape[0] * piece // sum(pieces)
        landed.append((yield swap(array[first : first + count], axis)))
        first += count
    return landed


def one_round(array, axis):
    theirs = swap(array, axis)
    if axis != "c":
        theirs = yield theirs
    return theirs


def gather_dim(array, axis, dim):
    if lax.axis_size(axis) != 2:
        return lax.all_gather(array, axis, axis=dim, tiled=True)
    theirs = yield from one_round(array, axis)
    return pair(array, theirs, axis, dim)


def scatter_dim(array, axis, dim):
    if lax.axis_size(axis) != 2:
        return lax.psum_scatter(array, axis, scatter_dimension=dim, tiled=True)
    mine, theirs = halves(array, axis, dim)
    theirs = yield from one_round(theirs, axis)
    return mine + theirs


def exchange(array, axis, cut, joined):
    if lax.axis_size(axis) != 2:
        return lax.all_to_all(array, axis, cut, joined, tiled=True)
    mine, theirs = halves(array, axis, cut)
    theirs = yield from one_round(theirs, axis)
    return pair(mine, theirs, axis, joined)


def gather_plane(array, first, second, last):
    cut = -(-array.shape[0] // 32) * 16
    by_first, by_second = yield (swap(array, first), swap(array, second))
    low, high = yield (swap(by_second[:cut], first), swap(by_first[cut:], second))
    near = jnp.concatenate([array, by_first, by_second, low, high], axis=0)
    return jnp.concatenate([near, swap(near, last)], axis=0)


def scatter_plane(array, first, second, last):
    half = array.shape[0] // 2
    array = array[:half] + swap(array[half:], last)
    rows = array.shape[0] // 4
    cut = -(-rows // 32) * 16
    here, by_first, by_second, both = (array[i * rows : (i + 1) * rows] for i in range(4))
    low, high = yield (swap(both[:cut], first), swap(both[cut:], second))
    by_second = jnp.concatenate([by_second[:cut] + low, by_second[cut:]], axis=0)
    by_first = jnp.concatenate([by_first[:cut], by_first[cut:] + high], axis=0)
    by_first, by_second = yield (swap(by_first, first), swap(by_second, second))
    return here + by_first + by_second


def scatter_line(array):
    if not ring_size():
        array = lax.psum_scatter(array, "zh", scatter_dimension=0, tiled=True)
        return lax.psum_scatter(array, "zl", scatter_dimension=1, tiled=True)[0, 0]
    blocks = array.reshape((4,) + array.shape[2:])
    here = lax.axis_index(("zh", "zl"))
    mine = lax.dynamic_index_in_dim(blocks, here, 0, False)
    theirs = yield tuple(
        lax.ppermute(
            lax.dynamic_index_in_dim(blocks, here ^ step, 0, False),
            ("zh", "zl"),
            [(i, i ^ step) for i in range(4)],
        )
        for step in (1, 2, 3)
    )
    return mine + theirs[0] + theirs[1] + theirs[2]


def ring_size():
    return 4 if lax.axis_size("zh") == 2 else 0


def ring_shift(array, step):
    return lax.ppermute(array, ("zh", "zl"), [(i, (i + step) % 4) for i in range(4)])


def gather_ring(array):
    if not ring_size():
        return [lax.all_gather(array, SEQ, axis=0, tiled=True)]
    along, across = [array], []
    for step in range(3):
        coming = ring_shift(along[-1], 1)
        across.append(swap(along[-1], "y"))
        if step == 0:
            coming = yield coming
        else:
            coming, across[step - 1] = yield (coming, across[step - 1])
        along.append(coming)
    across.append(swap(along[-1], "y"))
    across[2], across[3] = yield (across[2], across[3])
    return [jnp.concatenate(blocks, axis=0) for blocks in zip(along, across)]


def scatter_ring(blocks):
    if not ring_size():
        return lax.psum_scatter(blocks[0], SEQ, scatter_dimension=0, tiled=True)
    half = blocks[0].shape[0] // 2
    across = swap(blocks[3][half:], "y")
    later = swap(blocks[2][half:], "y")
    across = yield across
    running = blocks[3][:half] + across
    for step in (2, 1, 0):
        across = later
        coming = ring_shift(running, -1)
        if step:
            later = swap(blocks[step - 1][half:], "y")
        coming, across = yield (coming, across)
        running = blocks[step][:half] + across + coming
    return running


def ring_order(shards):
    places = jnp.arange(shards, dtype=jnp.int32)
    if not ring_size():
        return places
    along = lax.axis_index(("zh", "zl"))
    return (along - places // 2) % 4 * 2 + (places % 2 ^ lax.axis_index("y"))


def columns_of_qkv(weights):
    array = weights.reshape((3,) + (1,) * len(AXES) + weights.shape[1:])
    for axis in SEQ:
        array = yield from exchange(array, axis, 7, AXES.index(axis) + 1)
    for axis in ROWS:
        array = yield from gather_dim(array, axis, AXES.index(axis) + 1)
    return array.reshape(3, -1, array.shape[-1])


def sums_of_qkv(sums):
    sizes = tuple(lax.axis_size(axis) for axis in AXES)
    array = sums.reshape((3,) + sizes + (-1, sums.shape[-1]))
    for axis in reversed(ROWS):
        array = yield from scatter_dim(array, axis, AXES.index(axis) + 1)
    for axis in reversed(SEQ):
        array = yield from exchange(array, axis, AXES.index(axis) + 1, 7)
    return array.reshape((3,) + array.shape[-2:])


def exchange_first(weight):
    array = weight.reshape((1, 1, 1) + weight.shape)
    for axis in FFN_GROUP[:-1]:
        array = yield from exchange(array, axis, 4, FFN_DIMS.index(axis))
    return array


def exchange_last(array):
    axis = FFN_GROUP[-1]
    array = yield from exchange(array, axis, 4, FFN_DIMS.index(axis))
    return array.reshape(-1, array.shape[-1])


def sums_of_ffn(sums, wait=0):
    sizes = tuple(lax.axis_size(axis) for axis in FFN_DIMS)
    array = sums.reshape(sizes + (-1, sums.shape[-1]))
    for axis in reversed(FFN_GROUP):
        array = yield from exchange(array, axis, FFN_DIMS.index(axis), 4)
        if axis == FFN_GROUP[-1]:
            yield from pause(wait)
    return array.reshape(array.shape[-2:])


def near_blocks(array, axes, kept=()):
    sizes = [lax.axis_size(axis) for axis in AXES]
    lead = list(axes) + list(kept)
    depth = max(AXES.index(axis) for axis in lead) + 1
    lanes = array.shape[1] // math.prod(sizes[:depth])
    firsts = []
    for places in itertools.product(*(range(lax.axis_size(axis)) for axis in lead)):
        at = {axis: place for axis, place in zip(lead, places)}
        for axis in axes:
            at[axis] = relative(at[axis], axis)
        first = 0
        for axis, size in zip(AXES[:depth], sizes):
            first = first * size + at[axis]
        firsts.append(first)
    return reorder(array, firsts, lanes)


def reorder(array, firsts, lanes):
    def kernel(firsts_ref, array_ref, out_ref):
        for place in range(len(firsts)):
            first = pl.multiple_of(firsts_ref[place] * lanes, 128)
            out_ref[:, place * lanes : (place + 1) * lanes] = array_ref[:, pl.ds(first, lanes)]

    return pl.pallas_call(
        kernel,
        in_specs=[pl.BlockSpec(memory_space=pltpu.SMEM), pl.BlockSpec(memory_space=pltpu.VMEM)],
        out_specs=pl.BlockSpec(memory_space=pltpu.VMEM),
        out_shape=jax.ShapeDtypeStruct(array.shape, array.dtype),
        compiler_params=pltpu.CompilerParams(vmem_limit_bytes=8 * 2**20),
    )(jnp.stack([jnp.int32(first) for first in firsts]), array)


def relative(place, axis):
    return place if lax.axis_size(axis) != 2 else lax.axis_index(axis) ^ place


def near_blocks_back(array, axes, kept):
    sizes = [lax.axis_size(axis) for axis in AXES]
    lead = list(axes) + list(kept)
    depth = max(AXES.index(axis) for axis in lead) + 1
    lanes = array.shape[1] // math.prod(sizes[:depth])
    firsts = []
    for places in itertools.product(*(range(size) for size in sizes[:depth])):
        at = dict(zip(AXES, places))
        first = 0
        for axis in lead:
            place = relative(at[axis], axis) if axis in axes else at[axis]
            first = first * lax.axis_size(axis) + place
        firsts.append(first)
    return reorder(array, firsts, lanes)


def all_rows(parts):
    if lax.axis_size("zh") != 2:
        parts = [lax.all_gather(part, "zh", axis=0, tiled=True) for part in parts]
    return jnp.concatenate(parts, axis=0)


def part_of(sums, x, zh):
    rows = sums.shape[0] // 4
    first = (2 * x + zh) * rows
    return sums[first : first + rows]


def sums_over_all_zh(sums):
    half = sums.shape[0] // 2
    theirs = yield swap(sums[half:], "x")
    return lax.psum_scatter(sums[:half] + theirs, "zh", scatter_dimension=0, tiled=True)


def load_ordered(order_ref, refs, scratches, first=0):
    shards, _, here, _ = refs[0].shape
    for place in range(shards):
        block = order_ref[place]
        for ref, scratch in zip(refs, scratches):
            scratch[first + place * here : first + (place + 1) * here, :] = ref[block, 0]


def block_mask(doc_col_ref, doc_row_ref, pos_row_ref, first, rows, keys):
    query_pos = first + lax.broadcasted_iota(jnp.int32, (rows, 1), 0)
    in_reach = pos_row_ref[0, :, :keys] <= query_pos
    return in_reach & (doc_row_ref[0, :, :keys] == doc_col_ref[0, first : first + rows, :])


def heads_of(width):
    lane = lax.broadcasted_iota(jnp.int32, (1, width), 1) // HEAD
    return [lane == head for head in range(width // HEAD)]


def of_heads(parts, heads):
    total = parts[0]
    for part, head in zip(parts[1:], heads[1:]):
        total = jnp.where(head, part, total)
    return total


def block_probs(query, key, allowed):
    scores = jnp.where(allowed, dot(query, key, 1, 1), MASKED)
    weights = jnp.exp(scores - jnp.max(scores, axis=1, keepdims=True))
    return weights * (1.0 / jnp.sum(weights, axis=1, keepdims=True))


def forward_kernel(
    rows, order_ref, doc_col_ref, doc_row_ref, pos_row_ref, q_in, k_in, v_in, sk_ref, sv_ref, out_ref,
    q_ref, k_ref, v_ref,
):
    shards, _, here, width = out_ref.shape
    padded = sk_ref.shape[0]
    k_ref[:padded, :], v_ref[:padded, :] = sk_ref[...], sv_ref[...]
    load_ordered(order_ref, (q_in,), (q_ref,))
    load_ordered(order_ref, (k_in, v_in), (k_ref, v_ref), padded)
    heads = heads_of(width)
    for first in range(0, shards * here, rows):
        keys = padded + first + rows
        allowed = block_mask(doc_col_ref, doc_row_ref, pos_row_ref, first, rows, keys)
        query, key, value = q_ref[first : first + rows, :], k_ref[:keys, :], v_ref[:keys, :]
        outs = []
        for head in heads:
            probs = block_probs(jnp.where(head, query, jnp.zeros_like(query)), key, allowed)
            outs.append(dot(probs.astype(BF), value))
        q_ref[first : first + rows, :] = of_heads(outs, heads).astype(BF)
    for place in range(shards):
        out_ref[place, 0] = q_ref[place * here : (place + 1) * here, :]


def backward_kernel(
    rows, order_ref, doc_col_ref, doc_row_ref, pos_row_ref, q_in, k_in, v_in, sk_ref, sv_ref, g_in,
    dq_out, dk_out, dv_out, dsk_ref, dsv_ref,
    q_ref, k_ref, v_ref, g_ref, dk_sum, dv_sum,
):
    shards, _, here, width = g_in.shape
    padded = sk_ref.shape[0]
    k_ref[:padded, :], v_ref[:padded, :] = sk_ref[...], sv_ref[...]
    load_ordered(order_ref, (q_in,), (q_ref,))
    load_ordered(order_ref, (k_in, v_in), (k_ref, v_ref), padded)
    for place in range(shards):
        g_ref[place * here : (place + 1) * here, :] = g_in[place, 0]

    @pl.when(pl.program_id(1) == 0)
    def _():
        dsk_ref[...] = jnp.zeros_like(dsk_ref)
        dsv_ref[...] = jnp.zeros_like(dsv_ref)

    heads = heads_of(width)
    for first in reversed(range(0, shards * here, rows)):
        keys = padded + first + rows
        last = first + rows == shards * here
        allowed = block_mask(doc_col_ref, doc_row_ref, pos_row_ref, first, rows, keys)
        query, grad = q_ref[first : first + rows, :], g_ref[first : first + rows, :]
        key, value = k_ref[:keys, :], v_ref[:keys, :]
        query_t, grad_t = query.T, grad.T
        d_queries = []
        for place, head in enumerate(heads):
            probs = block_probs(jnp.where(head, query, jnp.zeros_like(query)), key, allowed)
            d_probs = dot(jnp.where(head, grad, jnp.zeros_like(grad)), value, 1, 1)
            product = probs * d_probs
            delta = jnp.sum(product, axis=1, keepdims=True)
            d_scores = (product - probs * delta).astype(BF)
            d_queries.append(dot(d_scores, key))
            lanes = slice(place * HEAD, (place + 1) * HEAD)
            d_key = dot(query_t[lanes], d_scores)
            d_value = dot(grad_t[lanes], probs.astype(BF))
            if last:
                dk_sum[lanes, :], dv_sum[lanes, :] = d_key, d_value
            else:
                dk_sum[lanes, :keys] += d_key
                dv_sum[lanes, :keys] += d_value
        d_query = of_heads(d_queries, heads).astype(BF)
        q_ref[first : first + rows, :] = (d_query.astype(F32) * 0.125).astype(BF)
    d_key, d_value = dk_sum[...].T, dv_sum[...].T
    dsk_ref[...] += d_key[:padded]
    dsv_ref[...] += d_value[:padded]
    k_ref[...], v_ref[...] = d_key.astype(BF), d_value.astype(BF)
    for place in range(shards):
        block = order_ref[place]
        tokens = slice(place * here, (place + 1) * here)
        dq_out[block, 0] = q_ref[tokens, :]
        tokens = slice(padded + place * here, padded + (place + 1) * here)
        dk_out[block, 0], dv_out[block, 0] = k_ref[tokens, :], v_ref[tokens, :]


def attention_calls(segs, shards, here, width, padded):
    lanes = min(4 * HEAD, width)
    length = shards * here
    rows = length if length <= 512 else 384
    grid = (width // lanes, segs)
    tok = pl.BlockSpec((shards, 1, here, lanes), lambda h, s: (0, s, 0, h))
    summed = pl.BlockSpec((padded, lanes), lambda h, s: (0, h))
    row = pl.BlockSpec((1, 1, padded + length), lambda h, s: (s, 0, 0))
    docs = [
        pl.BlockSpec(memory_space=pltpu.SMEM),
        pl.BlockSpec((1, length, 1), lambda h, s: (s, 0, 0)),
        row,
        row,
    ]
    params = pltpu.CompilerParams(
        dimension_semantics=("arbitrary", "arbitrary"), vmem_limit_bytes=24 * 2**20
    )
    tokens = jax.ShapeDtypeStruct((shards, segs, here, width), BF)
    sums = jax.ShapeDtypeStruct((padded, width), F32)
    queries, keys = pltpu.VMEM((length, lanes), BF), pltpu.VMEM((padded + length, lanes), BF)
    key_sums = pltpu.VMEM((lanes, padded + length), F32)
    work = 2 * segs * length * (length // 2 + padded) * width
    forward = pl.pallas_call(
        functools.partial(forward_kernel, rows),
        grid=grid,
        in_specs=docs + [tok] * 3 + [summed] * 2,
        out_specs=tok,
        out_shape=tokens,
        scratch_shapes=[queries, keys, keys],
        compiler_params=params,
        cost_estimate=pl.CostEstimate(
            flops=120 * work, bytes_accessed=8 * segs * length * width, transcendentals=0
        ),
    )
    backward = pl.pallas_call(
        functools.partial(backward_kernel, rows),
        grid=grid,
        in_specs=docs + [tok] * 3 + [summed] * 2 + [tok],
        out_specs=[tok] * 3 + [summed] * 2,
        out_shape=[tokens] * 3 + [sums] * 2,
        scratch_shapes=[queries, keys, keys, queries, key_sums, key_sums],
        compiler_params=params,
        cost_estimate=pl.CostEstimate(
            flops=160 * work, bytes_accessed=14 * segs * length * width, transcendentals=0
        ),
    )
    return forward, backward


def gelu_both(inputs):
    share = 0.5 * (1.0 + lax.erf(inputs * SQRT_HALF))
    slope = share + inputs * jnp.exp(-0.5 * inputs * inputs) * NORMAL_PEAK
    return inputs * share, slope


def per_device(
    tokens, summary, doc_ids, gain_attn, gain_ffn, w_query, w_key, w_value, w_out, w_up, w_down,
    cotangent,
):
    _, segs, here, model = tokens.shape
    per_seg = summary.shape[2]
    sum_rows = summary.shape[1] * per_seg
    padded = -(-sum_rows // 128) * 128
    length = doc_ids.shape[2]
    shards = length // here
    rows = segs * here
    shard_rows = w_query.shape[0]
    width = model // shards

    place = lax.axis_index(SEQ)

    flat = tokens.reshape(rows, model).astype(F32)
    standard, inverse = normalize(flat)
    hidden = (standard * gain_attn).astype(BF)
    cot = cotangent.reshape(rows, model)
    summary_flat = summary.reshape(sum_rows, model).astype(F32)
    summary_pad = jnp.pad(summary_flat, ((0, padded - sum_rows), (0, 0)))
    standard_sum, inverse_sum = normalize(summary_pad)
    hidden_sum = (standard_sum * gain_attn).astype(BF)

    docs = doc_ids.reshape(segs, length)
    last_docs = jnp.repeat(docs[: segs - 1, length - 1], per_seg)
    sum_docs = jnp.pad(last_docs, (0, padded - sum_rows), constant_values=-1)[None]
    doc_rows = jnp.concatenate([jnp.broadcast_to(sum_docs, (segs, padded)), docs], axis=1)
    far = jnp.where(
        jnp.arange(padded)[None] < jnp.arange(segs)[:, None] * per_seg, -1, length
    ).astype(jnp.int32)
    places = jnp.broadcast_to(jnp.arange(length, dtype=jnp.int32), (segs, length))
    pos_rows = jnp.concatenate([far, places], axis=1)
    doc_args = (ring_order(shards), docs[:, :, None], doc_rows[:, None], pos_rows[:, None])
    attend, attend_back = attention_calls(segs, shards, here, width, padded)
    split = (shards, segs, here, width)
    block_rows = shards * rows // max(ring_size(), 1)

    box = Box()
    out = {}

    half_sums = -(-sum_rows // 2)

    def in_halves(array):
        array = jnp.pad(array[:sum_rows], ((0, 2 * half_sums - sum_rows), (0, 0)))
        return array.reshape(2, half_sums, -1)

    def ready_early():
        yield ()
        place_y = lax.axis_index("y")
        sum_parts = [
            lax.dynamic_index_in_dim(in_halves(array), place_y, 0, False)
            for array in (standard_sum, inverse_sum)
        ]
        ready = yield (doc_args, hidden_sum, sum_parts)
        box["doc_args"], box["hidden_sum"], box["sum_parts"] = ready

    def critical():
        hidden_blocks = yield from gather_ring(hidden)
        w_qkv = yield from box.wait("w_qkv")
        doc_args, hidden_sum = box["doc_args"], box["hidden_sum"]
        def project(weight, scale=1.0):
            blocks = [(dot(block, weight) * scale).astype(BF) for block in hidden_blocks]
            return jnp.concatenate(blocks, axis=0).reshape(split)

        operands = [project(w_qkv[0], 0.125), project(w_qkv[1]), project(w_qkv[2])]
        operands += [dot(hidden_sum, w_qkv[1]).astype(BF), dot(hidden_sum, w_qkv[2]).astype(BF)]
        operands = yield operands
        attended = yield attend(*doc_args, *operands)

        attended = attended.reshape(shards, rows, width)
        attended = yield lax.all_to_all(attended, SEQ, 0, 0, tiled=True)
        attended = near_blocks(attended.swapaxes(0, 1).reshape(rows, model), ROWS)
        w_out_all = yield from box.wait("w_out")
        summed = dot(attended, w_out_all)
        mixed = flat + summed
        standard_ffn, inverse_ffn = normalize(mixed)
        normed = near_blocks((standard_ffn * gain_ffn).astype(BF), FFN_REST, ("c",))

        normed_all = yield from gather_plane(normed, *FFN_NEAR)
        cot_all = yield from box.wait("cot_all")
        w_up_here = yield from box.wait("w_up")
        active, slope = gelu_both(dot(normed_all, w_up_here))
        active = active.astype(BF)
        d_w_down = dot(cot_all, active, 0, 0).astype(BF)
        active, slope, d_w_down = yield (active, slope, d_w_down)
        box["d_w_down"] = d_w_down
        w_down_here = yield from box.wait("w_down")
        grad_upper = (slope * dot(cot_all, w_down_here)).astype(BF)
        grad_normed_part = dot(grad_upper, w_up_here, 1, 1).astype(BF)
        grad_upper, grad_normed_part = yield (grad_upper, grad_normed_part)
        near = scatter_plane(grad_normed_part, *FFN_NEAR)
        in_flight = next(near)
        d_w_up = dot(normed_all, grad_upper, 0, 0).astype(BF)
        in_flight, d_w_up, late_active, blocks = yield (in_flight, d_w_up, active, hidden_blocks)
        box["d_w_up"] = d_w_up
        ffn_out_part = dot(late_active, w_down_here, 1, 1).astype(BF)
        left = jnp.concatenate(blocks + [hidden_sum], axis=0)
        in_flight, ffn_out_part, left = yield (near.send(in_flight), ffn_out_part, left)
        box["ffn_out_part"] = ffn_out_part
        try:
            near.send(in_flight)
        except StopIteration as end:
            grad_normed = near_blocks_back(end.value, FFN_REST, ("c",)).astype(F32)
        grad_mixed = cot.astype(F32) + normalize_back(
            grad_normed, gain_ffn, standard_ffn, inverse_ffn
        )

        grad_branch = grad_mixed.astype(BF)
        grad_attended = near_blocks(dot(grad_branch, w_out_all, 1, 1).astype(BF), ROWS)
        grad_attended = grad_attended.reshape(rows, shards, width).swapaxes(0, 1)
        box["for_out"] = attended, grad_branch
        grad_attended = yield lax.all_to_all(grad_attended, SEQ, 0, 0, tiled=True)
        grads = yield attend_back(*doc_args, *operands, grad_attended.reshape(split))

        box["F"] = True
        d_qkv = [part.reshape(shards * rows, width) for part in grads[:3]]
        d_sums = [part.astype(BF) for part in grads[3:]]

        def grad_block(first):
            parts = [dot(d[first : first + block_rows], w, 1, 1) for d, w in zip(d_qkv, w_qkv)]
            return sum(parts).astype(BF)

        grad_hidden_blocks = [grad_block(i) for i in range(0, shards * rows, block_rows)]
        grad_sum_part = sum(dot(d, w, 1, 1) for d, w in zip(d_sums, w_qkv[1:])).astype(BF)
        d_w_qkv = [dot(left[: shards * rows], d_qkv[0], 0, 0).astype(BF)]
        for d, d_sum in zip(d_qkv[1:], d_sums):
            d_w_qkv.append(dot(left, jnp.concatenate([d, d_sum], axis=0), 0, 0).astype(BF))
        d_w_qkv = jnp.stack(d_w_qkv)
        box["sums"] = grad_sum_part
        scatter = scatter_ring(grad_hidden_blocks)
        try:
            in_flight = next(scatter)
            in_flight, d_w_qkv = yield (in_flight, d_w_qkv)
            box["d_w_qkv"] = d_w_qkv
            while True:
                in_flight = yield scatter.send(in_flight)
        except StopIteration as end:
            grad_hidden = end.value.astype(F32)
        box["d_w_qkv"] = d_w_qkv
        out["d_tokens"] = grad_mixed + normalize_back(grad_hidden, gain_attn, standard, inverse)
        ffn_out = yield from box.wait("ffn_out")
        ffn_out = near_blocks_back(ffn_out, FFN_REST, ("c",))
        out["activations"] = (mixed + ffn_out.astype(F32)).astype(BF)

    def cotangent_rows():
        yield from pause(5)
        cot_all = yield from gather_plane(near_blocks(cot, FFN_REST, ("c",)), *FFN_NEAR)
        box["cot_all"] = yield cot_all

    def weight_up():
        part = yield from exchange_first(w_up)
        yield ()
        part = yield from exchange_last(part)
        box["up"] = part
        far = []
        if lax.axis_size("zh") == 2:
            far = [jnp.concatenate((yield from in_pieces(part, "zh", 1, 2, 1)), axis=0)]
            far.append((yield swap(far[0], "x")))
        part_x = yield from box.wait("up_x")
        box["w_up"] = yield all_rows([part] + far[:1] + [part_x] + far[1:])

    def weight_up_x():
        part = yield from box.wait("up")
        half = part.shape[0] // 2
        low = yield swap(part[:half], "x")
        yield ()
        high = yield swap(part[half:], "x")
        box["up_x"] = jnp.concatenate([low, high], axis=0)

    def weight_down():
        yield ()
        part = yield from exchange_first(w_down)
        yield ()
        part = yield from exchange_last(part)
        box["down"] = part
        yield from pause(2)
        far = far_x = []
        if lax.axis_size("zh") == 2:
            step = part.shape[0] // 4
            low = yield swap(part[: 2 * step], "zh")
            third, low_x = yield (swap(part[2 * step : 3 * step], "zh"), swap(low, "x"))
            fourth = yield swap(part[3 * step :], "zh")
            high = jnp.concatenate([third, fourth], axis=0)
            high_x = yield swap(high, "x")
            far, far_x = [low, high], [low_x, high_x]
        part_x = yield from box.wait("down_x")
        box["w_down"] = all_rows([part, *far, part_x, *far_x])

    def weight_down_x():
        part = yield from box.wait("down")
        yield from pause(2)
        half = part.shape[0] // 2
        low = yield swap(part[:half], "x")
        yield ()
        high = yield swap(part[half:], "x")
        box["down_x"] = jnp.concatenate([low, high], axis=0)

    def weight_out():
        yield from pause(2)
        array = w_out.reshape((1,) * len(AXES) + w_out.shape)
        for axis in ("zh", "zl"):
            array = yield from gather_dim(array, axis, AXES.index(axis))
        half = array.shape[-1] // 2
        by_x, by_y = yield (swap(array, "x"), swap(array, "y"))
        low, high = yield (swap(by_y[..., :half], "x"), swap(by_x[..., half:], "y"))
        both = jnp.concatenate([low, high], axis=-1)
        dim_y = AXES.index("y")
        near = pair(array, by_y, "y", dim_y).reshape(-1, model)
        far = pair(by_x, both, "y", dim_y).reshape(-1, model)
        near_c, far_c = swap(near, "c"), swap(far, "c")
        box["w_out"] = yield jnp.concatenate([near, near_c, far, far_c], axis=0)

    def out_back():
        attended, grad_branch = yield from box.wait("for_out")
        half = model // 2
        far = dot(attended[:, half:], grad_branch, 0, 0).astype(BF)
        far = far[: half // 2] + swap(far[half // 2 :], "c")
        low = yield swap(far[: half // 4], "x")
        near = dot(attended[:, :half], grad_branch, 0, 0).astype(BF)
        near = near[: half // 2] + swap(near[half // 2 :], "c")
        near = yield near
        high = yield swap(far[half // 4 :], "x")
        array = near + jnp.concatenate([low, high], axis=0)
        seq_sizes = tuple(lax.axis_size(axis) for axis in SEQ)
        array = array.reshape((1, 1) + seq_sizes + (shard_rows, model))
        yield from pause(3)
        array = yield from scatter_dim(array, "y", AXES.index("y"))
        array = yield from scatter_line(array[0, 0])
        out["d_w_out"] = array.reshape(shard_rows, model).astype(F32)

    def down_back():
        sums = yield from box.wait("d_w_down")
        if lax.axis_size("zh") != 2:
            array = yield from sums_over_all_zh(sums)
        else:
            far, sent = part_of(sums, 0, 1), part_of(sums, 1, 1)
            near = part_of(sums, 1, 0)
            half = far.shape[0] // 2
            step = half // 2
            low = (yield swap(sent[:half], "x")) + far[:half]
            first, high = yield (swap(low[:step], "zh"), swap(sent[half:], "x"))
            high = high + far[half:]
            second = yield swap(low[step:], "zh")
            third = yield swap(high, "zh")
            near = yield swap(near, "x")
            far = jnp.concatenate([first, second, third], axis=0)
            array = part_of(sums, 0, 0) + near + far
        array = yield from sums_of_ffn(array, 2)
        out["d_w_down"] = array.astype(F32)

    def up_back():
        sums = yield from box.wait("d_w_up")
        if lax.axis_size("zh") != 2:
            array = yield from sums_over_all_zh(sums)
        else:
            far, sent = part_of(sums, 0, 1), part_of(sums, 1, 1)
            near = part_of(sums, 1, 0)
            far = far + jnp.concatenate((yield from in_pieces(sent, "x", 1, 1)), axis=0)
            pieces = yield from in_pieces(far, "zh", 1, 2, 1)
            near = yield swap(near, "x")
            array = part_of(sums, 0, 0) + near + jnp.concatenate(pieces, axis=0)
            yield ()
        array = yield from sums_of_ffn(array)
        out["d_w_up"] = array.astype(F32)

    def activations_back():
        part = yield from box.wait("ffn_out_part")
        part = yield from scatter_plane(part, *FFN_NEAR)
        yield from pause(3)
        box["ffn_out"] = yield part

    def qkv_back():
        array = yield from box.wait("d_w_qkv")
        array = yield from sums_of_qkv(array)
        out["d_w_query"], out["d_w_key"], out["d_w_value"] = array.astype(F32)

    def sums_back():
        grad_sum_part = yield from box.wait("sums")
        yield ()
        array = yield from scatter_dim(in_halves(grad_sum_part), "y", 0)
        for axis in ("zl", "zh"):
            if lax.axis_size(axis) == 2:
                theirs = yield swap(array, axis)
                array = array + theirs
            else:
                array = lax.psum(array, axis)
        grad_sum = array[0].astype(F32)
        standard_part, inverse_part = box["sum_parts"]
        part = normalize_back(grad_sum, gain_attn, standard_part, inverse_part).astype(BF)
        theirs = yield swap(part, "y")
        part = pair(part[None], theirs[None], "y", 0).reshape(2 * half_sums, model)
        out["d_summary"] = part[:sum_rows].astype(F32)

    together(
        ready_early=ready_early(),
        weight_qkv=box.put("w_qkv", columns_of_qkv(jnp.stack([w_query, w_key, w_value]))),
        weight_up=weight_up(),
        weight_up_x=weight_up_x(),
        weight_down=weight_down(),
        weight_down_x=weight_down_x(),
        weight_out=weight_out(),
        cotangent_rows=cotangent_rows(),
        critical=critical(),
        out_back=out_back(),
        down_back=down_back(),
        up_back=up_back(),
        activations_back=activations_back(),
        sums_back=sums_back(),
        qkv_back=qkv_back(),
    )

    def gain_sum(gain, *pairs):
        total = sum(jnp.sum(w.astype(F32) * d, axis=1) for w, d in pairs)
        shard = lax.axis_index(AXES)
        return total / lax.dynamic_slice_in_dim(gain, shard * shard_rows, shard_rows, 0)

    d_gain_attn = gain_sum(
        gain_attn,
        (w_query, out["d_w_query"]),
        (w_key, out["d_w_key"]),
        (w_value, out["d_w_value"]),
    )
    d_gain_ffn = gain_sum(gain_ffn, (w_up, out["d_w_up"]))
    return (
        out["activations"].reshape(tokens.shape),
        out["d_tokens"].reshape(tokens.shape),
        out["d_summary"].reshape(summary.shape),
        d_gain_attn,
        d_gain_ffn,
        out["d_w_query"],
        out["d_w_key"],
        out["d_w_value"],
        out["d_w_out"],
        out["d_w_up"],
        out["d_w_down"],
    )


def solution(mesh):
    rows, seq = mesh.shape["rows"], mesh.shape["seq"]
    fine = Mesh(mesh.devices.reshape(rows // 2, 2, seq // 4, 2, 2), AXES)
    by_token = P(ROWS, None, SEQ, None)
    by_row = P(ROWS, None, None, None)
    weight = P(AXES, None)
    return jax.shard_map(
        per_device,
        mesh=fine,
        in_specs=(by_token, by_row, P(ROWS, None, None), P(), P())
        + (weight,) * 6
        + (by_token,),
        out_specs=(by_token, by_token, by_row, P(AXES), P(AXES)) + (weight,) * 6,
        check_vma=False,
    )
```

```python
import functools
import itertools
import math

import jax
import jax.numpy as jnp
from jax import lax
from jax.experimental import pallas as pl
from jax.experimental.pallas import tpu as pltpu
from jax.sharding import Mesh, PartitionSpec as P

HEAD = 64
EPSILON = 1e-05
MASKED = -1e30
SQRT_HALF = 0.7071067811865476
NORMAL_PEAK = 0.3989422804014327

AXES = ("x", "c", "zh", "zl", "y")
ROWS = ("x", "c")
SEQ = ("zh", "zl", "y")
FFN_GROUP = ("c", "y", "zl")
FFN_DIMS = ("c", "zl", "y")
FFN_NEAR = ("y", "zl", "c")
FFN_REST = ("x", "zh")
PLAN = {
    "cot": 6,
    "up": (0, 1),
    "down": (1, 1),
    "up_zh": ((0, 1), (0, 2), (0, 1)),
    "up_x": ((0, 4),),
    "up_far": ((0, 4),),
    "down_zh": ((1, 1), (0, 1), (0, 1), (0, 1)),
    "down_x": ((2, 2), (1, 2)),
    "down_far": ((0, 2), (0, 2)),
    "out": (2, 0, 0, 0),
    "d_down_far": ((0, 2), (0, 2)),
    "d_down_zh": ((0, 1), (0, 1), (0, 2)),
    "d_down_near": ((1, 4),),
    "d_down_out": (1, 1),
    "d_up_far": ((0, 2), (0, 2)),
    "d_up_zh": ((1, 1), (0, 1), (0, 2)),
    "d_up_near": ((5, 4),),
    "d_up_out": (0, 0),
    "act": (0, 0, 3),
    "d_out": (0, 2, 2, 0),
    "sums": (0, 0, 0, 0),
    "qkv": (0, 0, 0, 0),
}
BF = jnp.bfloat16
F32 = jnp.float32


def dot(left, right, left_dim=1, right_dim=0):
    return lax.dot_general(
        left, right, (((left_dim,), (right_dim,)), ((), ())), preferred_element_type=F32
    )


def normalize(inputs):
    average = jnp.mean(inputs, axis=-1, keepdims=True)
    centred = inputs - average
    inverse = lax.rsqrt(jnp.mean(centred * centred, axis=-1, keepdims=True) + EPSILON)
    return centred * inverse, inverse


def normalize_back(upstream, scaling, standard, inverse):
    scaled = upstream * scaling
    return inverse * (
        scaled
        - jnp.mean(scaled, axis=-1, keepdims=True)
        - standard * jnp.mean(scaled * standard, axis=-1, keepdims=True)
    )


def swap(array, axis):
    return lax.ppermute(array, axis, [(0, 1), (1, 0)])


def pair(mine, theirs, axis, dim):
    first = lax.axis_index(axis) == 0
    return jnp.concatenate(
        [jnp.where(first, mine, theirs), jnp.where(first, theirs, mine)], axis=dim
    )


def halves(array, axis, dim):
    half = array.shape[dim] // 2
    place = lax.axis_index(axis)
    return (
        lax.dynamic_slice_in_dim(array, place * half, half, dim),
        lax.dynamic_slice_in_dim(array, (1 - place) * half, half, dim),
    )


def together(**transfers):
    flying = {}

    def advance(name, sent):
        try:
            with jax.named_scope(name):
                flying[name] = transfers[name].send(sent)
        except StopIteration:
            flying.pop(name, None)

    for name in transfers:
        advance(name, None)
    while flying:
        landed = lax.optimization_barrier(dict(flying))
        for name in transfers:
            if name in landed:
                advance(name, landed[name])


class Box(dict):
    def wait(self, key):
        while key not in self:
            yield ()
        return self[key]

    def put(self, key, transfer):
        self[key] = yield from transfer


def pause(rounds):
    for _ in range(rounds):
        yield ()


class Rows:
    def __init__(self, whole=None):
        self.pieces = [] if whole is None else [(0, 4, whole)]

    def add(self, first, count, array):
        self.pieces.append((first, count, array))

    def take(self, first, count):
        while not set(range(first, first + count)) <= self.held():
            yield ()
        found = []
        for start, held, array in sorted(self.pieces, key=lambda piece: piece[0]):
            low, high = max(start, first), min(start + held, first + count)
            if low < high:
                step = array.shape[0] // held
                found.append(array[(low - start) * step : (high - start) * step])
        return found[0] if len(found) == 1 else jnp.concatenate(found, axis=0)

    def held(self):
        return {start + i for start, count, _ in self.pieces for i in range(count)}


def send_rows(rows, axis, plan, landed, added=None):
    first = 0
    for rounds, count in plan:
        array = yield from rows.take(first, count)
        yield from pause(rounds)
        theirs = yield swap(array, axis)
        if added is not None:
            theirs = theirs + (yield from added.take(first, count))
        landed.add(first, count, theirs)
        first += count


def one_round(array, axis):
    theirs = swap(array, axis)
    if axis != "c":
        theirs = yield theirs
    return theirs


def gather_dim(array, axis, dim):
    if lax.axis_size(axis) != 2:
        return lax.all_gather(array, axis, axis=dim, tiled=True)
    theirs = yield from one_round(array, axis)
    return pair(array, theirs, axis, dim)


def scatter_dim(array, axis, dim):
    if lax.axis_size(axis) != 2:
        return lax.psum_scatter(array, axis, scatter_dimension=dim, tiled=True)
    mine, theirs = halves(array, axis, dim)
    theirs = yield from one_round(theirs, axis)
    return mine + theirs


def exchange(array, axis, cut, joined):
    if lax.axis_size(axis) != 2:
        return lax.all_to_all(array, axis, cut, joined, tiled=True)
    mine, theirs = halves(array, axis, cut)
    theirs = yield from one_round(theirs, axis)
    return pair(mine, theirs, axis, joined)


def gather_plane(array, first, second, last):
    cut = -(-array.shape[0] // 32) * 16
    by_first, by_second = yield (swap(array, first), swap(array, second))
    low, high = yield (swap(by_second[:cut], first), swap(by_first[cut:], second))
    near = jnp.concatenate([array, by_first, by_second, low, high], axis=0)
    return jnp.concatenate([near, swap(near, last)], axis=0)


def scatter_plane(array, first, second, last):
    half = array.shape[0] // 2
    array = array[:half] + swap(array[half:], last)
    rows = array.shape[0] // 4
    cut = -(-rows // 32) * 16
    here, by_first, by_second, both = (array[i * rows : (i + 1) * rows] for i in range(4))
    low, high = yield (swap(both[:cut], first), swap(both[cut:], second))
    by_second = jnp.concatenate([by_second[:cut] + low, by_second[cut:]], axis=0)
    by_first = jnp.concatenate([by_first[:cut], by_first[cut:] + high], axis=0)
    by_first, by_second = yield (swap(by_first, first), swap(by_second, second))
    return here + by_first + by_second


def scatter_line(array):
    if not ring_size():
        array = lax.psum_scatter(array, "zh", scatter_dimension=0, tiled=True)
        return lax.psum_scatter(array, "zl", scatter_dimension=1, tiled=True)[0, 0]
    blocks = array.reshape((4,) + array.shape[2:])
    here = lax.axis_index(("zh", "zl"))
    mine = lax.dynamic_index_in_dim(blocks, here, 0, False)
    theirs = yield tuple(
        lax.ppermute(
            lax.dynamic_index_in_dim(blocks, here ^ step, 0, False),
            ("zh", "zl"),
            [(i, i ^ step) for i in range(4)],
        )
        for step in (1, 2, 3)
    )
    return mine + theirs[0] + theirs[1] + theirs[2]


def ring_size():
    return 4 if lax.axis_size("zh") == 2 else 0


def ring_shift(array, step):
    return lax.ppermute(array, ("zh", "zl"), [(i, (i + step) % 4) for i in range(4)])


def gather_ring(array, others):
    if not ring_size():
        array = lax.all_gather(array, SEQ, axis=0, tiled=True)
        return jnp.concatenate([array, others], axis=0)
    rows = array.shape[0]

    def put(joined, block, place):
        return lax.dynamic_update_slice_in_dim(joined, block, place * rows, 0)

    joined = jnp.zeros((8 * rows + others.shape[0], array.shape[1]), array.dtype)
    joined = put(put(joined, array, 0), others, 8)
    across = [swap(array, "y")]
    along, joined = yield (ring_shift(array, 1), joined)
    for step in (1, 2):
        joined = put(joined, along, 2 * step)
        coming = ring_shift(along, 1)
        across.append(swap(along, "y"))
        if step == 2:
            joined = put(joined, across[0], 1)
        along, across[step - 1], joined = yield (coming, across[step - 1], joined)
    joined = put(put(joined, along, 6), across[1], 3)
    across.append(swap(along, "y"))
    across[2], across[3], joined = yield (across[2], across[3], joined)
    return put(put(joined, across[2], 5), across[3], 7)


def scatter_ring(block):
    if not ring_size():
        return lax.psum_scatter(block(0), SEQ, scatter_dimension=0, tiled=True)
    last, later = block(3), block(2)
    half = last.shape[0] // 2
    across = yield swap(last[half:], "y")
    running = last[:half] + across
    across = swap(later[half:], "y")
    for step in (2, 1, 0):
        here = later[:half]
        coming = ring_shift(running, -1)
        if step:
            later = block(step - 1)
            across_next = swap(later[half:], "y")
        coming, across = yield (coming, across)
        running = here + across + coming
        if step:
            across = across_next
    return running


def ring_order(shards):
    places = jnp.arange(shards, dtype=jnp.int32)
    if not ring_size():
        return places
    along = lax.axis_index(("zh", "zl"))
    return (along - places // 2) % 4 * 2 + (places % 2 ^ lax.axis_index("y"))


def columns_of_qkv(weights):
    array = weights.reshape((1,) * len(AXES) + weights.shape)
    for axis in SEQ:
        array = yield from exchange(array, axis, 6, AXES.index(axis))
    for axis in ROWS:
        array = yield from gather_dim(array, axis, AXES.index(axis))
    return array.reshape(-1, array.shape[-1])


def sums_of_cores(sums):
    sizes = tuple(lax.axis_size(axis) for axis in AXES)
    array = sums.reshape(sizes + (-1, sums.shape[-1]))
    return (yield from scatter_dim(array, "c", AXES.index("c")))


def sums_of_qkv(array):
    array = yield from scatter_dim(array, "x", AXES.index("x"))
    for axis in reversed(SEQ):
        array = yield from exchange(array, axis, AXES.index(axis), 6)
    return array.reshape(array.shape[-2:])


def side_by_side(weights, width):
    rows, cols = weights[0].shape

    def kernel(*refs):
        for part, ref in enumerate(refs[:3]):
            for place in range(cols // width):
                first = (3 * place + part) * width
                refs[3][:, first : first + width] = ref[:, place * width : (place + 1) * width]

    vmem = pl.BlockSpec(memory_space=pltpu.VMEM)
    return pl.pallas_call(
        kernel,
        in_specs=[vmem] * 3,
        out_specs=vmem,
        out_shape=jax.ShapeDtypeStruct((rows, 3 * cols), weights[0].dtype),
        compiler_params=pltpu.CompilerParams(vmem_limit_bytes=8 * 2**20),
    )(*weights)


def apart(array, width):
    rows, cols = array.shape[0], array.shape[1] // 3

    def kernel(ref, *outs):
        for part, out in enumerate(outs):
            for place in range(cols // width):
                first = (3 * place + part) * width
                block = ref[:, first : first + width].astype(F32)
                out[:, place * width : (place + 1) * width] = block

    vmem = pl.BlockSpec(memory_space=pltpu.VMEM)
    return pl.pallas_call(
        kernel,
        in_specs=[vmem],
        out_specs=[vmem] * 3,
        out_shape=[jax.ShapeDtypeStruct((rows, cols), F32)] * 3,
        compiler_params=pltpu.CompilerParams(vmem_limit_bytes=12 * 2**20),
    )(array)


def exchange_first(weight):
    array = weight.reshape((1, 1, 1) + weight.shape)
    for axis in FFN_GROUP[:-1]:
        array = yield from exchange(array, axis, 4, FFN_DIMS.index(axis))
    return array


def exchange_last(array):
    axis = FFN_GROUP[-1]
    array = yield from exchange(array, axis, 4, FFN_DIMS.index(axis))
    return array.reshape(-1, array.shape[-1])


def sums_of_ffn(sums, wait=0):
    sizes = tuple(lax.axis_size(axis) for axis in FFN_DIMS)
    array = sums.reshape(sizes + (-1, sums.shape[-1]))
    for axis in reversed(FFN_GROUP):
        array = yield from exchange(array, axis, FFN_DIMS.index(axis), 4)
        if axis == FFN_GROUP[-1]:
            yield from pause(wait)
    return array.reshape(array.shape[-2:])


def near_blocks(array, axes, kept=()):
    sizes = [lax.axis_size(axis) for axis in AXES]
    lead = list(axes) + list(kept)
    depth = max(AXES.index(axis) for axis in lead) + 1
    lanes = array.shape[1] // math.prod(sizes[:depth])
    firsts = []
    for places in itertools.product(*(range(lax.axis_size(axis)) for axis in lead)):
        at = {axis: place for axis, place in zip(lead, places)}
        for axis in axes:
            at[axis] = relative(at[axis], axis)
        first = 0
        for axis, size in zip(AXES[:depth], sizes):
            first = first * size + at[axis]
        firsts.append(first)
    return reorder(array, firsts, lanes)


def reorder(array, firsts, lanes):
    def kernel(firsts_ref, array_ref, out_ref):
        for place in range(len(firsts)):
            first = pl.multiple_of(firsts_ref[place] * lanes, 128)
            out_ref[:, place * lanes : (place + 1) * lanes] = array_ref[:, pl.ds(first, lanes)]

    return pl.pallas_call(
        kernel,
        in_specs=[pl.BlockSpec(memory_space=pltpu.SMEM), pl.BlockSpec(memory_space=pltpu.VMEM)],
        out_specs=pl.BlockSpec(memory_space=pltpu.VMEM),
        out_shape=jax.ShapeDtypeStruct(array.shape, array.dtype),
        compiler_params=pltpu.CompilerParams(vmem_limit_bytes=8 * 2**20),
    )(jnp.stack([jnp.int32(first) for first in firsts]), array)


def relative(place, axis):
    return place if lax.axis_size(axis) != 2 else lax.axis_index(axis) ^ place


def near_blocks_back(array, axes, kept):
    sizes = [lax.axis_size(axis) for axis in AXES]
    lead = list(axes) + list(kept)
    depth = max(AXES.index(axis) for axis in lead) + 1
    lanes = array.shape[1] // math.prod(sizes[:depth])
    firsts = []
    for places in itertools.product(*(range(size) for size in sizes[:depth])):
        at = dict(zip(AXES, places))
        first = 0
        for axis in lead:
            place = relative(at[axis], axis) if axis in axes else at[axis]
            first = first * lax.axis_size(axis) + place
        firsts.append(first)
    return reorder(array, firsts, lanes)


def all_rows(parts):
    if lax.axis_size("zh") != 2:
        parts = [lax.all_gather(part, "zh", axis=0, tiled=True) for part in parts]
    return jnp.concatenate(parts, axis=0)


def part_of(sums, x, zh):
    rows = sums.shape[0] // 4
    first = (2 * x + zh) * rows
    return sums[first : first + rows]


def sums_over_all_zh(sums):
    half = sums.shape[0] // 2
    theirs = yield swap(sums[half:], "x")
    return lax.psum_scatter(sums[:half] + theirs, "zh", scatter_dimension=0, tiled=True)


def load_ordered(segs, order_ref, tokens_ref, q_ref, k_ref, v_ref):
    length, width = q_ref.shape
    padded = k_ref.shape[0] - length
    here, first_sum = length // order_ref.shape[0], segs * length
    for part, ref in ((1, k_ref), (2, v_ref)):
        ref[:padded, :] = tokens_ref[first_sum:, part * width : (part + 1) * width]
    for place in range(order_ref.shape[0]):
        rows = tokens_ref[rows_of(segs, order_ref, place, here), :]
        q_ref[place * here : (place + 1) * here, :] = rows[:, :width] * BF(0.125)
        for part, ref in ((1, k_ref), (2, v_ref)):
            first = padded + place * here
            ref[first : first + here, :] = rows[:, part * width : (part + 1) * width]


def rows_of(segs, order_ref, place, here):
    first = (order_ref[place] * segs + pl.program_id(0)) * here
    return pl.ds(pl.multiple_of(first, 16), here)


def block_mask(doc_col_ref, doc_row_ref, pos_row_ref, first, rows, keys):
    query_pos = first + lax.broadcasted_iota(jnp.int32, (rows, 1), 0)
    in_reach = pos_row_ref[0, :, :keys] <= query_pos
    return in_reach & (doc_row_ref[0, :, :keys] == doc_col_ref[0, first : first + rows, :])


def heads_of(width):
    lane = lax.broadcasted_iota(jnp.int32, (1, width), 1) // HEAD
    return [lane == head for head in range(width // HEAD)]


def of_heads(parts, heads):
    total = parts[0]
    for part, head in zip(parts[1:], heads[1:]):
        total = jnp.where(head, part, total)
    return total


def block_probs(query, key, allowed):
    scores = jnp.where(allowed, dot(query, key, 1, 1), MASKED)
    weights = jnp.exp(scores - jnp.max(scores, axis=1, keepdims=True))
    return weights * (1.0 / jnp.sum(weights, axis=1, keepdims=True))


def forward_kernel(
    rows, segs, order_ref, doc_col_ref, doc_row_ref, pos_row_ref, tokens_ref, out_ref,
    q_ref, k_ref, v_ref,
):
    shards, _, here, width = out_ref.shape
    padded = k_ref.shape[0] - shards * here
    load_ordered(segs, order_ref, tokens_ref, q_ref, k_ref, v_ref)
    heads = heads_of(width)
    for first in range(0, shards * here, rows):
        keys = padded + first + rows
        allowed = block_mask(doc_col_ref, doc_row_ref, pos_row_ref, first, rows, keys)
        query, key, value = q_ref[first : first + rows, :], k_ref[:keys, :], v_ref[:keys, :]
        outs = []
        for head in heads:
            probs = block_probs(jnp.where(head, query, jnp.zeros_like(query)), key, allowed)
            outs.append(dot(probs.astype(BF), value))
        q_ref[first : first + rows, :] = of_heads(outs, heads).astype(BF)
    for place in range(shards):
        out_ref[place, 0] = q_ref[place * here : (place + 1) * here, :]


def backward_kernel(
    rows, segs, order_ref, doc_col_ref, doc_row_ref, pos_row_ref, tokens_ref, g_in, grads_out,
    q_ref, k_ref, v_ref, g_ref, dk_sum, dv_sum, sums,
):
    shards, _, here, width = g_in.shape
    padded = sums.shape[0]
    load_ordered(segs, order_ref, tokens_ref, q_ref, k_ref, v_ref)
    for place in range(shards):
        g_ref[place * here : (place + 1) * here, :] = g_in[place, 0]

    @pl.when(pl.program_id(0) == 0)
    def _():
        sums[...] = jnp.zeros_like(sums)

    heads = heads_of(width)
    for first in reversed(range(0, shards * here, rows)):
        keys = padded + first + rows
        last = first + rows == shards * here
        allowed = block_mask(doc_col_ref, doc_row_ref, pos_row_ref, first, rows, keys)
        query, grad = q_ref[first : first + rows, :], g_ref[first : first + rows, :]
        key, value = k_ref[:keys, :], v_ref[:keys, :]
        query_t, grad_t = query.T, grad.T
        d_queries = []
        for place, head in enumerate(heads):
            probs = block_probs(jnp.where(head, query, jnp.zeros_like(query)), key, allowed)
            d_probs = dot(jnp.where(head, grad, jnp.zeros_like(grad)), value, 1, 1)
            product = probs * d_probs
            delta = jnp.sum(product, axis=1, keepdims=True)
            d_scores = (product - probs * delta).astype(BF)
            d_queries.append(dot(d_scores, key))
            lanes = slice(place * HEAD, (place + 1) * HEAD)
            d_key = dot(query_t[lanes], d_scores)
            d_value = dot(grad_t[lanes], probs.astype(BF))
            if last:
                dk_sum[lanes, :], dv_sum[lanes, :] = d_key, d_value
            else:
                dk_sum[lanes, :keys] += d_key
                dv_sum[lanes, :keys] += d_value
        d_query = of_heads(d_queries, heads).astype(BF)
        q_ref[first : first + rows, :] = (d_query.astype(F32) * 0.125).astype(BF)
    d_key, d_value = dk_sum[...].T, dv_sum[...].T
    sums[:, width : 2 * width] += d_key[:padded]
    sums[:, 2 * width :] += d_value[:padded]
    k_ref[...], v_ref[...] = d_key.astype(BF), d_value.astype(BF)
    for place in range(shards):
        block = rows_of(segs, order_ref, place, here)
        grads_out[block, :width] = q_ref[place * here : (place + 1) * here, :]
        tokens = slice(padded + place * here, padded + (place + 1) * here)
        grads_out[block, width : 2 * width] = k_ref[tokens, :]
        grads_out[block, 2 * width :] = v_ref[tokens, :]

    @pl.when(pl.program_id(0) == segs - 1)
    def _():
        grads_out[segs * shards * here :, :] = sums[...].astype(BF)


def attention_calls(segs, shards, here, width, padded):
    length = shards * here
    rows = length if length <= 512 else 384
    block = pl.BlockSpec((shards, 1, here, width), lambda s: (0, s, 0, 0))
    joint_shape = (segs * length + padded, 3 * width)
    joint = pl.BlockSpec(joint_shape, lambda s: (0, 0))
    row = pl.BlockSpec((1, 1, padded + length), lambda s: (s, 0, 0))
    docs = [
        pl.BlockSpec(memory_space=pltpu.SMEM),
        pl.BlockSpec((1, length, 1), lambda s: (s, 0, 0)),
        row,
        row,
    ]
    params = pltpu.CompilerParams(
        dimension_semantics=("arbitrary",), vmem_limit_bytes=24 * 2**20
    )
    queries, keys = pltpu.VMEM((length, width), BF), pltpu.VMEM((padded + length, width), BF)
    key_sums = pltpu.VMEM((width, padded + length), F32)
    work = 2 * segs * length * (length // 2 + padded) * width
    forward = pl.pallas_call(
        functools.partial(forward_kernel, rows, segs),
        grid=(segs,),
        in_specs=docs + [joint],
        out_specs=block,
        out_shape=jax.ShapeDtypeStruct((shards, segs, here, width), BF),
        scratch_shapes=[queries, keys, keys],
        compiler_params=params,
        cost_estimate=pl.CostEstimate(
            flops=60 * work, bytes_accessed=8 * segs * length * width, transcendentals=0
        ),
    )
    backward = pl.pallas_call(
        functools.partial(backward_kernel, rows, segs),
        grid=(segs,),
        in_specs=docs + [joint, block],
        out_specs=joint,
        out_shape=jax.ShapeDtypeStruct(joint_shape, BF),
        scratch_shapes=[queries, keys, keys, queries, key_sums, key_sums]
        + [pltpu.VMEM((padded, 3 * width), F32)],
        compiler_params=params,
        cost_estimate=pl.CostEstimate(
            flops=90 * work, bytes_accessed=14 * segs * length * width, transcendentals=0
        ),
    )
    return forward, backward


def gelu_both(inputs):
    share = 0.5 * (1.0 + lax.erf(inputs * SQRT_HALF))
    slope = share + inputs * jnp.exp(-0.5 * inputs * inputs) * NORMAL_PEAK
    return inputs * share, slope


def per_device(
    tokens, summary, doc_ids, gain_attn, gain_ffn, w_query, w_key, w_value, w_out, w_up, w_down,
    cotangent,
):
    _, segs, here, model = tokens.shape
    per_seg = summary.shape[2]
    sum_rows = summary.shape[1] * per_seg
    padded = -(-sum_rows // 128) * 128
    length = doc_ids.shape[2]
    shards = length // here
    rows = segs * here
    shard_rows = w_query.shape[0]
    width = model // shards

    place = lax.axis_index(SEQ)

    flat = tokens.reshape(rows, model).astype(F32)
    standard, inverse = normalize(flat)
    hidden = (standard * gain_attn).astype(BF)
    cot = cotangent.reshape(rows, model)
    summary_flat = summary.reshape(sum_rows, model).astype(F32)
    summary_pad = jnp.pad(summary_flat, ((0, padded - sum_rows), (0, 0)))
    standard_sum, inverse_sum = normalize(summary_pad)
    hidden_sum = (standard_sum * gain_attn).astype(BF)

    docs = doc_ids.reshape(segs, length)
    last_docs = jnp.repeat(docs[: segs - 1, length - 1], per_seg)
    sum_docs = jnp.pad(last_docs, (0, padded - sum_rows), constant_values=-1)[None]
    doc_rows = jnp.concatenate([jnp.broadcast_to(sum_docs, (segs, padded)), docs], axis=1)
    far = jnp.where(
        jnp.arange(padded)[None] < jnp.arange(segs)[:, None] * per_seg, -1, length
    ).astype(jnp.int32)
    places = jnp.broadcast_to(jnp.arange(length, dtype=jnp.int32), (segs, length))
    pos_rows = jnp.concatenate([far, places], axis=1)
    doc_args = (ring_order(shards), docs[:, :, None], doc_rows[:, None], pos_rows[:, None])
    attend, attend_back = attention_calls(segs, shards, here, width, padded)
    split = (shards, segs, here, width)
    block_rows = shards * rows // max(ring_size(), 1)

    box = Box(hidden_sum=hidden_sum)
    out = {}

    half_sums = -(-sum_rows // 2)

    def in_halves(array):
        array = jnp.pad(array[:sum_rows], ((0, 2 * half_sums - sum_rows), (0, 0)))
        return array.reshape(2, half_sums, -1)

    def ready_early():
        yield ()
        place_y = lax.axis_index("y")
        sum_parts = [
            lax.dynamic_index_in_dim(in_halves(array), place_y, 0, False)
            for array in (standard_sum, inverse_sum)
        ]
        box["doc_args"], box["sum_parts"] = yield (doc_args, sum_parts)

    def critical():
        left = yield from gather_ring(hidden, box["hidden_sum"])
        w_qkv = yield from box.wait("w_qkv")
        doc_args = box["doc_args"]
        operands = dot(left, w_qkv).astype(BF)
        operands = yield operands
        attended = yield attend(*doc_args, operands)

        attended = attended.reshape(shards, rows, width)
        attended = yield lax.all_to_all(attended, SEQ, 0, 0, tiled=True)
        attended = near_blocks(attended.swapaxes(0, 1).reshape(rows, model), ROWS)
        w_out_all = yield from box.wait("w_out")
        summed = dot(attended, w_out_all)
        mixed = flat + summed
        standard_ffn, inverse_ffn = normalize(mixed)
        normed = near_blocks((standard_ffn * gain_ffn).astype(BF), FFN_REST, ("c",))

        normed_all = yield from gather_plane(normed, *FFN_NEAR)
        cot_all = yield from box.wait("cot_all")
        w_up_here = yield from box.wait("w_up")
        active, slope = gelu_both(dot(normed_all, w_up_here))
        active = active.astype(BF)
        d_w_down = dot(cot_all, active, 0, 0).astype(BF)
        active, slope, d_w_down = yield (active, slope, d_w_down)
        box["d_w_down"] = d_w_down
        w_down_here = yield from box.wait("w_down")
        grad_upper = (slope * dot(cot_all, w_down_here)).astype(BF)
        grad_normed_part = dot(grad_upper, w_up_here, 1, 1).astype(BF)
        grad_upper, grad_normed_part = yield (grad_upper, grad_normed_part)
        near = scatter_plane(grad_normed_part, *FFN_NEAR)
        in_flight = next(near)
        d_w_up = dot(normed_all, grad_upper, 0, 0).astype(BF)
        in_flight, d_w_up, late_active = yield (in_flight, d_w_up, active)
        box["d_w_up"] = d_w_up
        ffn_out_part = dot(late_active, w_down_here, 1, 1).astype(BF)
        in_flight, ffn_out_part = yield (near.send(in_flight), ffn_out_part)
        try:
            near.send(in_flight)
        except StopIteration as end:
            grad_normed = near_blocks_back(end.value, FFN_REST, ("c",)).astype(F32)
        grad_mixed = cot.astype(F32) + normalize_back(
            grad_normed, gain_ffn, standard_ffn, inverse_ffn
        )

        grad_branch = grad_mixed.astype(BF)
        grad_attended = near_blocks(dot(grad_branch, w_out_all, 1, 1).astype(BF), ROWS)
        grad_attended = grad_attended.reshape(rows, shards, width).swapaxes(0, 1)
        held = (attended, grad_branch, ffn_out_part, d_w_down, d_w_up)
        grad_attended, held = lax.optimization_barrier((grad_attended, held))
        attended, grad_branch, box["ffn_out_part"], box["d_w_down_late"], box["d_w_up_late"] = held
        box["for_out"] = attended, grad_branch
        grad_attended = yield lax.all_to_all(grad_attended, SEQ, 0, 0, tiled=True)
        grads = yield attend_back(*doc_args, operands, grad_attended.reshape(split))

        box["F"] = True
        def grad_block(k):
            rows_of_k = (late or [grads])[0][k * block_rows : (k + 1) * block_rows]
            return dot(rows_of_k, w_qkv, 1, 1).astype(BF)

        late = []
        d_w_qkv = yield from sums_of_cores(dot(left, grads, 0, 0).astype(BF))
        scatter = scatter_ring(grad_block)
        try:
            in_flight = next(scatter)
            in_flight, d_w_qkv, grads = yield (in_flight, d_w_qkv, grads)
            late.append(grads)
            box["d_w_qkv"] = d_w_qkv
            box["sums"] = dot(grads[shards * rows :], w_qkv, 1, 1).astype(BF)
            while True:
                in_flight = yield scatter.send(in_flight)
        except StopIteration as end:
            grad_hidden = end.value.astype(F32)
        if not late:
            box["d_w_qkv"] = d_w_qkv
            box["sums"] = dot(grads[shards * rows :], w_qkv, 1, 1).astype(BF)
        out["d_tokens"] = grad_mixed + normalize_back(grad_hidden, gain_attn, standard, inverse)
        ffn_out = yield from box.wait("ffn_out")
        ffn_out = near_blocks_back(ffn_out, FFN_REST, ("c",))
        out["activations"] = (mixed + ffn_out.astype(F32)).astype(BF)

    def cotangent_rows():
        yield from pause(PLAN["cot"])
        cot_all = yield from gather_plane(near_blocks(cot, FFN_REST, ("c",)), *FFN_NEAR)
        box["cot_all"] = yield cot_all

    def weight(name, shard):
        part, far, part_x, far_x = Rows(), Rows(), Rows(), Rows()

        def columns():
            yield from pause(PLAN[name][0])
            array = yield from exchange_first(shard)
            yield from pause(PLAN[name][1])
            array = yield from exchange_last(array)
            part.add(0, 4, array)

        def all_columns():
            parts = [(yield from part.take(0, 4))]
            if lax.axis_size("zh") == 2:
                parts.append((yield from far.take(0, 4)))
            parts.append((yield from part_x.take(0, 4)))
            if lax.axis_size("zh") == 2:
                parts.append((yield from far_x.take(0, 4)))
            box["w_" + name] = all_rows(parts)

        threads = {name: columns(), name + "_x": send_rows(part, "x", PLAN[name + "_x"], part_x)}
        if lax.axis_size("zh") == 2:
            threads[name + "_zh"] = send_rows(part, "zh", PLAN[name + "_zh"], far)
            threads[name + "_far"] = send_rows(far, "x", PLAN[name + "_far"], far_x)
        threads[name + "_all"] = all_columns()
        return threads

    def weight_sums(name):
        sent, own, near, far, landed, sent_near = (Rows() for _ in range(6))

        def start():
            sums = yield from box.wait("d_w_" + name)
            sent.add(0, 4, part_of(sums, 1, 1))
            own.add(0, 4, part_of(sums, 0, 1))
            sums = yield from box.wait("d_w_" + name + "_late")
            sent_near.add(0, 4, part_of(sums, 1, 0))

        def all_sums():
            sums = yield from box.wait("d_w_" + name + "_late")
            if lax.axis_size("zh") != 2:
                array = yield from sums_over_all_zh(sums)
            else:
                array = part_of(sums, 0, 0) + (yield from near.take(0, 4))
                array = array + (yield from landed.take(0, 4))
            waits = PLAN["d_" + name + "_out"]
            yield from pause(waits[0])
            array = yield from sums_of_ffn(array, waits[1])
            out["d_w_" + name] = array.astype(F32)

        threads = {"d_" + name: start()}
        if lax.axis_size("zh") == 2:
            plans = {step: PLAN["d_" + name + "_" + step] for step in ("far", "zh", "near")}
            threads["d_" + name + "_far"] = send_rows(sent, "x", plans["far"], far, own)
            threads["d_" + name + "_zh"] = send_rows(far, "zh", plans["zh"], landed)
            threads["d_" + name + "_near"] = send_rows(sent_near, "x", plans["near"], near)
        threads["d_" + name + "_all"] = all_sums()
        return threads

    def weight_out():
        waits = PLAN["out"]
        array = w_out.reshape((1,) * len(AXES) + w_out.shape)
        for rounds, axis in zip(waits, ("zh", "zl")):
            yield from pause(rounds)
            array = yield from gather_dim(array, axis, AXES.index(axis))
        yield from pause(waits[2])
        half = array.shape[-1] // 2
        by_x, by_y = yield (swap(array, "x"), swap(array, "y"))
        yield from pause(waits[3])
        low, high = yield (swap(by_y[..., :half], "x"), swap(by_x[..., half:], "y"))
        both = jnp.concatenate([low, high], axis=-1)
        dim_y = AXES.index("y")
        near = pair(array, by_y, "y", dim_y).reshape(-1, model)
        far = pair(by_x, both, "y", dim_y).reshape(-1, model)
        near_c, far_c = swap(near, "c"), swap(far, "c")
        box["w_out"] = yield jnp.concatenate([near, near_c, far, far_c], axis=0)

    def out_back():
        attended, grad_branch = yield from box.wait("for_out")
        half = model // 2
        far = dot(attended[:, half:], grad_branch, 0, 0).astype(BF)
        far = far[: half // 2] + swap(far[half // 2 :], "c")
        waits = PLAN["d_out"]
        yield from pause(waits[0])
        low = yield swap(far[: half // 4], "x")
        near = dot(attended[:, :half], grad_branch, 0, 0).astype(BF)
        near = near[: half // 2] + swap(near[half // 2 :], "c")
        near = yield near
        yield from pause(waits[1] - 1)
        high = yield swap(far[half // 4 :], "x")
        array = near + jnp.concatenate([low, high], axis=0)
        seq_sizes = tuple(lax.axis_size(axis) for axis in SEQ)
        array = array.reshape((1, 1) + seq_sizes + (shard_rows, model))
        yield from pause(waits[2])
        array = yield from scatter_dim(array, "y", AXES.index("y"))
        yield from pause(waits[3])
        array = yield from scatter_line(array[0, 0])
        out["d_w_out"] = array.reshape(shard_rows, model).astype(F32)

    def activations_back():
        part = yield from box.wait("ffn_out_part")
        waits = PLAN["act"]
        yield from pause(waits[0])
        part = yield from scatter_plane(part, *FFN_NEAR)
        yield from pause(waits[2])
        box["ffn_out"] = yield part

    def qkv_back():
        array = yield from box.wait("d_w_qkv")
        array = yield from sums_of_qkv(array)
        out["d_w_query"], out["d_w_key"], out["d_w_value"] = apart(array, width)

    def sums_back():
        grad_sum_part = yield from box.wait("sums")
        waits = PLAN["sums"]
        yield from pause(waits[0])
        array = yield from scatter_dim(in_halves(grad_sum_part), "y", 0)
        for rounds, axis in zip(waits[1:], ("zl", "zh")):
            yield from pause(rounds)
            if lax.axis_size(axis) == 2:
                theirs = yield swap(array, axis)
                array = array + theirs
            else:
                array = lax.psum(array, axis)
        grad_sum = array[0].astype(F32)
        standard_part, inverse_part = box["sum_parts"]
        part = normalize_back(grad_sum, gain_attn, standard_part, inverse_part).astype(BF)
        yield from pause(waits[3])
        theirs = yield swap(part, "y")
        part = pair(part[None], theirs[None], "y", 0).reshape(2 * half_sums, model)
        out["d_summary"] = part[:sum_rows].astype(F32)

    together(
        ready_early=ready_early(),
        weight_qkv=box.put("w_qkv", columns_of_qkv(side_by_side((w_query, w_key, w_value), width))),
        **weight("up", w_up),
        **weight("down", w_down),
        weight_out=weight_out(),
        cotangent_rows=cotangent_rows(),
        critical=critical(),
        out_back=out_back(),
        **weight_sums("down"),
        **weight_sums("up"),
        activations_back=activations_back(),
        sums_back=sums_back(),
        qkv_back=qkv_back(),
    )

    def gain_sum(gain, *pairs):
        total = sum(jnp.sum(w.astype(F32) * d, axis=1) for w, d in pairs)
        shard = lax.axis_index(AXES)
        return total / lax.dynamic_slice_in_dim(gain, shard * shard_rows, shard_rows, 0)

    d_gain_attn = gain_sum(
        gain_attn,
        (w_query, out["d_w_query"]),
        (w_key, out["d_w_key"]),
        (w_value, out["d_w_value"]),
    )
    d_gain_ffn = gain_sum(gain_ffn, (w_up, out["d_w_up"]))
    return (
        out["activations"].reshape(tokens.shape),
        out["d_tokens"].reshape(tokens.shape),
        out["d_summary"].reshape(summary.shape),
        d_gain_attn,
        d_gain_ffn,
        out["d_w_query"],
        out["d_w_key"],
        out["d_w_value"],
        out["d_w_out"],
        out["d_w_up"],
        out["d_w_down"],
    )


def solution(mesh):
    rows, seq = mesh.shape["rows"], mesh.shape["seq"]
    fine = Mesh(mesh.devices.reshape(rows // 2, 2, seq // 4, 2, 2), AXES)
    by_token = P(ROWS, None, SEQ, None)
    by_row = P(ROWS, None, None, None)
    weight = P(AXES, None)
    return jax.shard_map(
        per_device,
        mesh=fine,
        in_specs=(by_token, by_row, P(ROWS, None, None), P(), P())
        + (weight,) * 6
        + (by_token,),
        out_specs=(by_token, by_token, by_row, P(AXES), P(AXES)) + (weight,) * 6,
        check_vma=False,
    )
```

```python
import functools
import itertools
import math

import jax
import jax.numpy as jnp
from jax import lax
from jax.experimental import pallas as pl
from jax.experimental.pallas import tpu as pltpu
from jax.sharding import Mesh, PartitionSpec as P

HEAD = 64
EPSILON = 1e-05
MASKED = -1e30
SQRT_HALF = 0.7071067811865476
NORMAL_PEAK = 0.3989422804014327

AXES = ("x", "c", "zh", "zl", "y")
ROWS = ("x", "c")
SEQ = ("zh", "zl", "y")
FFN_GROUP = ("c", "y", "zl")
FFN_DIMS = ("c", "zl", "y")
FFN_NEAR = ("y", "zl", "c")
FFN_REST = ("x", "zh")
PLAN = {
    "cot": 6,
    "up": (0, 1),
    "down": (1, 1),
    "up_zh": ((0, 1), (0, 2), (0, 1)),
    "up_x": ((0, 4),),
    "up_far": ((1, 4),),
    "down_zh": ((1, 1), (0, 1), (0, 1), (0, 1)),
    "down_x": ((2, 2), (1, 2)),
    "down_far": ((0, 2), (0, 2)),
    "out": (2, 0, 0, 0),
    "d_down_far": ((0, 2), (0, 2)),
    "d_down_zh": ((0, 1), (0, 1), (0, 2)),
    "d_down_near": ((1, 4),),
    "d_down_out": (1, 1),
    "d_up_far": ((0, 2), (0, 2)),
    "d_up_zh": ((0, 1), (0, 1), (0, 2)),
    "d_up_near": ((5, 4),),
    "d_up_out": (0, 0),
    "act": (0, 0, 2),
    "d_out": (0, 2, 2, 0),
    "sums": (0, 0, 0, 0),
    "qkv": (0, 0, 0, 0),
}
BF = jnp.bfloat16
F32 = jnp.float32


def dot(left, right, left_dim=1, right_dim=0):
    return lax.dot_general(
        left, right, (((left_dim,), (right_dim,)), ((), ())), preferred_element_type=F32
    )


def normalize(inputs):
    average = jnp.mean(inputs, axis=-1, keepdims=True)
    centred = inputs - average
    inverse = lax.rsqrt(jnp.mean(centred * centred, axis=-1, keepdims=True) + EPSILON)
    return centred * inverse, inverse


def normalize_back(upstream, scaling, standard, inverse):
    scaled = upstream * scaling
    return inverse * (
        scaled
        - jnp.mean(scaled, axis=-1, keepdims=True)
        - standard * jnp.mean(scaled * standard, axis=-1, keepdims=True)
    )


def swap(array, axis):
    return lax.ppermute(array, axis, [(0, 1), (1, 0)])


def pair(mine, theirs, axis, dim):
    first = lax.axis_index(axis) == 0
    return jnp.concatenate(
        [jnp.where(first, mine, theirs), jnp.where(first, theirs, mine)], axis=dim
    )


def halves(array, axis, dim):
    half = array.shape[dim] // 2
    place = lax.axis_index(axis)
    return (
        lax.dynamic_slice_in_dim(array, place * half, half, dim),
        lax.dynamic_slice_in_dim(array, (1 - place) * half, half, dim),
    )


def together(**transfers):
    flying = {}

    def advance(name, sent):
        try:
            with jax.named_scope(name):
                flying[name] = transfers[name].send(sent)
        except StopIteration:
            flying.pop(name, None)

    for name in transfers:
        advance(name, None)
    while flying:
        landed = lax.optimization_barrier(dict(flying))
        for name in transfers:
            if name in landed:
                advance(name, landed[name])


class Box(dict):
    def wait(self, key):
        while key not in self:
            yield ()
        return self[key]

    def put(self, key, transfer):
        self[key] = yield from transfer


def pause(rounds):
    for _ in range(rounds):
        yield ()


class Rows:
    def __init__(self, whole=None):
        self.pieces = [] if whole is None else [(0, 4, whole)]

    def add(self, first, count, array):
        self.pieces.append((first, count, array))

    def take(self, first, count):
        while not set(range(first, first + count)) <= self.held():
            yield ()
        found = []
        for start, held, array in sorted(self.pieces, key=lambda piece: piece[0]):
            low, high = max(start, first), min(start + held, first + count)
            if low < high:
                step = array.shape[0] // held
                found.append(array[(low - start) * step : (high - start) * step])
        return found[0] if len(found) == 1 else jnp.concatenate(found, axis=0)

    def held(self):
        return {start + i for start, count, _ in self.pieces for i in range(count)}


def send_rows(rows, axis, plan, landed, added=None):
    first = 0
    for rounds, count in plan:
        array = yield from rows.take(first, count)
        yield from pause(rounds)
        theirs = yield swap(array, axis)
        if added is not None:
            theirs = theirs + (yield from added.take(first, count))
        landed.add(first, count, theirs)
        first += count


def one_round(array, axis):
    theirs = swap(array, axis)
    if axis != "c":
        theirs = yield theirs
    return theirs


def gather_dim(array, axis, dim):
    if lax.axis_size(axis) != 2:
        return lax.all_gather(array, axis, axis=dim, tiled=True)
    theirs = yield from one_round(array, axis)
    return pair(array, theirs, axis, dim)


def scatter_dim(array, axis, dim):
    if lax.axis_size(axis) != 2:
        return lax.psum_scatter(array, axis, scatter_dimension=dim, tiled=True)
    mine, theirs = halves(array, axis, dim)
    theirs = yield from one_round(theirs, axis)
    return mine + theirs


def exchange(array, axis, cut, joined):
    if lax.axis_size(axis) != 2:
        return lax.all_to_all(array, axis, cut, joined, tiled=True)
    mine, theirs = halves(array, axis, cut)
    theirs = yield from one_round(theirs, axis)
    return pair(mine, theirs, axis, joined)


def gather_plane(array, first, second, last):
    cut = -(-array.shape[0] // 32) * 16
    by_first, by_second = yield (swap(array, first), swap(array, second))
    low, high = yield (swap(by_second[:cut], first), swap(by_first[cut:], second))
    near = jnp.concatenate([array, by_first, by_second, low, high], axis=0)
    return jnp.concatenate([near, swap(near, last)], axis=0)


def scatter_plane(array, first, second, last):
    half = array.shape[0] // 2
    array = array[:half] + swap(array[half:], last)
    rows = array.shape[0] // 4
    cut = -(-rows // 32) * 16
    here, by_first, by_second, both = (array[i * rows : (i + 1) * rows] for i in range(4))
    low, high = yield (swap(both[:cut], first), swap(both[cut:], second))
    by_second = jnp.concatenate([by_second[:cut] + low, by_second[cut:]], axis=0)
    by_first = jnp.concatenate([by_first[:cut], by_first[cut:] + high], axis=0)
    by_first, by_second = yield (swap(by_first, first), swap(by_second, second))
    return here + by_first + by_second


def scatter_line(array):
    if not ring_size():
        array = lax.psum_scatter(array, "zh", scatter_dimension=0, tiled=True)
        return lax.psum_scatter(array, "zl", scatter_dimension=1, tiled=True)[0, 0]
    blocks = array.reshape((4,) + array.shape[2:])
    here = lax.axis_index(("zh", "zl"))
    mine = lax.dynamic_index_in_dim(blocks, here, 0, False)
    theirs = yield tuple(
        lax.ppermute(
            lax.dynamic_index_in_dim(blocks, here ^ step, 0, False),
            ("zh", "zl"),
            [(i, i ^ step) for i in range(4)],
        )
        for step in (1, 2, 3)
    )
    return mine + theirs[0] + theirs[1] + theirs[2]


def ring_size():
    return 4 if lax.axis_size("zh") == 2 else 0


def ring_shift(array, step):
    return lax.ppermute(array, ("zh", "zl"), [(i, (i + step) % 4) for i in range(4)])


def gather_ring(array, others):
    if not ring_size():
        array = lax.all_gather(array, SEQ, axis=0, tiled=True)
        return jnp.concatenate([array, others], axis=0)
    rows = array.shape[0]

    def put(joined, block, place):
        return lax.dynamic_update_slice_in_dim(joined, block, place * rows, 0)

    joined = jnp.zeros((8 * rows + others.shape[0], array.shape[1]), array.dtype)
    joined = put(put(joined, array, 0), others, 8)
    across = [swap(array, "y")]
    along, joined = yield (ring_shift(array, 1), joined)
    for step in (1, 2):
        joined = put(joined, along, 2 * step)
        coming = ring_shift(along, 1)
        across.append(swap(along, "y"))
        if step == 2:
            joined = put(joined, across[0], 1)
        along, across[step - 1], joined = yield (coming, across[step - 1], joined)
    joined = put(put(joined, along, 6), across[1], 3)
    across.append(swap(along, "y"))
    across[2], across[3], joined = yield (across[2], across[3], joined)
    return put(put(joined, across[2], 5), across[3], 7)


def scatter_ring(block):
    if not ring_size():
        return lax.psum_scatter(block(0), SEQ, scatter_dimension=0, tiled=True)
    last, later = block(3), block(2)
    half = last.shape[0] // 2
    across = yield swap(last[half:], "y")
    running = last[:half] + across
    across = swap(later[half:], "y")
    for step in (2, 1, 0):
        here = later[:half]
        coming = ring_shift(running, -1)
        if step:
            later = block(step - 1)
            across_next = swap(later[half:], "y")
        coming, across = yield (coming, across)
        running = here + across + coming
        if step:
            across = across_next
    return running


def ring_order(shards):
    places = jnp.arange(shards, dtype=jnp.int32)
    if not ring_size():
        return places
    along = lax.axis_index(("zh", "zl"))
    return (along - places // 2) % 4 * 2 + (places % 2 ^ lax.axis_index("y"))


def columns_of_qkv(weights):
    array = weights.reshape((1,) * len(AXES) + weights.shape)
    for axis in SEQ:
        array = yield from exchange(array, axis, 6, AXES.index(axis))
    for axis in ROWS:
        array = yield from gather_dim(array, axis, AXES.index(axis))
    return array.reshape(-1, array.shape[-1])


def sums_of_cores(sums):
    sizes = tuple(lax.axis_size(axis) for axis in AXES)
    array = sums.reshape(sizes + (-1, sums.shape[-1]))
    return (yield from scatter_dim(array, "c", AXES.index("c")))


def sums_of_qkv(array):
    array = yield from scatter_dim(array, "x", AXES.index("x"))
    for axis in reversed(SEQ):
        array = yield from exchange(array, axis, AXES.index(axis), 6)
    return array.reshape(array.shape[-2:])


def side_by_side(weights, width):
    rows, cols = weights[0].shape

    def kernel(*refs):
        for part, ref in enumerate(refs[:3]):
            for place in range(cols // width):
                first = (3 * place + part) * width
                refs[3][:, first : first + width] = ref[:, place * width : (place + 1) * width]

    vmem = pl.BlockSpec(memory_space=pltpu.VMEM)
    return pl.pallas_call(
        kernel,
        in_specs=[vmem] * 3,
        out_specs=vmem,
        out_shape=jax.ShapeDtypeStruct((rows, 3 * cols), weights[0].dtype),
        compiler_params=pltpu.CompilerParams(vmem_limit_bytes=8 * 2**20),
    )(*weights)


def apart(array, width):
    rows, cols = array.shape[0], array.shape[1] // 3

    def kernel(ref, *outs):
        for part, out in enumerate(outs):
            for place in range(cols // width):
                first = (3 * place + part) * width
                block = ref[:, first : first + width].astype(F32)
                out[:, place * width : (place + 1) * width] = block

    vmem = pl.BlockSpec(memory_space=pltpu.VMEM)
    return pl.pallas_call(
        kernel,
        in_specs=[vmem],
        out_specs=[vmem] * 3,
        out_shape=[jax.ShapeDtypeStruct((rows, cols), F32)] * 3,
        compiler_params=pltpu.CompilerParams(vmem_limit_bytes=12 * 2**20),
    )(array)


def exchange_first(weight):
    array = weight.reshape((1, 1, 1) + weight.shape)
    for axis in FFN_GROUP[:-1]:
        array = yield from exchange(array, axis, 4, FFN_DIMS.index(axis))
    return array


def exchange_last(array):
    axis = FFN_GROUP[-1]
    array = yield from exchange(array, axis, 4, FFN_DIMS.index(axis))
    return array.reshape(-1, array.shape[-1])


def sums_of_ffn(sums, wait=0):
    sizes = tuple(lax.axis_size(axis) for axis in FFN_DIMS)
    array = sums.reshape(sizes + (-1, sums.shape[-1]))
    for axis in reversed(FFN_GROUP):
        array = yield from exchange(array, axis, FFN_DIMS.index(axis), 4)
        if axis == FFN_GROUP[-1]:
            yield from pause(wait)
    return array.reshape(array.shape[-2:])


def near_blocks(array, axes, kept=()):
    sizes = [lax.axis_size(axis) for axis in AXES]
    lead = list(axes) + list(kept)
    depth = max(AXES.index(axis) for axis in lead) + 1
    lanes = array.shape[1] // math.prod(sizes[:depth])
    firsts = []
    for places in itertools.product(*(range(lax.axis_size(axis)) for axis in lead)):
        at = {axis: place for axis, place in zip(lead, places)}
        for axis in axes:
            at[axis] = relative(at[axis], axis)
        first = 0
        for axis, size in zip(AXES[:depth], sizes):
            first = first * size + at[axis]
        firsts.append(first)
    return reorder(array, firsts, lanes)


def reorder(array, firsts, lanes):
    if lanes % 128:
        parts = [lax.dynamic_slice_in_dim(array, first * lanes, lanes, 1) for first in firsts]
        return jnp.concatenate(parts, axis=1)

    def kernel(firsts_ref, array_ref, out_ref):
        for place in range(len(firsts)):
            first = pl.multiple_of(firsts_ref[place] * lanes, 128)
            out_ref[:, place * lanes : (place + 1) * lanes] = array_ref[:, pl.ds(first, lanes)]

    return pl.pallas_call(
        kernel,
        in_specs=[pl.BlockSpec(memory_space=pltpu.SMEM), pl.BlockSpec(memory_space=pltpu.VMEM)],
        out_specs=pl.BlockSpec(memory_space=pltpu.VMEM),
        out_shape=jax.ShapeDtypeStruct(array.shape, array.dtype),
        compiler_params=pltpu.CompilerParams(vmem_limit_bytes=8 * 2**20),
    )(jnp.stack([jnp.int32(first) for first in firsts]), array)


def relative(place, axis):
    return place if lax.axis_size(axis) != 2 else lax.axis_index(axis) ^ place


def near_blocks_back(array, axes, kept):
    sizes = [lax.axis_size(axis) for axis in AXES]
    lead = list(axes) + list(kept)
    depth = max(AXES.index(axis) for axis in lead) + 1
    lanes = array.shape[1] // math.prod(sizes[:depth])
    firsts = []
    for places in itertools.product(*(range(size) for size in sizes[:depth])):
        at = dict(zip(AXES, places))
        first = 0
        for axis in lead:
            place = relative(at[axis], axis) if axis in axes else at[axis]
            first = first * lax.axis_size(axis) + place
        firsts.append(first)
    return reorder(array, firsts, lanes)


def all_rows(parts):
    if lax.axis_size("zh") != 2:
        parts = [lax.all_gather(part, "zh", axis=0, tiled=True) for part in parts]
    return jnp.concatenate(parts, axis=0)


def part_of(sums, x, zh):
    rows = sums.shape[0] // 4
    first = (2 * x + zh) * rows
    return sums[first : first + rows]


def sums_over_all_zh(sums):
    half = sums.shape[0] // 2
    theirs = yield swap(sums[half:], "x")
    return lax.psum_scatter(sums[:half] + theirs, "zh", scatter_dimension=0, tiled=True)


def load_ordered(segs, order_ref, tokens_ref, q_ref, k_ref, v_ref):
    length, width = q_ref.shape
    padded = k_ref.shape[0] - length
    here, first_sum = length // order_ref.shape[0], segs * length
    for part, ref in ((1, k_ref), (2, v_ref)):
        ref[:padded, :] = tokens_ref[first_sum:, part * width : (part + 1) * width]
    for place in range(order_ref.shape[0]):
        rows = tokens_ref[rows_of(segs, order_ref, place, here), :]
        q_ref[place * here : (place + 1) * here, :] = rows[:, :width] * BF(0.125)
        for part, ref in ((1, k_ref), (2, v_ref)):
            first = padded + place * here
            ref[first : first + here, :] = rows[:, part * width : (part + 1) * width]


def rows_of(segs, order_ref, place, here):
    first = (order_ref[place] * segs + pl.program_id(0)) * here
    return pl.ds(pl.multiple_of(first, 16), here)


def block_mask(doc_col_ref, doc_row_ref, pos_row_ref, first, rows, keys):
    query_pos = first + lax.broadcasted_iota(jnp.int32, (rows, 1), 0)
    in_reach = pos_row_ref[0, :, :keys] <= query_pos
    return in_reach & (doc_row_ref[0, :, :keys] == doc_col_ref[0, first : first + rows, :])


def heads_of(width):
    lane = lax.broadcasted_iota(jnp.int32, (1, width), 1) // HEAD
    return [lane == head for head in range(width // HEAD)]


def of_heads(parts, heads):
    total = parts[0]
    for part, head in zip(parts[1:], heads[1:]):
        total = jnp.where(head, part, total)
    return total


def block_probs(query, key, allowed):
    scores = jnp.where(allowed, dot(query, key, 1, 1), MASKED)
    weights = jnp.exp(scores - jnp.max(scores, axis=1, keepdims=True))
    return weights * (1.0 / jnp.sum(weights, axis=1, keepdims=True))


def forward_kernel(
    rows, segs, order_ref, doc_col_ref, doc_row_ref, pos_row_ref, tokens_ref, out_ref,
    q_ref, k_ref, v_ref,
):
    shards, _, here, width = out_ref.shape
    padded = k_ref.shape[0] - shards * here
    load_ordered(segs, order_ref, tokens_ref, q_ref, k_ref, v_ref)
    heads = heads_of(width)
    for first in range(0, shards * here, rows):
        keys = padded + first + rows
        allowed = block_mask(doc_col_ref, doc_row_ref, pos_row_ref, first, rows, keys)
        query, key, value = q_ref[first : first + rows, :], k_ref[:keys, :], v_ref[:keys, :]
        outs = []
        for head in heads:
            probs = block_probs(jnp.where(head, query, jnp.zeros_like(query)), key, allowed)
            outs.append(dot(probs.astype(BF), value))
        q_ref[first : first + rows, :] = of_heads(outs, heads).astype(BF)
    for place in range(shards):
        out_ref[place, 0] = q_ref[place * here : (place + 1) * here, :]


def backward_kernel(
    rows, segs, order_ref, doc_col_ref, doc_row_ref, pos_row_ref, tokens_ref, g_in, grads_out,
    q_ref, k_ref, v_ref, g_ref, dk_sum, dv_sum, sums,
):
    shards, _, here, width = g_in.shape
    padded = sums.shape[0]
    load_ordered(segs, order_ref, tokens_ref, q_ref, k_ref, v_ref)
    for place in range(shards):
        g_ref[place * here : (place + 1) * here, :] = g_in[place, 0]

    @pl.when(pl.program_id(0) == 0)
    def _():
        sums[...] = jnp.zeros_like(sums)

    heads = heads_of(width)
    for first in reversed(range(0, shards * here, rows)):
        keys = padded + first + rows
        last = first + rows == shards * here
        allowed = block_mask(doc_col_ref, doc_row_ref, pos_row_ref, first, rows, keys)
        query, grad = q_ref[first : first + rows, :], g_ref[first : first + rows, :]
        key, value = k_ref[:keys, :], v_ref[:keys, :]
        query_t, grad_t = query.T, grad.T
        d_queries = []
        for place, head in enumerate(heads):
            probs = block_probs(jnp.where(head, query, jnp.zeros_like(query)), key, allowed)
            d_probs = dot(jnp.where(head, grad, jnp.zeros_like(grad)), value, 1, 1)
            product = probs * d_probs
            delta = jnp.sum(product, axis=1, keepdims=True)
            d_scores = (product - probs * delta).astype(BF)
            d_queries.append(dot(d_scores, key))
            lanes = slice(place * HEAD, (place + 1) * HEAD)
            d_key = dot(query_t[lanes], d_scores)
            d_value = dot(grad_t[lanes], probs.astype(BF))
            if last:
                dk_sum[lanes, :], dv_sum[lanes, :] = d_key, d_value
            else:
                dk_sum[lanes, :keys] += d_key
                dv_sum[lanes, :keys] += d_value
        d_query = of_heads(d_queries, heads).astype(BF)
        q_ref[first : first + rows, :] = (d_query.astype(F32) * 0.125).astype(BF)
    d_key, d_value = dk_sum[...].T, dv_sum[...].T
    sums[:, width : 2 * width] += d_key[:padded]
    sums[:, 2 * width :] += d_value[:padded]
    k_ref[...], v_ref[...] = d_key.astype(BF), d_value.astype(BF)
    for place in range(shards):
        block = rows_of(segs, order_ref, place, here)
        grads_out[block, :width] = q_ref[place * here : (place + 1) * here, :]
        tokens = slice(padded + place * here, padded + (place + 1) * here)
        grads_out[block, width : 2 * width] = k_ref[tokens, :]
        grads_out[block, 2 * width :] = v_ref[tokens, :]

    @pl.when(pl.program_id(0) == segs - 1)
    def _():
        grads_out[segs * shards * here :, :] = sums[...].astype(BF)


def attention_calls(segs, shards, here, width, padded):
    length = shards * here
    rows = length if length <= 512 else 384
    block = pl.BlockSpec((shards, 1, here, width), lambda s: (0, s, 0, 0))
    joint_shape = (segs * length + padded, 3 * width)
    joint = pl.BlockSpec(joint_shape, lambda s: (0, 0))
    row = pl.BlockSpec((1, 1, padded + length), lambda s: (s, 0, 0))
    docs = [
        pl.BlockSpec(memory_space=pltpu.SMEM),
        pl.BlockSpec((1, length, 1), lambda s: (s, 0, 0)),
        row,
        row,
    ]
    params = pltpu.CompilerParams(
        dimension_semantics=("arbitrary",), vmem_limit_bytes=24 * 2**20
    )
    queries, keys = pltpu.VMEM((length, width), BF), pltpu.VMEM((padded + length, width), BF)
    key_sums = pltpu.VMEM((width, padded + length), F32)
    work = 2 * segs * length * (length // 2 + padded) * width
    forward = pl.pallas_call(
        functools.partial(forward_kernel, rows, segs),
        grid=(segs,),
        in_specs=docs + [joint],
        out_specs=block,
        out_shape=jax.ShapeDtypeStruct((shards, segs, here, width), BF),
        scratch_shapes=[queries, keys, keys],
        compiler_params=params,
        cost_estimate=pl.CostEstimate(
            flops=60 * work, bytes_accessed=8 * segs * length * width, transcendentals=0
        ),
    )
    backward = pl.pallas_call(
        functools.partial(backward_kernel, rows, segs),
        grid=(segs,),
        in_specs=docs + [joint, block],
        out_specs=joint,
        out_shape=jax.ShapeDtypeStruct(joint_shape, BF),
        scratch_shapes=[queries, keys, keys, queries, key_sums, key_sums]
        + [pltpu.VMEM((padded, 3 * width), F32)],
        compiler_params=params,
        cost_estimate=pl.CostEstimate(
            flops=90 * work, bytes_accessed=14 * segs * length * width, transcendentals=0
        ),
    )
    return forward, backward


def gelu_both(inputs):
    share = 0.5 * (1.0 + lax.erf(inputs * SQRT_HALF))
    slope = share + inputs * jnp.exp(-0.5 * inputs * inputs) * NORMAL_PEAK
    return inputs * share, slope


def per_device(
    tokens, summary, doc_ids, gain_attn, gain_ffn, w_query, w_key, w_value, w_out, w_up, w_down,
    cotangent,
):
    _, segs, here, model = tokens.shape
    per_seg = summary.shape[2]
    sum_rows = summary.shape[1] * per_seg
    padded = -(-sum_rows // 128) * 128
    length = doc_ids.shape[2]
    shards = length // here
    rows = segs * here
    shard_rows = w_query.shape[0]
    width = model // shards

    place = lax.axis_index(SEQ)

    flat = tokens.reshape(rows, model).astype(F32)
    standard, inverse = normalize(flat)
    hidden = (standard * gain_attn).astype(BF)
    cot = cotangent.reshape(rows, model)
    summary_flat = summary.reshape(sum_rows, model).astype(F32)
    summary_pad = jnp.pad(summary_flat, ((0, padded - sum_rows), (0, 0)))
    standard_sum, inverse_sum = normalize(summary_pad)
    hidden_sum = (standard_sum * gain_attn).astype(BF)

    docs = doc_ids.reshape(segs, length)
    last_docs = jnp.repeat(docs[: segs - 1, length - 1], per_seg)
    sum_docs = jnp.pad(last_docs, (0, padded - sum_rows), constant_values=-1)[None]
    doc_rows = jnp.concatenate([jnp.broadcast_to(sum_docs, (segs, padded)), docs], axis=1)
    far = jnp.where(
        jnp.arange(padded)[None] < jnp.arange(segs)[:, None] * per_seg, -1, length
    ).astype(jnp.int32)
    places = jnp.broadcast_to(jnp.arange(length, dtype=jnp.int32), (segs, length))
    pos_rows = jnp.concatenate([far, places], axis=1)
    doc_args = (ring_order(shards), docs[:, :, None], doc_rows[:, None], pos_rows[:, None])
    attend, attend_back = attention_calls(segs, shards, here, width, padded)
    split = (shards, segs, here, width)
    block_rows = shards * rows // max(ring_size(), 1)

    box = Box(hidden_sum=hidden_sum)
    out = {}

    half_sums = -(-sum_rows // 2)

    def in_halves(array):
        array = jnp.pad(array[:sum_rows], ((0, 2 * half_sums - sum_rows), (0, 0)))
        return array.reshape(2, half_sums, -1)

    def ready_early():
        yield ()
        place_y = lax.axis_index("y")
        sum_parts = [
            lax.dynamic_index_in_dim(in_halves(array), place_y, 0, False)
            for array in (standard_sum, inverse_sum)
        ]
        box["doc_args"], box["sum_parts"] = yield (doc_args, sum_parts)

    def critical():
        left = yield from gather_ring(hidden, box["hidden_sum"])
        w_qkv = yield from box.wait("w_qkv")
        doc_args = box["doc_args"]
        operands = dot(left, w_qkv).astype(BF)
        operands = yield operands
        attended = yield attend(*doc_args, operands)

        attended = attended.reshape(shards, rows, width)
        attended = yield lax.all_to_all(attended, SEQ, 0, 0, tiled=True)
        attended = near_blocks(attended.swapaxes(0, 1).reshape(rows, model), ROWS)
        w_out_all = yield from box.wait("w_out")
        summed = dot(attended, w_out_all)
        mixed = flat + summed
        standard_ffn, inverse_ffn = normalize(mixed)
        normed = near_blocks((standard_ffn * gain_ffn).astype(BF), FFN_REST, ("c",))

        normed_all = yield from gather_plane(normed, *FFN_NEAR)
        cot_all = yield from box.wait("cot_all")
        w_up_here = yield from box.wait("w_up")
        active, slope = gelu_both(dot(normed_all, w_up_here))
        active, slope = active.astype(BF), slope.astype(BF)
        d_w_down = dot(cot_all, active, 0, 0).astype(BF)
        active, slope, d_w_down = yield (active, slope, d_w_down)
        box["d_w_down"] = d_w_down
        w_down_here = yield from box.wait("w_down")
        grad_upper = (slope * dot(cot_all, w_down_here)).astype(BF)
        grad_normed_part = dot(grad_upper, w_up_here, 1, 1).astype(BF)
        grad_upper, grad_normed_part = yield (grad_upper, grad_normed_part)
        near = scatter_plane(grad_normed_part, *FFN_NEAR)
        in_flight = next(near)
        d_w_up = dot(normed_all, grad_upper, 0, 0).astype(BF)
        in_flight, d_w_up, late_active = yield (in_flight, d_w_up, active)
        box["d_w_up"] = d_w_up
        ffn_out_part = dot(late_active, w_down_here, 1, 1).astype(BF)
        in_flight, ffn_out_part = yield (near.send(in_flight), ffn_out_part)
        try:
            near.send(in_flight)
        except StopIteration as end:
            grad_normed = near_blocks_back(end.value, FFN_REST, ("c",)).astype(F32)
        grad_mixed = cot.astype(F32) + normalize_back(
            grad_normed, gain_ffn, standard_ffn, inverse_ffn
        )

        grad_branch = grad_mixed.astype(BF)
        grad_attended = near_blocks(dot(grad_branch, w_out_all, 1, 1).astype(BF), ROWS)
        grad_attended = grad_attended.reshape(rows, shards, width).swapaxes(0, 1)
        held = (attended, grad_branch, ffn_out_part, d_w_down, d_w_up)
        grad_attended, held = lax.optimization_barrier((grad_attended, held))
        attended, grad_branch, box["ffn_out_part"], box["d_w_down_late"], box["d_w_up_late"] = held
        box["for_out"] = attended, grad_branch
        grad_attended = yield lax.all_to_all(grad_attended, SEQ, 0, 0, tiled=True)
        grads = yield attend_back(*doc_args, operands, grad_attended.reshape(split))

        box["F"] = True
        def grad_block(k):
            rows_of_k = (late or [grads])[0][k * block_rows : (k + 1) * block_rows]
            return dot(rows_of_k, w_qkv, 1, 1).astype(BF)

        late = []
        d_w_qkv = yield from sums_of_cores(dot(left, grads, 0, 0).astype(BF))
        scatter = scatter_ring(grad_block)
        try:
            in_flight = next(scatter)
            in_flight, d_w_qkv, grads = yield (in_flight, d_w_qkv, grads)
            late.append(grads)
            box["d_w_qkv"] = d_w_qkv
            box["sums"] = dot(grads[shards * rows :], w_qkv, 1, 1).astype(BF)
            while True:
                in_flight = yield scatter.send(in_flight)
        except StopIteration as end:
            grad_hidden = end.value.astype(F32)
        if not late:
            box["d_w_qkv"] = d_w_qkv
            box["sums"] = dot(grads[shards * rows :], w_qkv, 1, 1).astype(BF)
        out["d_tokens"] = grad_mixed + normalize_back(grad_hidden, gain_attn, standard, inverse)
        ffn_out = yield from box.wait("ffn_out")
        ffn_out = near_blocks_back(ffn_out, FFN_REST, ("c",))
        out["activations"] = (mixed + ffn_out.astype(F32)).astype(BF)

    def cotangent_rows():
        yield from pause(PLAN["cot"])
        cot_all = yield from gather_plane(near_blocks(cot, FFN_REST, ("c",)), *FFN_NEAR)
        box["cot_all"] = yield cot_all

    def weight(name, shard):
        part, far, part_x, far_x = Rows(), Rows(), Rows(), Rows()

        def columns():
            yield from pause(PLAN[name][0])
            array = yield from exchange_first(shard)
            yield from pause(PLAN[name][1])
            array = yield from exchange_last(array)
            part.add(0, 4, array)

        def all_columns():
            parts = [(yield from part.take(0, 4))]
            if lax.axis_size("zh") == 2:
                parts.append((yield from far.take(0, 4)))
            parts.append((yield from part_x.take(0, 4)))
            if lax.axis_size("zh") == 2:
                parts.append((yield from far_x.take(0, 4)))
            box["w_" + name] = all_rows(parts)

        threads = {name: columns(), name + "_x": send_rows(part, "x", PLAN[name + "_x"], part_x)}
        if lax.axis_size("zh") == 2:
            threads[name + "_zh"] = send_rows(part, "zh", PLAN[name + "_zh"], far)
            threads[name + "_far"] = send_rows(far, "x", PLAN[name + "_far"], far_x)
        threads[name + "_all"] = all_columns()
        return threads

    def weight_sums(name):
        sent, own, near, far, landed, sent_near = (Rows() for _ in range(6))

        def start():
            sums = yield from box.wait("d_w_" + name)
            sent.add(0, 4, part_of(sums, 1, 1))
            own.add(0, 4, part_of(sums, 0, 1))
            sums = yield from box.wait("d_w_" + name + "_late")
            sent_near.add(0, 4, part_of(sums, 1, 0))

        def all_sums():
            sums = yield from box.wait("d_w_" + name + "_late")
            if lax.axis_size("zh") != 2:
                array = yield from sums_over_all_zh(sums)
            else:
                array = part_of(sums, 0, 0) + (yield from near.take(0, 4))
                array = array + (yield from landed.take(0, 4))
            waits = PLAN["d_" + name + "_out"]
            yield from pause(waits[0])
            array = yield from sums_of_ffn(array, waits[1])
            out["d_w_" + name] = array.astype(F32)

        threads = {"d_" + name: start()}
        if lax.axis_size("zh") == 2:
            plans = {step: PLAN["d_" + name + "_" + step] for step in ("far", "zh", "near")}
            threads["d_" + name + "_far"] = send_rows(sent, "x", plans["far"], far, own)
            threads["d_" + name + "_zh"] = send_rows(far, "zh", plans["zh"], landed)
            threads["d_" + name + "_near"] = send_rows(sent_near, "x", plans["near"], near)
        threads["d_" + name + "_all"] = all_sums()
        return threads

    def weight_out():
        waits = PLAN["out"]
        array = w_out.reshape((1,) * len(AXES) + w_out.shape)
        for rounds, axis in zip(waits, ("zh", "zl")):
            yield from pause(rounds)
            array = yield from gather_dim(array, axis, AXES.index(axis))
        yield from pause(waits[2])
        half = array.shape[-1] // 2
        by_x, by_y = yield (swap(array, "x"), swap(array, "y"))
        yield from pause(waits[3])
        low, high = yield (swap(by_y[..., :half], "x"), swap(by_x[..., half:], "y"))
        both = jnp.concatenate([low, high], axis=-1)
        dim_y = AXES.index("y")
        near = pair(array, by_y, "y", dim_y).reshape(-1, model)
        far = pair(by_x, both, "y", dim_y).reshape(-1, model)
        near_c, far_c = swap(near, "c"), swap(far, "c")
        box["w_out"] = yield jnp.concatenate([near, near_c, far, far_c], axis=0)

    def out_back():
        attended, grad_branch = yield from box.wait("for_out")
        half = model // 2
        far = dot(attended[:, half:], grad_branch, 0, 0).astype(BF)
        far = far[: half // 2] + swap(far[half // 2 :], "c")
        waits = PLAN["d_out"]
        yield from pause(waits[0])
        low = yield swap(far[: half // 4], "x")
        near = dot(attended[:, :half], grad_branch, 0, 0).astype(BF)
        near = near[: half // 2] + swap(near[half // 2 :], "c")
        near = yield near
        yield from pause(waits[1] - 1)
        high = yield swap(far[half // 4 :], "x")
        array = near + jnp.concatenate([low, high], axis=0)
        seq_sizes = tuple(lax.axis_size(axis) for axis in SEQ)
        array = array.reshape((1, 1) + seq_sizes + (shard_rows, model))
        yield from pause(waits[2])
        array = yield from scatter_dim(array, "y", AXES.index("y"))
        yield from pause(waits[3])
        array = yield from scatter_line(array[0, 0])
        out["d_w_out"] = array.reshape(shard_rows, model).astype(F32)

    def activations_back():
        part = yield from box.wait("ffn_out_part")
        waits = PLAN["act"]
        yield from pause(waits[0])
        part = yield from scatter_plane(part, *FFN_NEAR)
        yield from pause(waits[2])
        box["ffn_out"] = yield part

    def qkv_back():
        array = yield from box.wait("d_w_qkv")
        array = yield from sums_of_qkv(array)
        out["d_w_query"], out["d_w_key"], out["d_w_value"] = apart(array, width)

    def sums_back():
        grad_sum_part = yield from box.wait("sums")
        waits = PLAN["sums"]
        yield from pause(waits[0])
        array = yield from scatter_dim(in_halves(grad_sum_part), "y", 0)
        for rounds, axis in zip(waits[1:], ("zl", "zh")):
            yield from pause(rounds)
            if lax.axis_size(axis) == 2:
                theirs = yield swap(array, axis)
                array = array + theirs
            else:
                array = lax.psum(array, axis)
        grad_sum = array[0].astype(F32)
        standard_part, inverse_part = box["sum_parts"]
        part = normalize_back(grad_sum, gain_attn, standard_part, inverse_part).astype(BF)
        yield from pause(waits[3])
        theirs = yield swap(part, "y")
        part = pair(part[None], theirs[None], "y", 0).reshape(2 * half_sums, model)
        out["d_summary"] = part[:sum_rows].astype(F32)

    together(
        ready_early=ready_early(),
        weight_qkv=box.put("w_qkv", columns_of_qkv(side_by_side((w_query, w_key, w_value), width))),
        **weight("up", w_up),
        **weight("down", w_down),
        weight_out=weight_out(),
        cotangent_rows=cotangent_rows(),
        critical=critical(),
        out_back=out_back(),
        **weight_sums("down"),
        **weight_sums("up"),
        activations_back=activations_back(),
        sums_back=sums_back(),
        qkv_back=qkv_back(),
    )

    def gain_sum(gain, *pairs):
        total = sum(jnp.sum(w.astype(F32) * d, axis=1) for w, d in pairs)
        shard = lax.axis_index(AXES)
        return total / lax.dynamic_slice_in_dim(gain, shard * shard_rows, shard_rows, 0)

    d_gain_attn = gain_sum(
        gain_attn,
        (w_query, out["d_w_query"]),
        (w_key, out["d_w_key"]),
        (w_value, out["d_w_value"]),
    )
    d_gain_ffn = gain_sum(gain_ffn, (w_up, out["d_w_up"]))
    return (
        out["activations"].reshape(tokens.shape),
        out["d_tokens"].reshape(tokens.shape),
        out["d_summary"].reshape(summary.shape),
        d_gain_attn,
        d_gain_ffn,
        out["d_w_query"],
        out["d_w_key"],
        out["d_w_value"],
        out["d_w_out"],
        out["d_w_up"],
        out["d_w_down"],
    )


def solution(mesh):
    rows, seq = mesh.shape["rows"], mesh.shape["seq"]
    fine = Mesh(mesh.devices.reshape(rows // 2, 2, seq // 4, 2, 2), AXES)
    by_token = P(ROWS, None, SEQ, None)
    by_row = P(ROWS, None, None, None)
    weight = P(AXES, None)
    return jax.shard_map(
        per_device,
        mesh=fine,
        in_specs=(by_token, by_row, P(ROWS, None, None), P(), P())
        + (weight,) * 6
        + (by_token,),
        out_specs=(by_token, by_token, by_row, P(AXES), P(AXES)) + (weight,) * 6,
        check_vma=False,
    )
```

```python
import functools
import itertools
import math

import jax
import jax.numpy as jnp
from jax import lax
from jax.experimental import pallas as pl
from jax.experimental.pallas import tpu as pltpu
from jax.sharding import Mesh, PartitionSpec as P

HEAD = 64
EPSILON = 1e-05
MASKED = -1e30
SQRT_HALF = 0.7071067811865476
NORMAL_PEAK = 0.3989422804014327

AXES = ("x", "c", "zh", "zl", "y")
ROWS = ("x", "c")
SEQ = ("zh", "zl", "y")
FFN_GROUP = ("c", "y", "zl")
FFN_DIMS = ("c", "zl", "y")
FFN_NEAR = ("y", "zl", "c")
FFN_REST = ("x", "zh")
PLAN = {
    "cot": 6,
    "up": (0, 1),
    "down": (1, 1),
    "up_zh": ((0, 1), (0, 2), (0, 1)),
    "up_x": ((0, 4),),
    "up_far": ((1, 4),),
    "down_zh": ((1, 1), (0, 1), (0, 1), (0, 1)),
    "down_x": ((2, 2), (1, 2)),
    "down_far": ((0, 2), (0, 2)),
    "out": (2, 0, 0, 0),
    "d_down_far": ((0, 2), (0, 2)),
    "d_down_zh": ((0, 1), (0, 1), (0, 2)),
    "d_down_near": ((1, 4),),
    "d_down_out": (1, 1),
    "d_up_far": ((0, 2), (0, 2)),
    "d_up_zh": ((0, 1), (0, 1), (0, 2)),
    "d_up_near": ((5, 4),),
    "d_up_out": (0, 0),
    "act": (0, 0, 2),
    "d_out": (0, 2, 2, 0),
    "sums": (0, 0, 0, 0),
    "qkv": (0, 0, 0, 0),
}
BF = jnp.bfloat16
F32 = jnp.float32


def dot(left, right, left_dim=1, right_dim=0):
    return lax.dot_general(
        left, right, (((left_dim,), (right_dim,)), ((), ())), preferred_element_type=F32
    )


def normalize(inputs):
    average = jnp.mean(inputs, axis=-1, keepdims=True)
    centred = inputs - average
    inverse = lax.rsqrt(jnp.mean(centred * centred, axis=-1, keepdims=True) + EPSILON)
    return centred * inverse, inverse


def normalize_back(upstream, scaling, standard, inverse):
    scaled = upstream * scaling
    return inverse * (
        scaled
        - jnp.mean(scaled, axis=-1, keepdims=True)
        - standard * jnp.mean(scaled * standard, axis=-1, keepdims=True)
    )


def swap(array, axis):
    return lax.ppermute(array, axis, [(0, 1), (1, 0)])


def pair(mine, theirs, axis, dim):
    first = lax.axis_index(axis) == 0
    return jnp.concatenate(
        [jnp.where(first, mine, theirs), jnp.where(first, theirs, mine)], axis=dim
    )


def halves(array, axis, dim):
    half = array.shape[dim] // 2
    place = lax.axis_index(axis)
    return (
        lax.dynamic_slice_in_dim(array, place * half, half, dim),
        lax.dynamic_slice_in_dim(array, (1 - place) * half, half, dim),
    )


def together(**transfers):
    flying = {}

    def advance(name, sent):
        try:
            with jax.named_scope(name):
                flying[name] = transfers[name].send(sent)
        except StopIteration:
            flying.pop(name, None)

    for name in transfers:
        advance(name, None)
    while flying:
        landed = lax.optimization_barrier(dict(flying))
        for name in transfers:
            if name in landed:
                advance(name, landed[name])


class Box(dict):
    def wait(self, key):
        while key not in self:
            yield ()
        return self[key]

    def put(self, key, transfer):
        self[key] = yield from transfer


def pause(rounds):
    for _ in range(rounds):
        yield ()


class Rows:
    def __init__(self, whole=None):
        self.pieces = [] if whole is None else [(0, 4, whole)]

    def add(self, first, count, array):
        self.pieces.append((first, count, array))

    def take(self, first, count):
        while not set(range(first, first + count)) <= self.held():
            yield ()
        found = []
        for start, held, array in sorted(self.pieces, key=lambda piece: piece[0]):
            low, high = max(start, first), min(start + held, first + count)
            if low < high:
                step = array.shape[0] // held
                found.append(array[(low - start) * step : (high - start) * step])
        return found[0] if len(found) == 1 else jnp.concatenate(found, axis=0)

    def held(self):
        return {start + i for start, count, _ in self.pieces for i in range(count)}


def send_rows(rows, axis, plan, landed, added=None):
    first = 0
    for rounds, count in plan:
        array = yield from rows.take(first, count)
        yield from pause(rounds)
        theirs = yield swap(array, axis)
        if added is not None:
            theirs = theirs + (yield from added.take(first, count))
        landed.add(first, count, theirs)
        first += count


def one_round(array, axis):
    theirs = swap(array, axis)
    if axis != "c":
        theirs = yield theirs
    return theirs


def gather_dim(array, axis, dim):
    if lax.axis_size(axis) != 2:
        return lax.all_gather(array, axis, axis=dim, tiled=True)
    theirs = yield from one_round(array, axis)
    return pair(array, theirs, axis, dim)


def scatter_dim(array, axis, dim):
    if lax.axis_size(axis) != 2:
        return lax.psum_scatter(array, axis, scatter_dimension=dim, tiled=True)
    mine, theirs = halves(array, axis, dim)
    theirs = yield from one_round(theirs, axis)
    return mine + theirs


def exchange(array, axis, cut, joined):
    if lax.axis_size(axis) != 2:
        return lax.all_to_all(array, axis, cut, joined, tiled=True)
    mine, theirs = halves(array, axis, cut)
    theirs = yield from one_round(theirs, axis)
    return pair(mine, theirs, axis, joined)


def gather_plane(array, first, second, last):
    cut = -(-array.shape[0] // 32) * 16
    by_first, by_second = yield (swap(array, first), swap(array, second))
    low, high = yield (swap(by_second[:cut], first), swap(by_first[cut:], second))
    near = jnp.concatenate([array, by_first, by_second, low, high], axis=0)
    return jnp.concatenate([near, swap(near, last)], axis=0)


def scatter_plane(array, first, second, last):
    half = array.shape[0] // 2
    array = array[:half] + swap(array[half:], last)
    rows = array.shape[0] // 4
    cut = -(-rows // 32) * 16
    here, by_first, by_second, both = (array[i * rows : (i + 1) * rows] for i in range(4))
    low, high = yield (swap(both[:cut], first), swap(both[cut:], second))
    by_second = jnp.concatenate([by_second[:cut] + low, by_second[cut:]], axis=0)
    by_first = jnp.concatenate([by_first[:cut], by_first[cut:] + high], axis=0)
    by_first, by_second = yield (swap(by_first, first), swap(by_second, second))
    return here + by_first + by_second


def scatter_line(array):
    if not ring_size():
        array = lax.psum_scatter(array, "zh", scatter_dimension=0, tiled=True)
        return lax.psum_scatter(array, "zl", scatter_dimension=1, tiled=True)[0, 0]
    blocks = array.reshape((4,) + array.shape[2:])
    here = lax.axis_index(("zh", "zl"))
    mine = lax.dynamic_index_in_dim(blocks, here, 0, False)
    theirs = yield tuple(
        lax.ppermute(
            lax.dynamic_index_in_dim(blocks, here ^ step, 0, False),
            ("zh", "zl"),
            [(i, i ^ step) for i in range(4)],
        )
        for step in (1, 2, 3)
    )
    return mine + theirs[0] + theirs[1] + theirs[2]


def ring_size():
    return 4 if lax.axis_size("zh") == 2 else 0


def ring_shift(array, step):
    return lax.ppermute(array, ("zh", "zl"), [(i, (i + step) % 4) for i in range(4)])


def gather_ring(array, others):
    if not ring_size():
        array = lax.all_gather(array, SEQ, axis=0, tiled=True)
        return jnp.concatenate([array, others], axis=0)
    rows = array.shape[0]

    def put(joined, block, place):
        return lax.dynamic_update_slice_in_dim(joined, block, place * rows, 0)

    joined = jnp.zeros((8 * rows + others.shape[0], array.shape[1]), array.dtype)
    joined = put(put(joined, array, 0), others, 8)
    across = [swap(array, "y")]
    along, joined = yield (ring_shift(array, 1), joined)
    for step in (1, 2):
        joined = put(joined, along, 2 * step)
        coming = ring_shift(along, 1)
        across.append(swap(along, "y"))
        if step == 2:
            joined = put(joined, across[0], 1)
        along, across[step - 1], joined = yield (coming, across[step - 1], joined)
    joined = put(put(joined, along, 6), across[1], 3)
    across.append(swap(along, "y"))
    across[2], across[3], joined = yield (across[2], across[3], joined)
    return put(put(joined, across[2], 5), across[3], 7)


def scatter_ring(block):
    if not ring_size():
        return lax.psum_scatter(block(0), SEQ, scatter_dimension=0, tiled=True)
    last, later = block(3), block(2)
    half = last.shape[0] // 2
    across = yield swap(last[half:], "y")
    running = last[:half] + across
    across = swap(later[half:], "y")
    for step in (2, 1, 0):
        here = later[:half]
        coming = ring_shift(running, -1)
        if step:
            later = block(step - 1)
            across_next = swap(later[half:], "y")
        coming, across = yield (coming, across)
        running = here + across + coming
        if step:
            across = across_next
    return running


def ring_order(shards):
    places = jnp.arange(shards, dtype=jnp.int32)
    if not ring_size():
        return places
    along = lax.axis_index(("zh", "zl"))
    return (along - places // 2) % 4 * 2 + (places % 2 ^ lax.axis_index("y"))


def columns_of_qkv(weights):
    array = weights.reshape((1,) * len(AXES) + weights.shape)
    for axis in SEQ:
        array = yield from exchange(array, axis, 6, AXES.index(axis))
    for axis in ROWS:
        array = yield from gather_dim(array, axis, AXES.index(axis))
    return array.reshape(-1, array.shape[-1])


def sums_of_cores(sums):
    sizes = tuple(lax.axis_size(axis) for axis in AXES)
    array = sums.reshape(sizes + (-1, sums.shape[-1]))
    return (yield from scatter_dim(array, "c", AXES.index("c")))


def sums_of_qkv(array):
    array = yield from scatter_dim(array, "x", AXES.index("x"))
    for axis in reversed(SEQ):
        array = yield from exchange(array, axis, AXES.index(axis), 6)
    return array.reshape(array.shape[-2:])


def side_by_side(weights, width):
    rows, cols = weights[0].shape

    def kernel(*refs):
        for part, ref in enumerate(refs[:3]):
            for place in range(cols // width):
                first = (3 * place + part) * width
                refs[3][:, first : first + width] = ref[:, place * width : (place + 1) * width]

    vmem = pl.BlockSpec(memory_space=pltpu.VMEM)
    return pl.pallas_call(
        kernel,
        in_specs=[vmem] * 3,
        out_specs=vmem,
        out_shape=jax.ShapeDtypeStruct((rows, 3 * cols), weights[0].dtype),
        compiler_params=pltpu.CompilerParams(vmem_limit_bytes=8 * 2**20),
    )(*weights)


def apart(array, width):
    rows, cols = array.shape[0], array.shape[1] // 3

    def kernel(ref, *outs):
        for part, out in enumerate(outs):
            for place in range(cols // width):
                first = (3 * place + part) * width
                block = ref[:, first : first + width].astype(F32)
                out[:, place * width : (place + 1) * width] = block

    vmem = pl.BlockSpec(memory_space=pltpu.VMEM)
    return pl.pallas_call(
        kernel,
        in_specs=[vmem],
        out_specs=[vmem] * 3,
        out_shape=[jax.ShapeDtypeStruct((rows, cols), F32)] * 3,
        compiler_params=pltpu.CompilerParams(vmem_limit_bytes=12 * 2**20),
    )(array)


def exchange_first(weight):
    array = weight.reshape((1, 1, 1) + weight.shape)
    for axis in FFN_GROUP[:-1]:
        array = yield from exchange(array, axis, 4, FFN_DIMS.index(axis))
    return array


def exchange_last(array):
    axis = FFN_GROUP[-1]
    array = yield from exchange(array, axis, 4, FFN_DIMS.index(axis))
    return array.reshape(-1, array.shape[-1])


def sums_of_ffn(sums, wait=0):
    sizes = tuple(lax.axis_size(axis) for axis in FFN_DIMS)
    array = sums.reshape(sizes + (-1, sums.shape[-1]))
    for axis in reversed(FFN_GROUP):
        array = yield from exchange(array, axis, FFN_DIMS.index(axis), 4)
        if axis == FFN_GROUP[-1]:
            yield from pause(wait)
    return array.reshape(array.shape[-2:])


def near_blocks(array, axes, kept=()):
    sizes = [lax.axis_size(axis) for axis in AXES]
    lead = list(axes) + list(kept)
    depth = max(AXES.index(axis) for axis in lead) + 1
    lanes = array.shape[1] // math.prod(sizes[:depth])
    firsts = []
    for places in itertools.product(*(range(lax.axis_size(axis)) for axis in lead)):
        at = {axis: place for axis, place in zip(lead, places)}
        for axis in axes:
            at[axis] = relative(at[axis], axis)
        first = 0
        for axis, size in zip(AXES[:depth], sizes):
            first = first * size + at[axis]
        firsts.append(first)
    return reorder(array, firsts, lanes)


def reorder(array, firsts, lanes):
    if lanes % 128:
        parts = [lax.dynamic_slice_in_dim(array, first * lanes, lanes, 1) for first in firsts]
        return jnp.concatenate(parts, axis=1)

    def kernel(firsts_ref, array_ref, out_ref):
        for place in range(len(firsts)):
            first = pl.multiple_of(firsts_ref[place] * lanes, 128)
            out_ref[:, place * lanes : (place + 1) * lanes] = array_ref[:, pl.ds(first, lanes)]

    return pl.pallas_call(
        kernel,
        in_specs=[pl.BlockSpec(memory_space=pltpu.SMEM), pl.BlockSpec(memory_space=pltpu.VMEM)],
        out_specs=pl.BlockSpec(memory_space=pltpu.VMEM),
        out_shape=jax.ShapeDtypeStruct(array.shape, array.dtype),
        compiler_params=pltpu.CompilerParams(vmem_limit_bytes=8 * 2**20),
    )(jnp.stack([jnp.int32(first) for first in firsts]), array)


def relative(place, axis):
    return place if lax.axis_size(axis) != 2 else lax.axis_index(axis) ^ place


def near_blocks_back(array, axes, kept):
    sizes = [lax.axis_size(axis) for axis in AXES]
    lead = list(axes) + list(kept)
    depth = max(AXES.index(axis) for axis in lead) + 1
    lanes = array.shape[1] // math.prod(sizes[:depth])
    firsts = []
    for places in itertools.product(*(range(size) for size in sizes[:depth])):
        at = dict(zip(AXES, places))
        first = 0
        for axis in lead:
            place = relative(at[axis], axis) if axis in axes else at[axis]
            first = first * lax.axis_size(axis) + place
        firsts.append(first)
    return reorder(array, firsts, lanes)


def all_rows(parts):
    if lax.axis_size("zh") != 2:
        parts = [lax.all_gather(part, "zh", axis=0, tiled=True) for part in parts]
    return jnp.concatenate(parts, axis=0)


def part_of(sums, x, zh):
    rows = sums.shape[0] // 4
    first = (2 * x + zh) * rows
    return sums[first : first + rows]


def sums_over_all_zh(sums):
    half = sums.shape[0] // 2
    theirs = yield swap(sums[half:], "x")
    return lax.psum_scatter(sums[:half] + theirs, "zh", scatter_dimension=0, tiled=True)


def load_ordered(segs, order_ref, tokens_ref, q_ref, k_ref, v_ref):
    length, width = q_ref.shape
    padded = k_ref.shape[0] - length
    here, first_sum = length // order_ref.shape[0], segs * length
    for part, ref in ((1, k_ref), (2, v_ref)):
        ref[:padded, :] = tokens_ref[first_sum:, part * width : (part + 1) * width]
    for place in range(order_ref.shape[0]):
        rows = tokens_ref[rows_of(segs, order_ref, place, here), :]
        q_ref[place * here : (place + 1) * here, :] = rows[:, :width] * BF(0.125)
        for part, ref in ((1, k_ref), (2, v_ref)):
            first = padded + place * here
            ref[first : first + here, :] = rows[:, part * width : (part + 1) * width]


def rows_of(segs, order_ref, place, here):
    first = (order_ref[place] * segs + pl.program_id(0)) * here
    return pl.ds(pl.multiple_of(first, 16), here)


def block_mask(doc_col_ref, doc_row_ref, pos_row_ref, first, rows, keys):
    query_pos = first + lax.broadcasted_iota(jnp.int32, (rows, 1), 0)
    in_reach = pos_row_ref[0, :, :keys] <= query_pos
    return in_reach & (doc_row_ref[0, :, :keys] == doc_col_ref[0, first : first + rows, :])


def heads_of(width):
    lane = lax.broadcasted_iota(jnp.int32, (1, width), 1) // HEAD
    return [lane == head for head in range(width // HEAD)]


def of_heads(parts, heads):
    total = parts[0]
    for part, head in zip(parts[1:], heads[1:]):
        total = jnp.where(head, part, total)
    return total


def block_probs(query, key, allowed):
    scores = jnp.where(allowed, dot(query, key, 1, 1), MASKED)
    weights = jnp.exp(scores - jnp.max(scores, axis=1, keepdims=True))
    return weights * (1.0 / jnp.sum(weights, axis=1, keepdims=True))


def forward_kernel(
    rows, segs, order_ref, doc_col_ref, doc_row_ref, pos_row_ref, tokens_ref, out_ref,
    q_ref, k_ref, v_ref,
):
    shards, _, here, width = out_ref.shape
    padded = k_ref.shape[0] - shards * here
    load_ordered(segs, order_ref, tokens_ref, q_ref, k_ref, v_ref)
    heads = heads_of(width)
    for first in range(0, shards * here, rows):
        keys = padded + first + rows
        allowed = block_mask(doc_col_ref, doc_row_ref, pos_row_ref, first, rows, keys)
        query, key, value = q_ref[first : first + rows, :], k_ref[:keys, :], v_ref[:keys, :]
        outs = []
        for head in heads:
            probs = block_probs(jnp.where(head, query, jnp.zeros_like(query)), key, allowed)
            outs.append(dot(probs.astype(BF), value))
        q_ref[first : first + rows, :] = of_heads(outs, heads).astype(BF)
    for place in range(shards):
        out_ref[place, 0] = q_ref[place * here : (place + 1) * here, :]


def backward_kernel(
    rows, segs, order_ref, doc_col_ref, doc_row_ref, pos_row_ref, tokens_ref, g_in, grads_out,
    q_ref, k_ref, v_ref, g_ref, dk_sum, dv_sum, sums,
):
    shards, _, here, width = g_in.shape
    padded = sums.shape[0]
    load_ordered(segs, order_ref, tokens_ref, q_ref, k_ref, v_ref)
    for place in range(shards):
        g_ref[place * here : (place + 1) * here, :] = g_in[place, 0]

    @pl.when(pl.program_id(0) == 0)
    def _():
        sums[...] = jnp.zeros_like(sums)

    heads = heads_of(width)
    for first in reversed(range(0, shards * here, rows)):
        keys = padded + first + rows
        last = first + rows == shards * here
        allowed = block_mask(doc_col_ref, doc_row_ref, pos_row_ref, first, rows, keys)
        query, grad = q_ref[first : first + rows, :], g_ref[first : first + rows, :]
        key, value = k_ref[:keys, :], v_ref[:keys, :]
        query_t, grad_t = query.T, grad.T
        d_queries = []
        for place, head in enumerate(heads):
            probs = block_probs(jnp.where(head, query, jnp.zeros_like(query)), key, allowed)
            d_probs = dot(jnp.where(head, grad, jnp.zeros_like(grad)), value, 1, 1)
            product = probs * d_probs
            delta = jnp.sum(product, axis=1, keepdims=True)
            d_scores = (product - probs * delta).astype(BF)
            d_queries.append(dot(d_scores, key))
            lanes = slice(place * HEAD, (place + 1) * HEAD)
            d_key = dot(query_t[lanes], d_scores)
            d_value = dot(grad_t[lanes], probs.astype(BF))
            if last:
                dk_sum[lanes, :], dv_sum[lanes, :] = d_key, d_value
            else:
                dk_sum[lanes, :keys] += d_key
                dv_sum[lanes, :keys] += d_value
        d_query = of_heads(d_queries, heads).astype(BF)
        q_ref[first : first + rows, :] = (d_query.astype(F32) * 0.125).astype(BF)
    d_key, d_value = dk_sum[...].T, dv_sum[...].T
    sums[:, width : 2 * width] += d_key[:padded]
    sums[:, 2 * width :] += d_value[:padded]
    k_ref[...], v_ref[...] = d_key.astype(BF), d_value.astype(BF)
    for place in range(shards):
        block = rows_of(segs, order_ref, place, here)
        grads_out[block, :width] = q_ref[place * here : (place + 1) * here, :]
        tokens = slice(padded + place * here, padded + (place + 1) * here)
        grads_out[block, width : 2 * width] = k_ref[tokens, :]
        grads_out[block, 2 * width :] = v_ref[tokens, :]

    @pl.when(pl.program_id(0) == segs - 1)
    def _():
        grads_out[segs * shards * here :, :] = sums[...].astype(BF)


def attention_calls(segs, shards, here, width, padded):
    length = shards * here
    rows = length if length <= 512 else 384
    block = pl.BlockSpec((shards, 1, here, width), lambda s: (0, s, 0, 0))
    joint_shape = (segs * length + padded, 3 * width)
    joint = pl.BlockSpec(joint_shape, lambda s: (0, 0))
    row = pl.BlockSpec((1, 1, padded + length), lambda s: (s, 0, 0))
    docs = [
        pl.BlockSpec(memory_space=pltpu.SMEM),
        pl.BlockSpec((1, length, 1), lambda s: (s, 0, 0)),
        row,
        row,
    ]
    params = pltpu.CompilerParams(
        dimension_semantics=("arbitrary",), vmem_limit_bytes=24 * 2**20
    )
    queries, keys = pltpu.VMEM((length, width), BF), pltpu.VMEM((padded + length, width), BF)
    key_sums = pltpu.VMEM((width, padded + length), F32)
    work = 2 * segs * length * (length // 2 + padded) * width
    forward = pl.pallas_call(
        functools.partial(forward_kernel, rows, segs),
        grid=(segs,),
        in_specs=docs + [joint],
        out_specs=block,
        out_shape=jax.ShapeDtypeStruct((shards, segs, here, width), BF),
        scratch_shapes=[queries, keys, keys],
        compiler_params=params,
        cost_estimate=pl.CostEstimate(
            flops=60 * work, bytes_accessed=8 * segs * length * width, transcendentals=0
        ),
    )
    backward = pl.pallas_call(
        functools.partial(backward_kernel, rows, segs),
        grid=(segs,),
        in_specs=docs + [joint, block],
        out_specs=joint,
        out_shape=jax.ShapeDtypeStruct(joint_shape, BF),
        scratch_shapes=[queries, keys, keys, queries, key_sums, key_sums]
        + [pltpu.VMEM((padded, 3 * width), F32)],
        compiler_params=params,
        cost_estimate=pl.CostEstimate(
            flops=90 * work, bytes_accessed=14 * segs * length * width, transcendentals=0
        ),
    )
    return forward, backward


def gelu_both(inputs):
    share = 0.5 * (1.0 + lax.erf(inputs * SQRT_HALF))
    slope = share + inputs * jnp.exp(-0.5 * inputs * inputs) * NORMAL_PEAK
    return inputs * share, slope


def per_device(
    tokens, summary, doc_ids, gain_attn, gain_ffn, w_query, w_key, w_value, w_out, w_up, w_down,
    cotangent,
):
    _, segs, here, model = tokens.shape
    per_seg = summary.shape[2]
    sum_rows = summary.shape[1] * per_seg
    padded = -(-sum_rows // 128) * 128
    length = doc_ids.shape[2]
    shards = length // here
    rows = segs * here
    shard_rows = w_query.shape[0]
    width = model // shards

    place = lax.axis_index(SEQ)

    flat = tokens.reshape(rows, model).astype(F32)
    standard, inverse = normalize(flat)
    hidden = (standard * gain_attn).astype(BF)
    cot = cotangent.reshape(rows, model)
    summary_flat = summary.reshape(sum_rows, model).astype(F32)
    summary_pad = jnp.pad(summary_flat, ((0, padded - sum_rows), (0, 0)))
    standard_sum, inverse_sum = normalize(summary_pad)
    hidden_sum = (standard_sum * gain_attn).astype(BF)

    docs = doc_ids.reshape(segs, length)
    last_docs = jnp.repeat(docs[: segs - 1, length - 1], per_seg)
    sum_docs = jnp.pad(last_docs, (0, padded - sum_rows), constant_values=-1)[None]
    doc_rows = jnp.concatenate([jnp.broadcast_to(sum_docs, (segs, padded)), docs], axis=1)
    far = jnp.where(
        jnp.arange(padded)[None] < jnp.arange(segs)[:, None] * per_seg, -1, length
    ).astype(jnp.int32)
    places = jnp.broadcast_to(jnp.arange(length, dtype=jnp.int32), (segs, length))
    pos_rows = jnp.concatenate([far, places], axis=1)
    doc_args = (ring_order(shards), docs[:, :, None], doc_rows[:, None], pos_rows[:, None])
    attend, attend_back = attention_calls(segs, shards, here, width, padded)
    split = (shards, segs, here, width)
    block_rows = shards * rows // max(ring_size(), 1)

    box = Box(hidden_sum=hidden_sum)
    out = {}

    half_sums = -(-sum_rows // 2)

    def in_halves(array):
        array = jnp.pad(array[:sum_rows], ((0, 2 * half_sums - sum_rows), (0, 0)))
        return array.reshape(2, half_sums, -1)

    def ready_early():
        yield ()
        place_y = lax.axis_index("y")
        sum_parts = [
            lax.dynamic_index_in_dim(in_halves(array), place_y, 0, False)
            for array in (standard_sum, inverse_sum)
        ]
        box["doc_args"], box["sum_parts"] = yield (doc_args, sum_parts)

    def critical():
        left = yield from gather_ring(hidden, box["hidden_sum"])
        w_qkv = yield from box.wait("w_qkv")
        doc_args = box["doc_args"]
        operands = dot(left, w_qkv).astype(BF)
        operands = yield operands
        attended = yield attend(*doc_args, operands)

        attended = attended.reshape(shards, rows, width)
        attended = yield lax.all_to_all(attended, SEQ, 0, 0, tiled=True)
        attended = near_blocks(attended.swapaxes(0, 1).reshape(rows, model), ROWS)
        w_out_all = yield from box.wait("w_out")
        summed = dot(attended, w_out_all)
        mixed = flat + summed
        standard_ffn, inverse_ffn = normalize(mixed)
        normed = near_blocks((standard_ffn * gain_ffn).astype(BF), FFN_REST, ("c",))

        normed_all = yield from gather_plane(normed, *FFN_NEAR)
        cot_all = yield from box.wait("cot_all")
        w_up_here = yield from box.wait("w_up")
        active, slope = gelu_both(dot(normed_all, w_up_here))
        active, slope = active.astype(BF), slope.astype(BF)
        d_w_down = dot(cot_all, active, 0, 0).astype(BF)
        active, slope, d_w_down = yield (active, slope, d_w_down)
        box["d_w_down"] = d_w_down
        w_down_here = yield from box.wait("w_down")
        grad_upper = (slope * dot(cot_all, w_down_here)).astype(BF)
        grad_normed_part = dot(grad_upper, w_up_here, 1, 1).astype(BF)
        grad_upper, grad_normed_part = yield (grad_upper, grad_normed_part)
        near = scatter_plane(grad_normed_part, *FFN_NEAR)
        in_flight = next(near)
        d_w_up = dot(normed_all, grad_upper, 0, 0).astype(BF)
        in_flight, d_w_up, late_active = yield (in_flight, d_w_up, active)
        box["d_w_up"] = d_w_up
        ffn_out_part = dot(late_active, w_down_here, 1, 1).astype(BF)
        in_flight, ffn_out_part = yield (near.send(in_flight), ffn_out_part)
        try:
            near.send(in_flight)
        except StopIteration as end:
            grad_normed = near_blocks_back(end.value, FFN_REST, ("c",)).astype(F32)
        grad_mixed = cot.astype(F32) + normalize_back(
            grad_normed, gain_ffn, standard_ffn, inverse_ffn
        )

        grad_branch = grad_mixed.astype(BF)
        grad_attended = near_blocks(dot(grad_branch, w_out_all, 1, 1).astype(BF), ROWS)
        grad_attended = grad_attended.reshape(rows, shards, width).swapaxes(0, 1)
        held = (attended, grad_branch, ffn_out_part, d_w_down, d_w_up)
        grad_attended, held = lax.optimization_barrier((grad_attended, held))
        attended, grad_branch, box["ffn_out_part"], box["d_w_down_late"], box["d_w_up_late"] = held
        box["for_out"] = attended, grad_branch
        grad_attended = yield lax.all_to_all(grad_attended, SEQ, 0, 0, tiled=True)
        grads = yield attend_back(*doc_args, operands, grad_attended.reshape(split))

        box["F"] = True
        def grad_block(k):
            rows_of_k = (late or [grads])[0][k * block_rows : (k + 1) * block_rows]
            return dot(rows_of_k, w_qkv, 1, 1).astype(BF)

        late = []
        d_w_qkv = yield from sums_of_cores(dot(left, grads, 0, 0).astype(BF))
        scatter = scatter_ring(grad_block)
        try:
            in_flight = next(scatter)
            in_flight, d_w_qkv, grads = yield (in_flight, d_w_qkv, grads)
            late.append(grads)
            box["d_w_qkv"] = d_w_qkv
            box["sums"] = dot(grads[shards * rows :], w_qkv, 1, 1).astype(BF)
            while True:
                in_flight = yield scatter.send(in_flight)
        except StopIteration as end:
            grad_hidden = end.value.astype(F32)
        if not late:
            box["d_w_qkv"] = d_w_qkv
            box["sums"] = dot(grads[shards * rows :], w_qkv, 1, 1).astype(BF)
        out["d_tokens"] = grad_mixed + normalize_back(grad_hidden, gain_attn, standard, inverse)
        ffn_out = yield from box.wait("ffn_out")
        ffn_out = near_blocks_back(ffn_out, FFN_REST, ("c",))
        out["activations"] = (mixed + ffn_out.astype(F32)).astype(BF)

    def cotangent_rows():
        yield from pause(PLAN["cot"])
        cot_all = yield from gather_plane(near_blocks(cot, FFN_REST, ("c",)), *FFN_NEAR)
        box["cot_all"] = yield cot_all

    def weight(name, shard):
        part, far, part_x, far_x = Rows(), Rows(), Rows(), Rows()

        def columns():
            yield from pause(PLAN[name][0])
            array = yield from exchange_first(shard)
            yield from pause(PLAN[name][1])
            array = yield from exchange_last(array)
            part.add(0, 4, array)

        def all_columns():
            parts = [(yield from part.take(0, 4))]
            if lax.axis_size("zh") == 2:
                parts.append((yield from far.take(0, 4)))
            parts.append((yield from part_x.take(0, 4)))
            if lax.axis_size("zh") == 2:
                parts.append((yield from far_x.take(0, 4)))
            columns_here = all_rows(parts)
            if name == "up":
                columns_here = yield columns_here
            box["w_" + name] = columns_here

        threads = {name: columns(), name + "_x": send_rows(part, "x", PLAN[name + "_x"], part_x)}
        if lax.axis_size("zh") == 2:
            threads[name + "_zh"] = send_rows(part, "zh", PLAN[name + "_zh"], far)
            threads[name + "_far"] = send_rows(far, "x", PLAN[name + "_far"], far_x)
        threads[name + "_all"] = all_columns()
        return threads

    def weight_sums(name):
        sent, own, near, far, landed, sent_near = (Rows() for _ in range(6))

        def start():
            sums = yield from box.wait("d_w_" + name)
            sent.add(0, 4, part_of(sums, 1, 1))
            own.add(0, 4, part_of(sums, 0, 1))
            sums = yield from box.wait("d_w_" + name + "_late")
            sent_near.add(0, 4, part_of(sums, 1, 0))

        def all_sums():
            sums = yield from box.wait("d_w_" + name + "_late")
            if lax.axis_size("zh") != 2:
                array = yield from sums_over_all_zh(sums)
            else:
                array = part_of(sums, 0, 0) + (yield from near.take(0, 4))
                array = array + (yield from landed.take(0, 4))
            waits = PLAN["d_" + name + "_out"]
            yield from pause(waits[0])
            array = yield from sums_of_ffn(array, waits[1])
            out["d_w_" + name] = array.astype(F32)

        threads = {"d_" + name: start()}
        if lax.axis_size("zh") == 2:
            plans = {step: PLAN["d_" + name + "_" + step] for step in ("far", "zh", "near")}
            threads["d_" + name + "_far"] = send_rows(sent, "x", plans["far"], far, own)
            threads["d_" + name + "_zh"] = send_rows(far, "zh", plans["zh"], landed)
            threads["d_" + name + "_near"] = send_rows(sent_near, "x", plans["near"], near)
        threads["d_" + name + "_all"] = all_sums()
        return threads

    def weight_out():
        waits = PLAN["out"]
        array = w_out.reshape((1,) * len(AXES) + w_out.shape)
        for rounds, axis in zip(waits, ("zh", "zl")):
            yield from pause(rounds)
            array = yield from gather_dim(array, axis, AXES.index(axis))
        yield from pause(waits[2])
        half = array.shape[-1] // 2
        by_x, by_y = yield (swap(array, "x"), swap(array, "y"))
        yield from pause(waits[3])
        low, high = yield (swap(by_y[..., :half], "x"), swap(by_x[..., half:], "y"))
        both = jnp.concatenate([low, high], axis=-1)
        dim_y = AXES.index("y")
        near = pair(array, by_y, "y", dim_y).reshape(-1, model)
        far = pair(by_x, both, "y", dim_y).reshape(-1, model)
        near_c, far_c = swap(near, "c"), swap(far, "c")
        box["w_out"] = yield jnp.concatenate([near, near_c, far, far_c], axis=0)

    def out_back():
        attended, grad_branch = yield from box.wait("for_out")
        half = model // 2
        far = dot(attended[:, half:], grad_branch, 0, 0).astype(BF)
        far = far[: half // 2] + swap(far[half // 2 :], "c")
        waits = PLAN["d_out"]
        yield from pause(waits[0])
        low = yield swap(far[: half // 4], "x")
        near = dot(attended[:, :half], grad_branch, 0, 0).astype(BF)
        near = near[: half // 2] + swap(near[half // 2 :], "c")
        near = yield near
        yield from pause(waits[1] - 1)
        high = yield swap(far[half // 4 :], "x")
        array = near + jnp.concatenate([low, high], axis=0)
        seq_sizes = tuple(lax.axis_size(axis) for axis in SEQ)
        array = array.reshape((1, 1) + seq_sizes + (shard_rows, model))
        yield from pause(waits[2])
        array = yield from scatter_dim(array, "y", AXES.index("y"))
        yield from pause(waits[3])
        array = yield from scatter_line(array[0, 0])
        out["d_w_out"] = array.reshape(shard_rows, model).astype(F32)

    def activations_back():
        part = yield from box.wait("ffn_out_part")
        waits = PLAN["act"]
        yield from pause(waits[0])
        part = yield from scatter_plane(part, *FFN_NEAR)
        yield from pause(waits[2])
        box["ffn_out"] = yield part

    def qkv_back():
        array = yield from box.wait("d_w_qkv")
        array = yield from sums_of_qkv(array)
        out["d_w_query"], out["d_w_key"], out["d_w_value"] = apart(array, width)

    def sums_back():
        grad_sum_part = yield from box.wait("sums")
        waits = PLAN["sums"]
        yield from pause(waits[0])
        array = yield from scatter_dim(in_halves(grad_sum_part), "y", 0)
        for rounds, axis in zip(waits[1:], ("zl", "zh")):
            yield from pause(rounds)
            if lax.axis_size(axis) == 2:
                theirs = yield swap(array, axis)
                array = array + theirs
            else:
                array = lax.psum(array, axis)
        grad_sum = array[0].astype(F32)
        standard_part, inverse_part = box["sum_parts"]
        part = normalize_back(grad_sum, gain_attn, standard_part, inverse_part).astype(BF)
        yield from pause(waits[3])
        theirs = yield swap(part, "y")
        part = pair(part[None], theirs[None], "y", 0).reshape(2 * half_sums, model)
        out["d_summary"] = part[:sum_rows].astype(F32)

    together(
        ready_early=ready_early(),
        weight_qkv=box.put("w_qkv", columns_of_qkv(side_by_side((w_query, w_key, w_value), width))),
        **weight("up", w_up),
        **weight("down", w_down),
        weight_out=weight_out(),
        cotangent_rows=cotangent_rows(),
        critical=critical(),
        out_back=out_back(),
        **weight_sums("down"),
        **weight_sums("up"),
        activations_back=activations_back(),
        sums_back=sums_back(),
        qkv_back=qkv_back(),
    )

    def gain_sum(gain, *pairs):
        total = sum(jnp.sum(w.astype(F32) * d, axis=1) for w, d in pairs)
        shard = lax.axis_index(AXES)
        return total / lax.dynamic_slice_in_dim(gain, shard * shard_rows, shard_rows, 0)

    d_gain_attn = gain_sum(
        gain_attn,
        (w_query, out["d_w_query"]),
        (w_key, out["d_w_key"]),
        (w_value, out["d_w_value"]),
    )
    d_gain_ffn = gain_sum(gain_ffn, (w_up, out["d_w_up"]))
    return (
        out["activations"].reshape(tokens.shape),
        out["d_tokens"].reshape(tokens.shape),
        out["d_summary"].reshape(summary.shape),
        d_gain_attn,
        d_gain_ffn,
        out["d_w_query"],
        out["d_w_key"],
        out["d_w_value"],
        out["d_w_out"],
        out["d_w_up"],
        out["d_w_down"],
    )


def solution(mesh):
    rows, seq = mesh.shape["rows"], mesh.shape["seq"]
    fine = Mesh(mesh.devices.reshape(rows // 2, 2, seq // 4, 2, 2), AXES)
    by_token = P(ROWS, None, SEQ, None)
    by_row = P(ROWS, None, None, None)
    weight = P(AXES, None)
    return jax.shard_map(
        per_device,
        mesh=fine,
        in_specs=(by_token, by_row, P(ROWS, None, None), P(), P())
        + (weight,) * 6
        + (by_token,),
        out_specs=(by_token, by_token, by_row, P(AXES), P(AXES)) + (weight,) * 6,
        check_vma=False,
    )
```
